128 devices in a mesh: pipe: 4 (over x_lo, core), dp: 32 (over y, z, x_hi).
Axes of the slice: x: 4 (x_hi: 2, x_lo: 2; x = x_hi * 2 + x_lo), y: 4, z: 4, core: 2. Of those that a mesh axis runs over, the one named last changes fastest.
Arguments:
- section_input: bfloat16 [4, 8192, 2048], P('pipe', 'dp'), may hold values from -6 to 6
- top_grad: bfloat16 [8192, 2048], P('dp'), may hold values from -6 to 6
- w_in: bfloat16 [4, 2048, 3072], P('pipe', 'dp'), may hold values from -0.125 to 0.125
- w_out: bfloat16 [4, 1024, 2048], P('pipe', 'dp'), may hold values from -0.1875 to 0.1875
- segments: int32 [64, 128], P('dp'), may hold values from 0 to 3, never falling along the last dimension, each value on 1 to 64 neighbouring positions
Outputs:
- section_grads: bfloat16 [4, 8192, 2048], P('pipe', 'dp')
- w_in_grad: float32 [4, 2048, 3072], P('pipe', 'dp')
- w_out_grad: float32 [4, 1024, 2048], P('pipe', 'dp')
The draws below stay inside these ranges and needn't reach their ends.
Inputs may be any that keep to these rules, and one draw needn't show every extreme that they name: `segments`: in every row the history numbers run 0 to 3 without falling, each history has 1 to 64 positions, and one has exactly 64.
All inputs are finite; a program needn't handle non-finite values.
Results may differ from the reference program's by a relative error of at most 0.03.
Values may be sent and summed in bfloat16 or wider, within the bound.
No kernel may reach another device: no remote copies, remote signals or barrier semaphores. Data moves between devices by JAX's collectives and lax.ppermute only.
A program may use at most 128 MiB of HBM per device.

```python
import math
import jax
import jax.numpy as jnp
import numpy as np
from jax import lax

D = 2048
HEADS = 16
QK_DIM = 32
V_DIM = 64
HV = 1024
F1 = 3072
TOK_MB = 128
MICRO = 2
SEGS = 4
SEG_MOST = 64
SECTIONS = 4
TOKENS = 8192
MB_ROWS = 64
N_PIPE = 4
N_DP = 32


def spiked(array, own_key, source, target, shards_of, factor):
    owner, partner = [(jnp.arange(array.shape[dim]) // (array.shape[dim] // shards_of)).reshape([-1 if axis == dim else 1 for axis in range(array.ndim)]) for dim in (source, target)]
    chosen = jax.random.permutation(own_key, shards_of)[partner]
    strong = (owner == chosen) | (owner == (partner + shards_of // 2) % shards_of)
    return jnp.where(strong, factor * array, array)


def levels(rng, dims, split, smallest, largest):
    def one(dim, shards_of):
        heights = jax.random.uniform(jax.random.fold_in(jax.random.fold_in(rng, 6), dim), (shards_of,), jnp.float32, smallest / len(split), largest / len(split))
        return jnp.repeat(jnp.exp(heights), dims[dim] // shards_of).reshape((-1,) + (1,) * (len(dims) - dim - 1))

    loudness = one(*split[0])
    for cut in split[1:]:
        loudness = loudness * one(*cut)
    return loudness


def profile(count, total, reach, skew):
    loads = [(1 << 20) // math.isqrt(standing ** skew) + 1 for standing in range(2, count + 1)]
    spare, given = total - reach - (count - 1), [1] * (count - 1)
    while spare > 0:
        free = [i for i in range(count - 1) if given[i] < reach]
        mass, left = sum([loads[i] for i in free]), spare
        for i in free:
            extra = min(reach - given[i], max(1, left * loads[i] // mass), spare)
            given[i] = given[i] + extra
            spare = spare - extra
    return np.array([reach] + given)


def ragged_sizes(stream_key, amount, total, bound, lean):
    if amount == 2:
        one = jax.random.randint(stream_key, (), max(1, total - bound), min(bound, total - 1) + 1)
        return jnp.stack([one, total - one])
    tallies = jnp.asarray(profile(amount, total, bound, lean), jnp.int32)
    twos = (amount - 1) // 2
    giver, receiver = tallies[1:1 + 2 * twos:2], tallies[2:2 + 2 * twos:2]
    room = jnp.minimum(giver - 1, bound - receiver)
    moved = jax.random.randint(jax.random.fold_in(stream_key, 1), (twos,), 0, 1 << 20) % (room + 1)
    tallies = tallies.at[1:1 + 2 * twos:2].set(giver - moved).at[2:2 + 2 * twos:2].set(receiver + moved)
    return tallies[jax.random.permutation(jax.random.fold_in(stream_key, 2), amount)]


def gaussian(rng, dims, width, most, cuts=(), kind=jnp.bfloat16):
    gain = levels(rng, dims, cuts, -0.22, 0.18) if cuts else 1.0
    array = jax.random.normal(rng, dims, jnp.float32) * width * gain
    return jnp.minimum(jnp.maximum(array, -most), most).astype(kind)


def heavy_noise(own_key, shape, spread, reach, cuts, heavy, kind=jnp.bfloat16):
    values = spread * jax.random.normal(own_key, shape, jnp.float32)
    if cuts:
        values = values * levels(own_key, shape, cuts, -0.22, 0.18)
    return jnp.clip(spiked(values, jax.random.fold_in(own_key, 3), *heavy), -reach, reach).astype(kind)


def setup_inputs(seed: int = 0) -> dict:
    seeds = jax.random.split(jax.random.key(seed), 6)
    section_input = heavy_noise(seeds[0], (SECTIONS, TOKENS, D), 1.0, 6.0, ((0, 4), (1, 32)), (1, 2, 32, 2.75))
    top_grad = gaussian(seeds[1], (TOKENS, D), 1.0, 6.0, ((0, 32),))
    w_in = gaussian(seeds[2], (SECTIONS, D, F1), D ** -0.5, 0.125, ((0, 4), (1, 32)))
    w_out = gaussian(seeds[3], (SECTIONS, HV, D), HV ** -0.5, 0.1875, ((0, 4), (1, 32)))
    segments = jax.vmap(lambda own: jnp.searchsorted(jnp.cumsum(ragged_sizes(own, SEGS, TOK_MB, SEG_MOST, 2)), jnp.arange(TOK_MB), side="right"))(jax.random.split(seeds[4], MB_ROWS)).reshape((MB_ROWS, TOK_MB)).astype(jnp.int32)
    return {"section_input": section_input, "top_grad": top_grad, "w_in": w_in, "w_out": w_out, "segments": segments}


EPSILON = 1e-05

def norm_rows(values):
    center = values - lax.optimization_barrier(jnp.mean(values, axis=-1, keepdims=True))
    return center * lax.rsqrt(lax.optimization_barrier(jnp.mean(center * center, axis=-1, keepdims=True)) + EPSILON)

def silu_slope(preact):
    squash = jax.nn.sigmoid(preact)
    return squash * (1.0 + preact * (1.0 - squash))

def contract_rows(left, right):
    return lax.dot_general(left, right, (((0,), (0,)), ((), ())), preferred_element_type=jnp.float32)

def forward_front(inputs, w_first):
    normed = norm_rows(inputs.astype(jnp.float32)).astype(jnp.bfloat16)
    preact = jnp.dot(normed, w_first, preferred_element_type=jnp.float32)
    return (normed, preact, jax.nn.silu(preact).astype(jnp.bfloat16))

def attend(activated, history):
    row_count = activated.shape[0]
    value_cols = HEADS * V_DIM
    query_cols = HEADS * QK_DIM
    active32 = activated.astype(jnp.float32)
    gating = active32[:, :value_cols]
    values = active32[:, value_cols:2 * value_cols].reshape(row_count, HEADS, V_DIM)
    queries = active32[:, 2 * value_cols:2 * value_cols + query_cols].reshape(row_count, HEADS, QK_DIM)
    key_rows = active32[:, 2 * value_cols + query_cols:].reshape(row_count, HEADS, QK_DIM)
    scores = jnp.einsum('qhd,khd->hqk', queries, key_rows) * QK_DIM ** (-0.5)
    same_doc = history[:, None] == history[None, :]
    positions = lax.broadcasted_iota(jnp.int32, (row_count, row_count), 0)
    columns = lax.broadcasted_iota(jnp.int32, (row_count, row_count), 1)
    allowed = jnp.logical_and(same_doc, columns <= positions)
    counts = lax.optimization_barrier(jnp.sum(same_doc.astype(jnp.float32), axis=1))
    weights_mask = allowed.astype(jnp.float32) / counts[:, None]
    weights = jax.nn.silu(scores) * weights_mask[None]
    mixed = jnp.einsum('hqk,khd->qhd', weights, values).reshape(row_count, value_cols)
    return norm_rows(mixed) * gating

def layer_back(inputs, normed, preact, activated, upstream, history, w_first, w_second):
    gated_full, pull = jax.vjp(lambda active_in: attend(active_in, history), activated)
    gated = gated_full.astype(jnp.bfloat16)
    grad_second = contract_rows(gated, upstream)
    grad_gated = lax.dot_general(upstream, w_second, (((1,), (1,)), ((), ())), preferred_element_type=jnp.float32)
    grad_active, = pull(grad_gated)
    grad_preact = (grad_active.astype(jnp.float32) * silu_slope(preact)).astype(jnp.bfloat16)
    grad_normed = lax.dot_general(grad_preact, w_first, (((1,), (1,)), ((), ())), preferred_element_type=jnp.float32)
    _, pull_norm = jax.vjp(norm_rows, inputs.astype(jnp.float32))
    grad_through, = pull_norm(grad_normed)
    grad_input = (upstream.astype(jnp.float32) + grad_through).astype(jnp.bfloat16)
    return (grad_input, grad_preact, grad_second)

def reference(section_input, top_grad, w_in, w_out, segments):
    upstream_all = top_grad
    section_list = []
    first_list = []
    second_list = []
    for section in range(N_PIPE - 1, -1, -1):
        inputs_all = section_input[section]
        w_first = w_in[section]
        w_second = w_out[section]
        upstream_now = upstream_all

        def device_step(carry, device):
            total_in, total_out = carry
            acc_in = jnp.zeros((D, F1), jnp.float32)
            acc_out = jnp.zeros((HV, D), jnp.float32)
            pieces = []
            for micro_index in range(MICRO):
                block = (device * MICRO + micro_index).astype(jnp.int32)
                start = (block * TOK_MB).astype(jnp.int32)
                inputs = lax.dynamic_slice_in_dim(inputs_all, start, TOK_MB, 0)
                upstream = lax.dynamic_slice_in_dim(upstream_now, start, TOK_MB, 0)
                history = lax.dynamic_index_in_dim(segments, block, 0, keepdims=False)
                normed, preact, activated = forward_front(inputs, w_first)
                grad_input, grad_preact, grad_second = layer_back(inputs, normed, preact, activated, upstream, history, w_first, w_second)
                acc_in = acc_in + contract_rows(normed, grad_preact)
                acc_out = acc_out + grad_second
                pieces.append(grad_input)
            total_in = total_in + lax.optimization_barrier(acc_in.astype(jnp.bfloat16)).astype(jnp.float32)
            total_out = total_out + lax.optimization_barrier(acc_out.astype(jnp.bfloat16)).astype(jnp.float32)
            return ((total_in, total_out), jnp.concatenate(pieces, axis=0))
        start_sums = (jnp.zeros((D, F1), jnp.float32), jnp.zeros((HV, D), jnp.float32))
        (total_in, total_out), grad_blocks = lax.scan(device_step, start_sums, jnp.arange(N_DP, dtype=jnp.int32))
        upstream_all = grad_blocks.reshape(TOKENS, D)
        section_list.insert(0, upstream_all)
        first_list.insert(0, total_in)
        second_list.insert(0, total_out)
    return (jnp.stack(section_list), jnp.stack(first_list), jnp.stack(second_list))
```

```python
import jax
import jax.numpy as jnp
from jax import lax
from jax.experimental import pallas as pl
from jax.experimental.pallas import tpu as pltpu
from jax.sharding import PartitionSpec as P

HEADS = 16
QK_DIM = 32
V_DIM = 64
EPSILON = 1e-05
D = 2048
HV = 1024
F1 = 3072
QCOL = 2 * HV
KCOL = QCOL + HEADS * QK_DIM
LEN = 128
TOKENS = 256
SIDE = 4
HALF_IN = F1 // 2
HALF_OUT = D // 2
SCALE = QK_DIM ** (-0.5)
VMEM_LIMIT = 56 * 1024 * 1024
BF16 = jnp.bfloat16
F32 = jnp.float32

NT = (((1,), (1,)), ((), ()))
TN = (((0,), (0,)), ((), ()))


def mm(left, right, dims):
    return lax.dot_general(left, right, dims, preferred_element_type=F32)


def shifted(dy, dz, dx):
    pairs = []
    for i in range(32):
        y, z, x = i // 8, (i // 2) % 4, i % 2
        pairs.append((i, ((y + dy) % 4 * 4 + (z + dz) % 4) * 2 + (x + dx) % 2))
    return pairs


def send(array, dy, dz, dx):
    return lax.ppermute(array, "dp", shifted(dy, dz, dx))


def any_spec():
    return pl.BlockSpec(memory_space=pl.ANY)


def smem_spec():
    return pl.BlockSpec(memory_space=pltpu.SMEM)


def vmem_spec():
    return pl.BlockSpec(memory_space=pltpu.VMEM)


def block_row(y, z, dy, dz, rows):
    cell = lax.rem(y + dy + SIDE, SIDE) * SIDE + lax.rem(z + dz + SIDE, SIDE)
    return pl.multiple_of(cell * rows, rows)


def lane_group(width):
    return lax.broadcasted_iota(jnp.int32, (LEN, LEN), 1) // width


def keep(mask, tile):
    return jnp.where(mask, tile, jnp.zeros_like(tile))


def front_kernel(place, x_ref, wm_ref, *refs):
    pieces_a, pieces_b = refs[0:4], refs[4:8]
    normed, slope, act, attn, turn, xhat, gated, rstd_in, rstd_mid, w_full = refs[8:18]
    w_buf, mixed, sems, out_sem = refs[18:22]
    y, z = place[0], place[1]
    first, second = [], []
    for k in range(SIDE):
        for j in range(SIDE):
            row = block_row(y, z, -j, -k, LEN)
            n = k * SIDE + j
            first.append(
                pltpu.make_async_copy(
                    pieces_a[k].at[j], w_buf.at[pl.ds(row, LEN), pl.ds(0, HALF_IN)], sems.at[n]
                )
            )
            second.append(
                pltpu.make_async_copy(
                    pieces_b[j].at[k],
                    w_buf.at[pl.ds(row, LEN), pl.ds(HALF_IN, HALF_IN)],
                    sems.at[16 + n],
                )
            )
    for copy in first + second:
        copy.start()

    @pl.loop(0, TOKENS // 32)
    def _(step):
        rows = pl.ds(pl.multiple_of(step * 32, 32), 32)
        values = x_ref[rows, :].astype(F32)
        center = values - jnp.mean(values, axis=-1, keepdims=True)
        rstd = lax.rsqrt(jnp.mean(center * center, axis=-1, keepdims=True) + EPSILON)
        normed[rows, :] = (center * rstd).astype(BF16)
        rstd_in[rows, :] = jnp.broadcast_to(rstd, (32, LEN))

    def columns(step):
        cols = pl.ds(pl.multiple_of(step * 256, 256), 256)
        pre = jnp.dot(normed[...], w_buf[:, cols], preferred_element_type=F32)
        squash = jax.nn.sigmoid(pre)
        act[:, cols] = (pre * squash).astype(BF16)
        slope[:, cols] = (squash * (1.0 + pre * (1.0 - squash))).astype(BF16)

    for copy in first:
        copy.wait()
    pl.loop(0, HALF_IN // 256)(columns)
    for copy in second:
        copy.wait()
    whole = pltpu.make_async_copy(w_buf, w_full, out_sem)
    whole.start()
    pl.loop(HALF_IN // 256, F1 // 256)(columns)

    quarter, half = lane_group(QK_DIM), lane_group(V_DIM)

    @pl.loop(0, TOKENS // LEN)
    def _(m):
        rows = pl.ds(pl.multiple_of(m * LEN, LEN), LEN)
        mask = wm_ref[m]
        for h4 in range(4):
            q4 = act[rows, QCOL + LEN * h4 : QCOL + LEN * (h4 + 1)]
            k4 = act[rows, KCOL + LEN * h4 : KCOL + LEN * (h4 + 1)]
            for pair in range(2):
                tile = 2 * h4 + pair
                v2 = act[rows, HV + LEN * tile : HV + LEN * (tile + 1)]
                total = jnp.zeros((LEN, LEN), F32)
                for e in range(2):
                    h = 2 * tile + e
                    score = mm(keep(quarter == 2 * pair + e, q4), k4, NT) * SCALE
                    squash = jax.nn.sigmoid(score)
                    weight = (score * squash * mask).astype(BF16)
                    attn[m, h] = weight
                    turn[m, h] = (
                        squash * (1.0 + score * (1.0 - squash)) * mask * SCALE
                    ).astype(BF16)
                    total += jnp.dot(weight, keep(half == e, v2), preferred_element_type=F32)
                mixed[:, LEN * tile : LEN * (tile + 1)] = total
        values = mixed[...]
        center = values - jnp.mean(values, axis=-1, keepdims=True)
        rstd = lax.rsqrt(jnp.mean(center * center, axis=-1, keepdims=True) + EPSILON)
        hat = center * rstd
        xhat[rows, :] = hat
        rstd_mid[rows, :] = jnp.broadcast_to(rstd, (LEN, LEN))
        gated[rows, :] = (hat * act[rows, :HV].astype(F32)).astype(BF16)

    whole.wait()


def front(place, inputs, masks, pieces_a, pieces_b):
    shapes = [
        ((TOKENS, D), BF16),
        ((TOKENS, F1), BF16),
        ((TOKENS, F1), BF16),
        ((2, HEADS, LEN, LEN), BF16),
        ((2, HEADS, LEN, LEN), BF16),
        ((TOKENS, HV), F32),
        ((TOKENS, HV), BF16),
        ((TOKENS, LEN), F32),
        ((TOKENS, LEN), F32),
        ((D, F1), BF16),
    ]
    return pl.pallas_call(
        front_kernel,
        out_shape=[jax.ShapeDtypeStruct(*s) for s in shapes],
        in_specs=[smem_spec(), vmem_spec(), vmem_spec()] + [any_spec()] * 8,
        out_specs=[vmem_spec()] * 9 + [any_spec()],
        scratch_shapes=[
            pltpu.VMEM((D, F1), BF16),
            pltpu.VMEM((LEN, HV), F32),
            pltpu.SemaphoreType.DMA((32,)),
            pltpu.SemaphoreType.DMA,
        ],
        compiler_params=pltpu.CompilerParams(vmem_limit_bytes=VMEM_LIMIT),
        cost_estimate=pl.CostEstimate(
            flops=2 * TOKENS * D * F1, bytes_accessed=40_000_000, transcendentals=1_500_000
        ),
        name="front",
    )(place, inputs, masks, *pieces_a, *pieces_b)


def arrange_kernel(place, *refs):
    pieces_a, pieces_b, full, sems = refs[0:4], refs[4:8], refs[8], refs[9]
    y, z = place[0], place[1]
    copies = []
    for k in range(SIDE):
        for j in range(SIDE):
            row = block_row(y, z, -j, -k, V_DIM)
            n = k * SIDE + j
            copies.append(
                pltpu.make_async_copy(
                    pieces_a[k].at[j], full.at[pl.ds(row, V_DIM), pl.ds(0, HALF_OUT)], sems.at[n]
                )
            )
            copies.append(
                pltpu.make_async_copy(
                    pieces_b[j].at[k],
                    full.at[pl.ds(row, V_DIM), pl.ds(HALF_OUT, HALF_OUT)],
                    sems.at[16 + n],
                )
            )
    for copy in copies:
        copy.start()
    for copy in copies:
        copy.wait()


def arrange(place, pieces_a, pieces_b):
    return pl.pallas_call(
        arrange_kernel,
        out_shape=jax.ShapeDtypeStruct((HV, D), BF16),
        in_specs=[smem_spec()] + [any_spec()] * 8,
        out_specs=any_spec(),
        scratch_shapes=[pltpu.SemaphoreType.DMA((32,))],
        compiler_params=pltpu.CompilerParams(vmem_limit_bytes=VMEM_LIMIT),
        cost_estimate=pl.CostEstimate(flops=0, bytes_accessed=8_400_000, transcendentals=0),
        name="arrange",
    )(place, *pieces_a, *pieces_b)


def chain_kernel(n_carried, info, *refs):
    incoming, top, w_in, w_out, normed, slope, act, attn, turn, xhat, rstd_in, rstd_mid = refs[:12]
    refs = refs[12 + n_carried :]
    outgoing, ups_out, gp_out, grads_out = refs[:4]
    (
        b_ups, b_win, b_wout, b_normed, b_slope, b_act, b_attn, b_turn, b_xhat, b_rin, b_rmid,
        gp, big, sems,
    ) = refs[4:]
    slot, dest, is_top = info[0], info[1], info[2]
    rows = pl.ds(pl.multiple_of(slot * LEN, LEN), LEN)
    dest_rows = pl.ds(pl.multiple_of(dest * LEN, LEN), LEN)

    get_top = pltpu.make_async_copy(top.at[rows, :], b_ups, sems.at[0])
    get_in = pltpu.make_async_copy(incoming, b_ups, sems.at[0])

    @pl.when(is_top == 1)
    def _():
        get_top.start()

    @pl.when(is_top == 0)
    def _():
        get_in.start()

    get_wout = pltpu.make_async_copy(w_out, b_wout, sems.at[1])
    get_wout.start()
    pairs = [
        (act.at[rows, :], b_act),
        (xhat.at[rows, :], b_xhat),
        (rstd_mid.at[rows, :], b_rmid),
        (slope.at[rows, :], b_slope),
        (attn.at[slot], b_attn),
        (turn.at[slot], b_turn),
        (w_in, b_win),
        (normed.at[rows, :], b_normed),
        (rstd_in.at[rows, :], b_rin),
    ]
    copies = [pltpu.make_async_copy(a, b, sems.at[2 + i]) for i, (a, b) in enumerate(pairs)]
    for copy in copies:
        copy.start()
    get_in.wait()
    get_wout.wait()
    put_ups = pltpu.make_async_copy(b_ups, ups_out.at[dest_rows, :], sems.at[12])
    put_ups.start()

    for c in range(HV // 256):
        big[:, 256 * c : 256 * (c + 1)] = mm(
            b_ups[...], b_wout[256 * c : 256 * (c + 1), :], NT
        )
    for copy in copies[:6]:
        copy.wait()
    grad_gated = big[:, :HV]
    hat = b_xhat[...]
    moved = grad_gated * b_act[:, :HV].astype(F32)
    mean_one = jnp.mean(moved, axis=-1, keepdims=True)
    mean_hat = jnp.mean(moved * hat, axis=-1, keepdims=True)
    gp[:, :HV] = (
        (grad_gated * hat).astype(BF16).astype(F32) * b_slope[:, :HV].astype(F32)
    ).astype(BF16)
    big[:, HV : 2 * HV] = b_rmid[:, :1] * (moved - mean_one - hat * mean_hat)

    quarter, half = lane_group(QK_DIM), lane_group(V_DIM)

    def put(value, col):
        cols = slice(col, col + LEN)
        gp[:, cols] = (
            value.astype(BF16).astype(F32) * b_slope[:, cols].astype(F32)
        ).astype(BF16)

    for h4 in range(4):
        q4 = b_act[:, QCOL + LEN * h4 : QCOL + LEN * (h4 + 1)]
        k4 = b_act[:, KCOL + LEN * h4 : KCOL + LEN * (h4 + 1)]
        grad_q = jnp.zeros((LEN, LEN), F32)
        grad_k = jnp.zeros((LEN, LEN), F32)
        for pair in range(2):
            tile = 2 * h4 + pair
            v2 = b_act[:, HV + LEN * tile : HV + LEN * (tile + 1)]
            g2 = big[:, HV + LEN * tile : HV + LEN * (tile + 1)].astype(BF16)
            grad_v = jnp.zeros((LEN, LEN), F32)
            for e in range(2):
                h = 2 * tile + e
                gh = keep(half == e, g2)
                grad_s = (mm(gh, v2, NT) * b_turn[h].astype(F32)).astype(BF16)
                grad_v += mm(b_attn[h], gh, TN)
                own = quarter == 2 * pair + e
                grad_q += jnp.dot(grad_s, keep(own, k4), preferred_element_type=F32)
                grad_k += mm(grad_s, keep(own, q4), TN)
            put(grad_v, HV + LEN * tile)
        put(grad_q, QCOL + LEN * h4)
        put(grad_k, KCOL + LEN * h4)

    put_gp = pltpu.make_async_copy(gp, gp_out.at[dest_rows, :], sems.at[13])
    put_gp.start()
    for copy in copies[6:]:
        copy.wait()
    for c in range(D // 256):
        big[:, 256 * c : 256 * (c + 1)] = mm(gp[...], b_win[256 * c : 256 * (c + 1), :], NT)
    @pl.loop(0, LEN // 32)
    def _(step):
        part = pl.ds(pl.multiple_of(step * 32, 32), 32)
        grad = big[part, :]
        hat_in = b_normed[part, :].astype(F32)
        one = jnp.mean(grad, axis=-1, keepdims=True)
        two = jnp.mean(grad * hat_in, axis=-1, keepdims=True)
        outgoing[part, :] = (
            b_ups[part, :].astype(F32) + b_rin[part, :1] * (grad - one - hat_in * two)
        ).astype(BF16)

    put_grads = pltpu.make_async_copy(outgoing, grads_out.at[dest_rows, :], sems.at[14])
    put_grads.start()
    put_ups.wait()
    put_gp.wait()
    put_grads.wait()


def chain_step(info, incoming, top, w_in, w_out, saved, carried):
    kept = [((3 * LEN, D), BF16), ((3 * LEN, F1), BF16), ((3 * LEN, D), BF16)]
    shapes = [((LEN, D), BF16)] + kept
    operands = [info, incoming, top, w_in, w_out, *saved, *carried]
    aliases = {13 + i: 1 + i for i in range(len(carried))}

    def kernel(*refs):
        chain_kernel(len(carried), *refs)

    return pl.pallas_call(
        kernel,
        out_shape=[jax.ShapeDtypeStruct(*s) for s in shapes],
        in_specs=[smem_spec()] + [any_spec()] * (len(operands) - 1),
        out_specs=[vmem_spec()] + [any_spec()] * 3,
        input_output_aliases=aliases,
        scratch_shapes=[
            pltpu.VMEM((LEN, D), BF16),
            pltpu.VMEM((D, F1), BF16),
            pltpu.VMEM((HV, D), BF16),
            pltpu.VMEM((LEN, D), BF16),
            pltpu.VMEM((LEN, F1), BF16),
            pltpu.VMEM((LEN, F1), BF16),
            pltpu.VMEM((HEADS, LEN, LEN), BF16),
            pltpu.VMEM((HEADS, LEN, LEN), BF16),
            pltpu.VMEM((LEN, HV), F32),
            pltpu.VMEM((LEN, LEN), F32),
            pltpu.VMEM((LEN, LEN), F32),
            pltpu.VMEM((LEN, F1), BF16),
            pltpu.VMEM((LEN, D), F32),
            pltpu.SemaphoreType.DMA((15,)),
        ],
        compiler_params=pltpu.CompilerParams(vmem_limit_bytes=VMEM_LIMIT),
        cost_estimate=pl.CostEstimate(
            flops=2 * LEN * D * (F1 + HV), bytes_accessed=22_000_000, transcendentals=0
        ),
        name="chain",
    )(*operands)


def weights_kernel(place, normed, gated, ups, gp, *refs):
    parts_a, parts_b, outs_a, outs_b = refs[0:4], refs[4:8], refs[8:12], refs[12:16]
    buf, buf_out, sems, sems_out = refs[16:20]
    y, z = place[0], place[1]
    for c in range(HV // 256):
        rows = slice(256 * c, 256 * (c + 1))
        buf_out[rows, :] = mm(gated[:, rows], ups[...], TN).astype(BF16)
    waits = []
    for k in range(SIDE):
        for j in range(SIDE):
            n = k * SIDE + j
            row = block_row(y, z, j, k, V_DIM)
            waits.append(
                pltpu.make_async_copy(
                    buf_out.at[pl.ds(row, V_DIM), pl.ds(0, HALF_OUT)],
                    outs_a[k].at[j],
                    sems_out.at[n],
                )
            )
            waits.append(
                pltpu.make_async_copy(
                    buf_out.at[pl.ds(row, V_DIM), pl.ds(HALF_OUT, HALF_OUT)],
                    outs_b[j].at[k],
                    sems_out.at[16 + n],
                )
            )
    for copy in waits:
        copy.start()
    pending = [None, None]
    for n in range(SIDE * SIDE):
        k, j = n // SIDE, n % SIDE
        turn = n % 2
        if pending[turn] is not None:
            for copy in pending[turn]:
                copy.wait()
        col = block_row(y, z, j, k, LEN)
        left = normed[:, pl.ds(col, LEN)]
        buf[turn] = mm(left, gp[...], TN).astype(BF16)
        pending[turn] = (
            pltpu.make_async_copy(
                buf.at[turn, :, pl.ds(0, HALF_IN)], parts_a[k].at[j], sems.at[2 * turn]
            ),
            pltpu.make_async_copy(
                buf.at[turn, :, pl.ds(HALF_IN, HALF_IN)], parts_b[j].at[k], sems.at[2 * turn + 1]
            ),
        )
        for copy in pending[turn]:
            copy.start()
    for two in pending:
        for copy in two:
            copy.wait()
    for copy in waits:
        copy.wait()


def weight_parts(place, normed, gated, ups, gp):
    shapes = [((SIDE, LEN, HALF_IN), BF16)] * 8 + [((SIDE, V_DIM, HALF_OUT), BF16)] * 8
    zero = lambda i: (0, 0)
    return pl.pallas_call(
        weights_kernel,
        grid=(1,),
        out_shape=[jax.ShapeDtypeStruct(*s) for s in shapes],
        in_specs=[
            smem_spec(),
            pl.BlockSpec((TOKENS, D), zero),
            pl.BlockSpec((TOKENS, HV), zero),
            pl.BlockSpec((TOKENS, D), zero),
            pl.BlockSpec((TOKENS, F1), zero),
        ],
        out_specs=[any_spec()] * 16,
        scratch_shapes=[
            pltpu.VMEM((2, LEN, F1), BF16),
            pltpu.VMEM((HV, D), BF16),
            pltpu.SemaphoreType.DMA((4,)),
            pltpu.SemaphoreType.DMA((32,)),
        ],
        compiler_params=pltpu.CompilerParams(vmem_limit_bytes=VMEM_LIMIT),
        cost_estimate=pl.CostEstimate(
            flops=2 * TOKENS * D * (F1 + HV), bytes_accessed=20_000_000, transcendentals=0
        ),
        name="weight_parts",
    )(place, normed, gated, ups, gp)


def gathered(shard, x, cut):
    other = send(shard, 0, 0, 1)
    block = jnp.where(
        x == 0, jnp.concatenate([shard, other], 0), jnp.concatenate([other, shard], 0)
    )
    half_a, half_b = block[:, :cut], block[:, cut:]
    a_one = jnp.stack([half_a] + [send(half_a, j, 0, 0) for j in (1, 2, 3)])
    b_one = jnp.stack([half_b] + [send(half_b, 0, k, 0) for k in (1, 2, 3)])
    pieces_a = [a_one] + [send(a_one, 0, k, 0) for k in (1, 2, 3)]
    pieces_b = [b_one] + [send(b_one, j, 0, 0) for j in (1, 2, 3)]
    return pieces_a, pieces_b


def added(arrays):
    total = arrays[0].astype(F32)
    for array in arrays[1:]:
        total = total + array.astype(F32)
    return total


def scattered(parts_a, parts_b, x):
    a_one = added([parts_a[0]] + [send(parts_a[k], 0, k, 0) for k in (1, 2, 3)]).astype(BF16)
    b_one = added([parts_b[0]] + [send(parts_b[j], j, 0, 0) for j in (1, 2, 3)]).astype(BF16)
    a_two = added([a_one[0]] + [send(a_one[j], j, 0, 0) for j in (1, 2, 3)])
    b_two = added([b_one[0]] + [send(b_one[k], 0, k, 0) for k in (1, 2, 3)])
    block = jnp.concatenate([a_two, b_two], 1)
    rows = block.shape[0] // 2
    away = lax.dynamic_slice_in_dim(block, (1 - x) * rows, rows, 0).astype(BF16)
    stay = lax.dynamic_slice_in_dim(block, x * rows, rows, 0)
    return stay + send(away, 0, 0, 1).astype(F32)


def body(section_input, top_grad, w_in, w_out, segments):
    section = lax.axis_index("pipe")
    spot = lax.axis_index("dp")
    y, z, x = spot // 8, (spot // 2) % 4, spot % 2
    place = jnp.stack([y, z]).astype(jnp.int32)
    in_a, in_b = gathered(w_in[0], x, HALF_IN)
    out_a, out_b = gathered(w_out[0], x, HALF_OUT)

    same = segments[:, :, None] == segments[:, None, :]
    lower = lax.broadcasted_iota(jnp.int32, (LEN, LEN), 1) <= lax.broadcasted_iota(
        jnp.int32, (LEN, LEN), 0
    )
    counts = jnp.sum(same.astype(F32), axis=2, keepdims=True)
    masks = jnp.where(jnp.logical_and(same, lower[None]), 1.0 / counts, 0.0)

    normed, slope, act, attn, turn, xhat, gated, rstd_in, rstd_mid, w_first = front(
        place, section_input[0], masks, in_a, in_b
    )
    w_second = arrange(place, out_a, out_b)
    saved = (normed, slope, act, attn, turn, xhat, rstd_in, rstd_mid)

    incoming = top_grad[:LEN]
    carried = ()
    for step in range(5):
        slot = step - (3 - section)
        real = jnp.logical_and(slot >= 0, slot < 2)
        info = jnp.stack(
            [jnp.clip(slot, 0, 1), jnp.where(real, slot, 2), jnp.where(section == 3, 1, 0)]
        ).astype(jnp.int32)
        outgoing, *carried = chain_step(
            info, incoming, top_grad, w_first, w_second, saved, tuple(carried)
        )
        if step < 4:
            incoming = lax.ppermute(outgoing, "pipe", [(1, 0), (2, 1), (3, 2)])
    ups, gp, grads = carried

    parts = weight_parts(place, normed, gated, ups, gp)
    grad_first = scattered(parts[0:4], parts[4:8], x)
    grad_out = scattered(parts[8:12], parts[12:16], x)
    return (grads[None, :TOKENS], grad_first[None], grad_out[None])


def solution(mesh):
    return jax.shard_map(
        body,
        mesh=mesh,
        in_specs=(
            P("pipe", "dp", None),
            P("dp", None),
            P("pipe", "dp", None),
            P("pipe", "dp", None),
            P("dp", None),
        ),
        out_specs=(P("pipe", "dp", None), P("pipe", "dp", None), P("pipe", "dp", None)),
        check_vma=False,
    )
```

```python
import jax
import jax.numpy as jnp
from jax import lax
from jax.experimental import pallas as pl
from jax.experimental.pallas import tpu as pltpu
from jax.sharding import PartitionSpec as P

HEADS = 16
QK_DIM = 32
V_DIM = 64
EPSILON = 1e-05
D = 2048
HV = 1024
F1 = 3072
QCOL = 2 * HV
KCOL = QCOL + HEADS * QK_DIM
LEN = 128
TOKENS = 256
SIDE = 4
HALF_IN = F1 // 2
HALF_OUT = D // 2
FOLD = HALF_OUT // 2
PACK = HALF_IN + FOLD
SCALE = QK_DIM ** (-0.5)
VMEM_LIMIT = 56 * 1024 * 1024
BF16 = jnp.bfloat16
F32 = jnp.float32

NT = (((1,), (1,)), ((), ()))
TN = (((0,), (0,)), ((), ()))


def mm(left, right, dims):
    return lax.dot_general(left, right, dims, preferred_element_type=F32)


def shifted(dy, dz, dx):
    pairs = []
    for i in range(32):
        y, z, x = i // 8, (i // 2) % 4, i % 2
        pairs.append((i, ((y + dy) % 4 * 4 + (z + dz) % 4) * 2 + (x + dx) % 2))
    return pairs


def send(array, dy, dz, dx):
    return lax.ppermute(array, "dp", shifted(dy, dz, dx))


def any_spec():
    return pl.BlockSpec(memory_space=pl.ANY)


def smem_spec():
    return pl.BlockSpec(memory_space=pltpu.SMEM)


def vmem_spec():
    return pl.BlockSpec(memory_space=pltpu.VMEM)


def block_row(y, z, dy, dz, rows):
    cell = lax.rem(y + dy + SIDE, SIDE) * SIDE + lax.rem(z + dz + SIDE, SIDE)
    return pl.multiple_of(cell * rows, rows)


def lane_group(width):
    return lax.broadcasted_iota(jnp.int32, (LEN, LEN), 1) // width


def keep(mask, tile):
    return jnp.where(mask, tile, jnp.zeros_like(tile))


def piece_blocks(pieces):
    own, plus, minus, far_low, far_high = pieces
    found = []
    for j in range(SIDE):
        found.append((own.at[j], j, 0))
        found.append((plus.at[j], j, 1))
        found.append((minus.at[j], j, 3))
        found.append((far_low.at[j] if j < 2 else far_high.at[j - 2], j, 2))
    return found


def front_kernel(place, x_ref, wm_ref, *refs):
    normed, slope, act, attn, turn, xhat, gated, rstd_in, rstd_mid, w_full = refs[10:20]
    w_buf, mixed, sems, out_sem = refs[20:24]
    y, z = place[0], place[1]
    first, second = [], []
    for n, (block, j, k) in enumerate(piece_blocks(refs[0:5])):
        row = block_row(y, z, -j, -k, LEN)
        spot = w_buf.at[pl.ds(row, LEN), pl.ds(0, HALF_IN)]
        first.append(pltpu.make_async_copy(block, spot, sems.at[n]))
    for n, (block, k, j) in enumerate(piece_blocks(refs[5:10])):
        row = block_row(y, z, -j, -k, LEN)
        spot = w_buf.at[pl.ds(row, LEN), pl.ds(HALF_IN, HALF_IN)]
        second.append(pltpu.make_async_copy(block, spot, sems.at[16 + n]))
    for copy in first + second:
        copy.start()

    @pl.loop(0, TOKENS // 32)
    def _(step):
        rows = pl.ds(pl.multiple_of(step * 32, 32), 32)
        values = x_ref[rows, :].astype(F32)
        center = values - jnp.mean(values, axis=-1, keepdims=True)
        rstd = lax.rsqrt(jnp.mean(center * center, axis=-1, keepdims=True) + EPSILON)
        normed[rows, :] = (center * rstd).astype(BF16)
        rstd_in[rows, :] = jnp.broadcast_to(rstd, (32, LEN))

    def columns(step):
        cols = pl.ds(pl.multiple_of(step * 256, 256), 256)
        pre = jnp.dot(normed[...], w_buf[:, cols], preferred_element_type=F32)
        squash = jax.nn.sigmoid(pre)
        act[:, cols] = (pre * squash).astype(BF16)
        slope[:, cols] = (squash * (1.0 + pre * (1.0 - squash))).astype(BF16)

    for copy in first:
        copy.wait()
    pl.loop(0, HALF_IN // 256)(columns)
    for copy in second:
        copy.wait()
    whole = pltpu.make_async_copy(w_buf, w_full, out_sem)
    whole.start()
    pl.loop(HALF_IN // 256, F1 // 256)(columns)

    quarter, half = lane_group(QK_DIM), lane_group(V_DIM)

    @pl.loop(0, TOKENS // LEN)
    def _(m):
        rows = pl.ds(pl.multiple_of(m * LEN, LEN), LEN)
        mask = wm_ref[m]
        for h4 in range(4):
            q4 = act[rows, QCOL + LEN * h4 : QCOL + LEN * (h4 + 1)]
            k4 = act[rows, KCOL + LEN * h4 : KCOL + LEN * (h4 + 1)]
            for pair in range(2):
                tile = 2 * h4 + pair
                v2 = act[rows, HV + LEN * tile : HV + LEN * (tile + 1)]
                total = jnp.zeros((LEN, LEN), F32)
                for e in range(2):
                    h = 2 * tile + e
                    score = mm(keep(quarter == 2 * pair + e, q4), k4, NT) * SCALE
                    squash = jax.nn.sigmoid(score)
                    weight = (score * squash * mask).astype(BF16)
                    attn[m, h] = weight
                    turn[m, h] = (
                        squash * (1.0 + score * (1.0 - squash)) * mask * SCALE
                    ).astype(BF16)
                    total += jnp.dot(weight, keep(half == e, v2), preferred_element_type=F32)
                mixed[:, LEN * tile : LEN * (tile + 1)] = total
        values = mixed[...]
        center = values - jnp.mean(values, axis=-1, keepdims=True)
        rstd = lax.rsqrt(jnp.mean(center * center, axis=-1, keepdims=True) + EPSILON)
        hat = center * rstd
        xhat[rows, :] = hat
        rstd_mid[rows, :] = jnp.broadcast_to(rstd, (LEN, LEN))
        gated[rows, :] = (hat * act[rows, :HV].astype(F32)).astype(BF16)

    whole.wait()


def front(place, inputs, masks, pieces_a, pieces_b):
    shapes = [
        ((TOKENS, D), BF16),
        ((TOKENS, F1), BF16),
        ((TOKENS, F1), BF16),
        ((2, HEADS, LEN, LEN), BF16),
        ((2, HEADS, LEN, LEN), BF16),
        ((TOKENS, HV), F32),
        ((TOKENS, HV), BF16),
        ((TOKENS, LEN), F32),
        ((TOKENS, LEN), F32),
        ((D, F1), BF16),
    ]
    return pl.pallas_call(
        front_kernel,
        out_shape=[jax.ShapeDtypeStruct(*s) for s in shapes],
        in_specs=[smem_spec(), vmem_spec(), vmem_spec()] + [any_spec()] * 10,
        out_specs=[vmem_spec()] * 9 + [any_spec()],
        scratch_shapes=[
            pltpu.VMEM((D, F1), BF16),
            pltpu.VMEM((LEN, HV), F32),
            pltpu.SemaphoreType.DMA((32,)),
            pltpu.SemaphoreType.DMA,
        ],
        compiler_params=pltpu.CompilerParams(vmem_limit_bytes=VMEM_LIMIT),
        cost_estimate=pl.CostEstimate(
            flops=2 * TOKENS * D * F1, bytes_accessed=40_000_000, transcendentals=1_500_000
        ),
        name="front",
    )(place, inputs, masks, *pieces_a, *pieces_b)


def arrange_kernel(place, *refs):
    full, sems = refs[10], refs[11]
    y, z = place[0], place[1]
    copies = []
    for half in range(2):
        for block, i, o in piece_blocks(refs[5 * half : 5 * half + 5]):
            j, k = (i, o) if half == 0 else (o, i)
            row = block_row(y, z, -j, -k, V_DIM)
            for fold in range(2):
                spot = full.at[pl.ds(row, V_DIM), pl.ds(HALF_OUT * half + FOLD * fold, FOLD)]
                copies.append(
                    pltpu.make_async_copy(
                        block.at[pl.ds(V_DIM * fold, V_DIM), :], spot, sems.at[len(copies)]
                    )
                )
    for copy in copies:
        copy.start()
    for copy in copies:
        copy.wait()


def arrange(place, pieces_a, pieces_b):
    return pl.pallas_call(
        arrange_kernel,
        out_shape=jax.ShapeDtypeStruct((HV, D), BF16),
        in_specs=[smem_spec()] + [any_spec()] * 10,
        out_specs=vmem_spec(),
        scratch_shapes=[pltpu.SemaphoreType.DMA((64,))],
        compiler_params=pltpu.CompilerParams(vmem_limit_bytes=VMEM_LIMIT),
        cost_estimate=pl.CostEstimate(flops=0, bytes_accessed=8_400_000, transcendentals=0),
        name="arrange",
    )(place, *pieces_a, *pieces_b)


def chain_body(n_sources, n_carried, info, *refs):
    sources, refs = refs[:n_sources], refs[n_sources:]
    w_in, w_out, normed, slope, act, attn, turn, xhat, rstd_in, rstd_mid = refs[:10]
    refs = refs[10 + n_carried :]
    outgoing, ups_out, gp_out, grads_out = refs[:4]
    (
        b_ups, b_win, b_wout, b_normed, b_slope, b_act, b_attn, b_turn, b_xhat, b_rin, b_rmid,
        gp, big, sems,
    ) = refs[4:]
    slot, source = info[0], info[1]
    rows = pl.ds(pl.multiple_of(slot * LEN, LEN), LEN)
    gets = []
    for i, ref in enumerate(sources):
        held = ref.at[rows, :] if i == 0 else ref
        gets.append(pltpu.make_async_copy(held, b_ups, sems.at[0]))
        pl.when(source == i)(gets[i].start)
    get_wout = pltpu.make_async_copy(w_out, b_wout, sems.at[1])
    get_wout.start()
    pairs = [
        (act.at[rows, :], b_act),
        (xhat.at[rows, :], b_xhat),
        (rstd_mid.at[rows, :], b_rmid),
        (slope.at[rows, :], b_slope),
        (attn.at[slot], b_attn),
        (turn.at[slot], b_turn),
        (w_in, b_win),
        (normed.at[rows, :], b_normed),
        (rstd_in.at[rows, :], b_rin),
    ]
    copies = [pltpu.make_async_copy(a, b, sems.at[2 + i]) for i, (a, b) in enumerate(pairs)]
    for copy in copies:
        copy.start()
    gets[0].wait()
    get_wout.wait()
    put_ups = pltpu.make_async_copy(b_ups, ups_out.at[rows, :], sems.at[12])
    put_ups.start()

    for c in range(HV // 256):
        big[:, 256 * c : 256 * (c + 1)] = mm(
            b_ups[...], b_wout[256 * c : 256 * (c + 1), :], NT
        )
    for copy in copies[:6]:
        copy.wait()
    grad_gated = big[:, :HV]
    hat = b_xhat[...]
    moved = grad_gated * b_act[:, :HV].astype(F32)
    mean_one = jnp.mean(moved, axis=-1, keepdims=True)
    mean_hat = jnp.mean(moved * hat, axis=-1, keepdims=True)
    gp[:, :HV] = (
        (grad_gated * hat).astype(BF16).astype(F32) * b_slope[:, :HV].astype(F32)
    ).astype(BF16)
    big[:, HV : 2 * HV] = b_rmid[:, :1] * (moved - mean_one - hat * mean_hat)

    quarter, half = lane_group(QK_DIM), lane_group(V_DIM)

    def put(value, col):
        cols = slice(col, col + LEN)
        gp[:, cols] = (
            value.astype(BF16).astype(F32) * b_slope[:, cols].astype(F32)
        ).astype(BF16)

    for h4 in range(4):
        q4 = b_act[:, QCOL + LEN * h4 : QCOL + LEN * (h4 + 1)]
        k4 = b_act[:, KCOL + LEN * h4 : KCOL + LEN * (h4 + 1)]
        grad_q = jnp.zeros((LEN, LEN), F32)
        grad_k = jnp.zeros((LEN, LEN), F32)
        for pair in range(2):
            tile = 2 * h4 + pair
            v2 = b_act[:, HV + LEN * tile : HV + LEN * (tile + 1)]
            g2 = big[:, HV + LEN * tile : HV + LEN * (tile + 1)].astype(BF16)
            grad_v = jnp.zeros((LEN, LEN), F32)
            for e in range(2):
                h = 2 * tile + e
                gh = keep(half == e, g2)
                grad_s = (mm(gh, v2, NT) * b_turn[h].astype(F32)).astype(BF16)
                grad_v += mm(b_attn[h], gh, TN)
                own = quarter == 2 * pair + e
                grad_q += jnp.dot(grad_s, keep(own, k4), preferred_element_type=F32)
                grad_k += mm(grad_s, keep(own, q4), TN)
            put(grad_v, HV + LEN * tile)
        put(grad_q, QCOL + LEN * h4)
        put(grad_k, KCOL + LEN * h4)

    put_gp = pltpu.make_async_copy(gp, gp_out.at[rows, :], sems.at[13])
    put_gp.start()
    for copy in copies[6:]:
        copy.wait()
    for c in range(D // 256):
        big[:, 256 * c : 256 * (c + 1)] = mm(gp[...], b_win[256 * c : 256 * (c + 1), :], NT)
    @pl.loop(0, LEN // 32)
    def _(step):
        part = pl.ds(pl.multiple_of(step * 32, 32), 32)
        grad = big[part, :]
        hat_in = b_normed[part, :].astype(F32)
        one = jnp.mean(grad, axis=-1, keepdims=True)
        two = jnp.mean(grad * hat_in, axis=-1, keepdims=True)
        outgoing[part, :] = (
            b_ups[part, :].astype(F32) + b_rin[part, :1] * (grad - one - hat_in * two)
        ).astype(BF16)

    put_grads = pltpu.make_async_copy(outgoing, grads_out.at[rows, :], sems.at[14])
    put_grads.start()
    put_ups.wait()
    put_gp.wait()
    put_grads.wait()


def chain_step(info, sources, w_in, w_out, saved, carried):
    kept = [((TOKENS, D), BF16), ((TOKENS, F1), BF16), ((TOKENS, D), BF16)]
    shapes = [((LEN, D), BF16)] + kept
    operands = [info, *sources, w_in, w_out, *saved, *carried]
    before = len(operands) - len(carried)
    aliases = {before + i: 1 + i for i in range(len(carried))}

    def kernel(info, *refs):
        @pl.when(info[2] == 1)
        def _():
            chain_body(len(sources), len(carried), info, *refs)

    return pl.pallas_call(
        kernel,
        out_shape=[jax.ShapeDtypeStruct(*s) for s in shapes],
        in_specs=[smem_spec()] + [any_spec()] * (len(operands) - 1),
        out_specs=[vmem_spec()] + [any_spec()] * 3,
        input_output_aliases=aliases,
        scratch_shapes=[
            pltpu.VMEM((LEN, D), BF16),
            pltpu.VMEM((D, F1), BF16),
            pltpu.VMEM((HV, D), BF16),
            pltpu.VMEM((LEN, D), BF16),
            pltpu.VMEM((LEN, F1), BF16),
            pltpu.VMEM((LEN, F1), BF16),
            pltpu.VMEM((HEADS, LEN, LEN), BF16),
            pltpu.VMEM((HEADS, LEN, LEN), BF16),
            pltpu.VMEM((LEN, HV), F32),
            pltpu.VMEM((LEN, LEN), F32),
            pltpu.VMEM((LEN, LEN), F32),
            pltpu.VMEM((LEN, F1), BF16),
            pltpu.VMEM((LEN, D), F32),
            pltpu.SemaphoreType.DMA((15,)),
        ],
        compiler_params=pltpu.CompilerParams(vmem_limit_bytes=VMEM_LIMIT),
        cost_estimate=pl.CostEstimate(
            flops=2 * LEN * D * (F1 + HV), bytes_accessed=22_000_000, transcendentals=0
        ),
        name="chain",
    )(*operands)


def weights_kernel(jobs, place, normed_t, gated_t, ups, gp, *refs):
    outs, (buf_in, buf_out, sems) = refs[: len(jobs)], refs[len(jobs) :]
    y, z = place[0], place[1]
    pending = [None, None]
    count = 0
    for out, (half, blocks) in zip(outs, jobs):
        for at, (dy, dz) in enumerate(blocks):
            turn = count % 2
            count += 1
            if pending[turn] is not None:
                for copy in pending[turn]:
                    copy.wait()
            row = block_row(y, z, dy, dz, LEN)
            left = normed_t[pl.ds(row, LEN), :]
            right = gp[:, HALF_IN * half : HALF_IN * (half + 1)]
            buf_in[turn] = jnp.dot(left, right, preferred_element_type=F32).astype(BF16)
            row = block_row(y, z, dy, dz, V_DIM)
            left = gated_t[pl.ds(row, V_DIM), :]
            right = ups[:, HALF_OUT * half : HALF_OUT * (half + 1)]
            buf_out[turn] = jnp.dot(left, right, preferred_element_type=F32).astype(BF16)
            copies = [
                pltpu.make_async_copy(
                    buf_in.at[turn], out.at[at, :, pl.ds(0, HALF_IN)], sems.at[turn, 0]
                )
            ]
            for fold in range(2):
                copies.append(
                    pltpu.make_async_copy(
                        buf_out.at[turn, :, pl.ds(FOLD * fold, FOLD)],
                        out.at[at, pl.ds(V_DIM * fold, V_DIM), pl.ds(HALF_IN, FOLD)],
                        sems.at[turn, 1 + fold],
                    )
                )
            for copy in copies:
                copy.start()
            pending[turn] = copies
    for copies in pending:
        for copy in copies:
            copy.wait()


def weight_parts(name, jobs, place, normed_t, gated_t, ups, gp):
    blocks = sum(len(job[1]) for job in jobs)
    return pl.pallas_call(
        lambda *refs: weights_kernel(jobs, *refs),
        out_shape=[jax.ShapeDtypeStruct((len(job[1]), LEN, PACK), BF16) for job in jobs],
        in_specs=[smem_spec()] + [vmem_spec()] * 4,
        out_specs=[any_spec()] * len(jobs),
        scratch_shapes=[
            pltpu.VMEM((2, LEN, HALF_IN), BF16),
            pltpu.VMEM((2, V_DIM, HALF_OUT), BF16),
            pltpu.SemaphoreType.DMA((2, 3)),
        ],
        compiler_params=pltpu.CompilerParams(vmem_limit_bytes=VMEM_LIMIT),
        cost_estimate=pl.CostEstimate(
            flops=2 * TOKENS * LEN * PACK * blocks,
            bytes_accessed=4_000_000 + 2 * LEN * PACK * blocks,
            transcendentals=0,
        ),
        name=name,
    )(place, normed_t, gated_t, ups, gp)


FAR_JOBS = (
    (0, ((0, 2), (1, 2))),
    (0, ((2, 2), (3, 2))),
    (1, ((2, 0), (2, 1))),
    (1, ((2, 2), (2, 3))),
)
NEAR_JOBS = (
    (0, ((0, 1), (1, 1), (2, 1), (3, 1))),
    (0, ((0, 3), (1, 3), (2, 3), (3, 3))),
    (1, ((1, 0), (1, 1), (1, 2), (1, 3))),
    (1, ((3, 0), (3, 1), (3, 2), (3, 3))),
    (0, ((0, 0), (1, 0), (2, 0), (3, 0))),
    (1, ((0, 0), (0, 1), (0, 2), (0, 3))),
)


def along(axis, by):
    return (by, 0, 0) if axis == "y" else (0, by, 0)


def spread(block, axis):
    half = block.shape[0] // 2
    plus = send(block, *along(axis, 1))
    minus = send(block, *along(axis, -1))
    far_low = send(plus[:half], *along(axis, 1))
    far_high = send(minus[half:], *along(axis, -1))
    return plus, minus, far_low, far_high


def lined(block, axis):
    plus, minus, far_low, far_high = spread(block, axis)
    return jnp.stack([block, plus, jnp.concatenate([far_low, far_high], 0), minus])


def gathered(first, second, x):
    packed = jnp.concatenate([first, jnp.concatenate([second[:, :HALF_OUT], second[:, HALF_OUT:]], 0)], 1)
    other = send(packed, 0, 0, 1)
    low = jnp.where(x == 0, packed, other)
    high = jnp.where(x == 0, other, packed)
    rows = second.shape[0]
    lines = []
    for half in range(2):
        cols = slice(HALF_IN * half, HALF_IN * (half + 1))
        part = slice(rows * half, rows * (half + 1))
        out = jnp.concatenate([low[part, F1:], high[part, F1:]], 0)
        block = jnp.concatenate(
            [
                jnp.concatenate([low[:, cols], high[:, cols]], 0),
                jnp.concatenate([out[:, :FOLD], out[:, FOLD:]], 0),
            ],
            1,
        )
        lines.append(lined(block, "yz"[half]))
    pieces = []
    late = jnp.zeros((), BF16)
    for cols in (slice(0, HALF_IN), slice(HALF_IN, PACK)):
        for half in range(2):
            line = lines[half][:, :, cols] + late
            pieces.append((line, *spread(line, "zy"[half])))
        if cols.start == 0:
            late = sum(jnp.minimum(jnp.abs(p[i][0, 0, 0]), 0.0) for p in pieces for i in (3, 4))
    return pieces


def added(*arrays):
    total = arrays[0].astype(F32)
    for array in arrays[1:]:
        total = total + array.astype(F32)
    return total


def joined(own, plus, minus, far_low, far_high, axis):
    half = far_low.shape[0]
    through = send(far_low, *along(axis, 1))
    back = send(far_high, *along(axis, -1))
    plus = jnp.concatenate([added(plus[:half], through).astype(BF16), plus[half:]], 0)
    minus = jnp.concatenate([minus[:half], added(minus[half:], back).astype(BF16)], 0)
    return added(own, send(plus, *along(axis, 1)), send(minus, *along(axis, -1)))


def scattered(far, near, x):
    a_one = joined(near[4], near[0], near[1], far[0], far[1], "z").astype(BF16)
    b_one = joined(near[5], near[2], near[3], far[2], far[3], "y").astype(BF16)
    ends = []
    for line, axis in ((a_one, "y"), (b_one, "z")):
        ends.append(joined(line[0], line[1], line[3], line[2, :V_DIM], line[2, V_DIM:], axis))
    first = jnp.concatenate([end[:, :HALF_IN] for end in ends], 1)
    folded = jnp.concatenate([end[:, HALF_IN:] for end in ends], 1)
    outs = [folded[:V_DIM, :FOLD], folded[V_DIM:, :FOLD], folded[:V_DIM, FOLD:], folded[V_DIM:, FOLD:]]
    second = jnp.concatenate(outs, 1)
    sides = []
    for side in range(2):
        mine = second[32 * side : 32 * (side + 1)]
        tall = jnp.concatenate([mine[:, :HALF_OUT], mine[:, HALF_OUT:]], 0)
        sides.append(jnp.concatenate([first[64 * side : 64 * (side + 1)], tall], 1))
    away = jnp.where(x == 0, sides[1], sides[0]).astype(BF16)
    total = jnp.where(x == 0, sides[0], sides[1]) + send(away, 0, 0, 1).astype(F32)
    grad_out = jnp.concatenate([total[:32, F1:], total[32:, F1:]], 1)
    return total[:, :F1], grad_out


def body(section_input, top_grad, w_in, w_out, segments):
    section = lax.axis_index("pipe")
    spot = lax.axis_index("dp")
    y, z, x = spot // 8, (spot // 2) % 4, spot % 2
    place = jnp.stack([y, z]).astype(jnp.int32)
    in_a, in_b, out_a, out_b = gathered(w_in[0], w_out[0], x)

    same = segments[:, :, None] == segments[:, None, :]
    lower = lax.broadcasted_iota(jnp.int32, (LEN, LEN), 1) <= lax.broadcasted_iota(
        jnp.int32, (LEN, LEN), 0
    )
    counts = jnp.sum(same.astype(F32), axis=2, keepdims=True)
    masks = jnp.where(jnp.logical_and(same, lower[None]), 1.0 / counts, 0.0)

    normed, slope, act, attn, turn, xhat, gated, rstd_in, rstd_mid, w_first = front(
        place, section_input[0], masks, in_a, in_b
    )
    after = (rstd_in[0, 0] < 0.0).astype(jnp.int32)
    w_second = arrange(place + after, out_a, out_b)
    saved = (normed, slope, act, attn, turn, xhat, rstd_in, rstd_mid)

    def step(slots, sources, carried):
        slot, source, busy = jnp.int32(0), jnp.int32(0), jnp.int32(0)
        for which, (own, origin) in slots.items():
            slot = jnp.where(section == which, own, slot)
            source = jnp.where(section == which, origin, source)
            busy = jnp.where(section == which, 1, busy)
        info = jnp.stack([slot, source, busy]).astype(jnp.int32)
        outgoing, *carried = chain_step(
            info, (top_grad, *sources), w_first, w_second, saved, tuple(carried)
        )
        return outgoing, carried

    def below(array, which):
        return lax.ppermute(array, "pipe", [(which, which - 1)])

    out_0, carried = step({3: (0, 0)}, (), ())
    out_1, carried = step({3: (1, 0), 2: (0, 1)}, (below(out_0, 3),), carried)
    to_one = below(out_1, 2)
    out_2, carried = step({2: (1, 1)}, (below(out_1, 3),), carried)
    again = below(out_2, 2)
    out_3, carried = step({1: (0, 1)}, (to_one,), carried)
    out_4, carried = step({1: (1, 1), 0: (0, 2)}, (again, below(out_3, 1)), carried)
    _, carried = step({0: (1, 1)}, (below(out_4, 1),), carried)
    ups, gp, grads = carried

    normed_t, gated_t = normed.T, gated.T
    far = weight_parts("far_parts", FAR_JOBS, place, normed_t, gated_t, ups, gp)
    near = weight_parts("near_parts", NEAR_JOBS, place, normed_t, gated_t, ups, gp)
    grad_first, grad_out = scattered(far, near, x)
    return (grads[None], grad_first[None], grad_out[None])


def solution(mesh):
    return jax.shard_map(
        body,
        mesh=mesh,
        in_specs=(
            P("pipe", "dp", None),
            P("dp", None),
            P("pipe", "dp", None),
            P("pipe", "dp", None),
            P("dp", None),
        ),
        out_specs=(P("pipe", "dp", None), P("pipe", "dp", None), P("pipe", "dp", None)),
        check_vma=False,
    )
```

```python
import jax
import jax.numpy as jnp
from jax import lax
from jax.experimental import pallas as pl
from jax.experimental.pallas import tpu as pltpu
from jax.sharding import PartitionSpec as P

HEADS = 16
QK_DIM = 32
V_DIM = 64
EPSILON = 1e-05
D = 2048
HV = 1024
F1 = 3072
QCOL = 2 * HV
KCOL = QCOL + HEADS * QK_DIM
LEN = 128
TOKENS = 256
SIDE = 4
HALF_IN = F1 // 2
HALF_OUT = D // 2
FOLD = HALF_OUT // 2
PACK = HALF_IN + FOLD
SCALE = QK_DIM ** (-0.5)
VMEM_LIMIT = 16 * 1024 * 1024
BF16 = jnp.bfloat16
F32 = jnp.float32

NT = (((1,), (1,)), ((), ()))
TN = (((0,), (0,)), ((), ()))


def mm(left, right, dims):
    return lax.dot_general(left, right, dims, preferred_element_type=F32)


def shifted(dy, dz, dx):
    pairs = []
    for i in range(32):
        y, z, x = i // 8, (i // 2) % 4, i % 2
        pairs.append((i, ((y + dy) % 4 * 4 + (z + dz) % 4) * 2 + (x + dx) % 2))
    return pairs


def send(array, dy, dz, dx):
    return lax.ppermute(array, "dp", shifted(dy, dz, dx))


def any_spec():
    return pl.BlockSpec(memory_space=pl.ANY)


def smem_spec():
    return pl.BlockSpec(memory_space=pltpu.SMEM)


def vmem_spec():
    return pl.BlockSpec(memory_space=pltpu.VMEM)


def block_row(y, z, dy, dz, rows):
    cell = lax.rem(y + dy + SIDE, SIDE) * SIDE + lax.rem(z + dz + SIDE, SIDE)
    return pl.multiple_of(cell * rows, rows)


def lane_group(width):
    return lax.broadcasted_iota(jnp.int32, (LEN, LEN), 1) // width


def keep(mask, tile):
    return jnp.where(mask, tile, jnp.zeros_like(tile))


def piece_blocks(pieces):
    own, plus, minus, far_low, far_high = pieces
    found = []
    for j in range(SIDE):
        found.append((own.at[j], j, 0))
        found.append((plus.at[j], j, 1))
        found.append((minus.at[j], j, 3))
        found.append(((far_low if j < 2 else far_high).at[j % far_low.shape[0]], j, 2))
    return found


def front_kernel(place, x_ref, wm_ref, *refs):
    normed, slope, act, attn, turn, xhat, gated, rstd_in, rstd_mid, w_buf = refs[10:20]
    mixed, sems = refs[20:22]
    y, z = place[0], place[1]
    first, second = [], []
    for n, (block, j, k) in enumerate(piece_blocks(refs[0:5])):
        row = block_row(y, z, -j, -k, LEN)
        spot = w_buf.at[pl.ds(row, LEN), pl.ds(0, HALF_IN)]
        first.append(pltpu.make_async_copy(block, spot, sems.at[n]))
    for n, (block, k, j) in enumerate(piece_blocks(refs[5:10])):
        row = block_row(y, z, -j, -k, LEN)
        spot = w_buf.at[pl.ds(row, LEN), pl.ds(HALF_IN, HALF_IN)]
        second.append(pltpu.make_async_copy(block, spot, sems.at[16 + n]))
    for copy in first + second:
        copy.start()

    @pl.loop(0, TOKENS // 32)
    def _(step):
        rows = pl.ds(pl.multiple_of(step * 32, 32), 32)
        values = x_ref[rows, :].astype(F32)
        center = values - jnp.mean(values, axis=-1, keepdims=True)
        rstd = lax.rsqrt(jnp.mean(center * center, axis=-1, keepdims=True) + EPSILON)
        normed[rows, :] = (center * rstd).astype(BF16)
        rstd_in[rows, :] = jnp.broadcast_to(rstd, (32, LEN))

    def columns(step):
        cols = pl.ds(pl.multiple_of(step * 256, 256), 256)
        pre = jnp.dot(normed[...], w_buf[:, cols], preferred_element_type=F32)
        squash = jax.nn.sigmoid(pre)
        act[:, cols] = (pre * squash).astype(BF16)
        slope[:, cols] = (squash * (1.0 + pre * (1.0 - squash))).astype(BF16)

    for copy in first:
        copy.wait()
    pl.loop(0, HALF_IN // 256)(columns)
    for copy in second:
        copy.wait()
    pl.loop(HALF_IN // 256, F1 // 256)(columns)

    quarter, half = lane_group(QK_DIM), lane_group(V_DIM)

    @pl.loop(0, TOKENS // LEN)
    def _(m):
        rows = pl.ds(pl.multiple_of(m * LEN, LEN), LEN)
        mask = wm_ref[m]
        for h4 in range(4):
            q4 = act[rows, QCOL + LEN * h4 : QCOL + LEN * (h4 + 1)]
            k4 = act[rows, KCOL + LEN * h4 : KCOL + LEN * (h4 + 1)]
            for pair in range(2):
                tile = 2 * h4 + pair
                v2 = act[rows, HV + LEN * tile : HV + LEN * (tile + 1)]
                total = jnp.zeros((LEN, LEN), F32)
                for e in range(2):
                    h = 2 * tile + e
                    score = mm(keep(quarter == 2 * pair + e, q4), k4, NT) * SCALE
                    squash = jax.nn.sigmoid(score)
                    weight = (score * squash * mask).astype(BF16)
                    attn[m, h] = weight
                    turn[m, h] = (
                        squash * (1.0 + score * (1.0 - squash)) * mask * SCALE
                    ).astype(BF16)
                    total += jnp.dot(weight, keep(half == e, v2), preferred_element_type=F32)
                mixed[:, LEN * tile : LEN * (tile + 1)] = total
        values = mixed[...]
        center = values - jnp.mean(values, axis=-1, keepdims=True)
        rstd = lax.rsqrt(jnp.mean(center * center, axis=-1, keepdims=True) + EPSILON)
        hat = center * rstd
        xhat[rows, :] = hat
        rstd_mid[rows, :] = jnp.broadcast_to(rstd, (LEN, LEN))
        gated[rows, :] = (hat * act[rows, :HV].astype(F32)).astype(BF16)


def front(place, inputs, masks, pieces_a, pieces_b):
    shapes = [
        ((TOKENS, D), BF16),
        ((TOKENS, F1), BF16),
        ((TOKENS, F1), BF16),
        ((2, HEADS, LEN, LEN), BF16),
        ((2, HEADS, LEN, LEN), BF16),
        ((TOKENS, HV), F32),
        ((TOKENS, HV), BF16),
        ((TOKENS, LEN), F32),
        ((TOKENS, LEN), F32),
        ((D, F1), BF16),
    ]
    return pl.pallas_call(
        front_kernel,
        out_shape=[jax.ShapeDtypeStruct(*s) for s in shapes],
        in_specs=[smem_spec(), vmem_spec(), vmem_spec()] + [any_spec()] * 10,
        out_specs=[vmem_spec()] * 10,
        scratch_shapes=[pltpu.VMEM((LEN, HV), F32), pltpu.SemaphoreType.DMA((32,))],
        compiler_params=pltpu.CompilerParams(vmem_limit_bytes=VMEM_LIMIT),
        cost_estimate=pl.CostEstimate(
            flops=2 * TOKENS * D * F1, bytes_accessed=40_000_000, transcendentals=1_500_000
        ),
        name="front",
    )(place, inputs, masks, *pieces_a, *pieces_b)


def arrange_kernel(place, *refs):
    full, sems = refs[10], refs[11]
    y, z = place[0], place[1]
    copies = []
    for half in range(2):
        for block, i, o in piece_blocks(refs[5 * half : 5 * half + 5]):
            j, k = (i, o) if half == 0 else (o, i)
            row = block_row(y, z, -j, -k, V_DIM)
            for fold in range(2):
                spot = full.at[pl.ds(row, V_DIM), pl.ds(HALF_OUT * half + FOLD * fold, FOLD)]
                copies.append(
                    pltpu.make_async_copy(
                        block.at[pl.ds(V_DIM * fold, V_DIM), :], spot, sems.at[len(copies)]
                    )
                )
    for copy in copies:
        copy.start()
    for copy in copies:
        copy.wait()


def arrange(place, pieces_a, pieces_b):
    return pl.pallas_call(
        arrange_kernel,
        out_shape=jax.ShapeDtypeStruct((HV, D), BF16),
        in_specs=[smem_spec()] + [any_spec()] * 10,
        out_specs=vmem_spec(),
        scratch_shapes=[pltpu.SemaphoreType.DMA((64,))],
        compiler_params=pltpu.CompilerParams(vmem_limit_bytes=VMEM_LIMIT),
        cost_estimate=pl.CostEstimate(flops=0, bytes_accessed=8_400_000, transcendentals=0),
        name="arrange",
    )(place, *pieces_a, *pieces_b)


def chain_body(n_sources, n_carried, info, *refs):
    sources, refs = refs[:n_sources], refs[n_sources:]
    w_in, w_out, normed, slope, act, attn, turn, xhat, rstd_in, rstd_mid = refs[:10]
    outgoing, ups_out, gp_out, grads_out, ups, gp, big, sems = refs[10 + n_carried :]
    slot, source = info[0], info[1]
    rows = pl.ds(pl.multiple_of(slot * LEN, LEN), LEN)
    for i, ref in enumerate(sources):
        @pl.when(source == i)
        def _():
            ups[...] = ref[rows, :] if i == 0 else ref[...]

    put_ups = pltpu.make_async_copy(ups, ups_out.at[rows, :], sems.at[0])
    put_ups.start()

    for c in range(HV // 256):
        big[:, 256 * c : 256 * (c + 1)] = mm(ups[...], w_out[256 * c : 256 * (c + 1), :], NT)
    sums = [jnp.zeros((LEN, LEN), F32)] * 2
    for c in range(HV // LEN):
        cols = slice(LEN * c, LEN * (c + 1))
        hat = xhat[rows, cols]
        moved = big[:, cols] * act[rows, cols].astype(F32)
        sums = [sums[0] + moved, sums[1] + moved * hat]
        gp[:, cols] = (
            (big[:, cols] * hat).astype(BF16).astype(F32) * slope[rows, cols].astype(F32)
        ).astype(BF16)
        big[:, HV + LEN * c : HV + LEN * (c + 1)] = moved
    mean_one = jnp.sum(sums[0], axis=-1, keepdims=True) / HV
    mean_hat = jnp.sum(sums[1], axis=-1, keepdims=True) / HV
    rstd = rstd_mid[rows, :]

    quarter, half = lane_group(QK_DIM), lane_group(V_DIM)

    def put(value, col):
        cols = slice(col, col + LEN)
        gp[:, cols] = (
            value.astype(BF16).astype(F32) * slope[rows, cols].astype(F32)
        ).astype(BF16)

    for h4 in range(4):
        q4 = act[rows, QCOL + LEN * h4 : QCOL + LEN * (h4 + 1)]
        k4 = act[rows, KCOL + LEN * h4 : KCOL + LEN * (h4 + 1)]
        grad_q = jnp.zeros((LEN, LEN), F32)
        grad_k = jnp.zeros((LEN, LEN), F32)
        for pair in range(2):
            tile = 2 * h4 + pair
            v2 = act[rows, HV + LEN * tile : HV + LEN * (tile + 1)]
            moved = big[:, HV + LEN * tile : HV + LEN * (tile + 1)]
            hat = xhat[rows, LEN * tile : LEN * (tile + 1)]
            g2 = (rstd * (moved - mean_one - hat * mean_hat)).astype(BF16)
            grad_v = jnp.zeros((LEN, LEN), F32)
            for e in range(2):
                h = 2 * tile + e
                gh = keep(half == e, g2)
                grad_s = (mm(gh, v2, NT) * turn[slot, h].astype(F32)).astype(BF16)
                grad_v += mm(attn[slot, h], gh, TN)
                own = quarter == 2 * pair + e
                grad_q += jnp.dot(grad_s, keep(own, k4), preferred_element_type=F32)
                grad_k += mm(grad_s, keep(own, q4), TN)
            put(grad_v, HV + LEN * tile)
        put(grad_q, QCOL + LEN * h4)
        put(grad_k, KCOL + LEN * h4)

    put_gp = pltpu.make_async_copy(gp, gp_out.at[rows, :], sems.at[1])
    put_gp.start()
    sums = [jnp.zeros((LEN, LEN), F32)] * 2
    for c in range(D // 256):
        big[:, 256 * c : 256 * (c + 1)] = mm(gp[...], w_in[256 * c : 256 * (c + 1), :], NT)
        for cols in (slice(256 * c, 256 * c + LEN), slice(256 * c + LEN, 256 * (c + 1))):
            grad = big[:, cols]
            sums = [sums[0] + grad, sums[1] + grad * normed[rows, cols].astype(F32)]
    one = jnp.sum(sums[0], axis=-1, keepdims=True) / D
    two = jnp.sum(sums[1], axis=-1, keepdims=True) / D
    rstd = rstd_in[rows, :]
    for c in range(D // LEN):
        cols = slice(LEN * c, LEN * (c + 1))
        moved = rstd * (big[:, cols] - one - normed[rows, cols].astype(F32) * two)
        outgoing[:, cols] = (ups[:, cols].astype(F32) + moved).astype(BF16)
    put_grads = pltpu.make_async_copy(outgoing, grads_out.at[rows, :], sems.at[2])
    put_grads.start()
    put_ups.wait()
    put_gp.wait()
    put_grads.wait()


def chain_step(info, sources, w_in, w_out, saved, carried):
    kept = [((TOKENS, D), BF16), ((TOKENS, F1), BF16), ((TOKENS, D), BF16)]
    shapes = [((LEN, D), BF16)] + kept
    operands = [info, *sources, w_in, w_out, *saved, *carried]
    before = len(operands) - len(carried)
    aliases = {before + i: 1 + i for i in range(len(carried))}

    def kernel(info, *refs):
        @pl.when(info[2] == 1)
        def _():
            chain_body(len(sources), len(carried), info, *refs)

    return pl.pallas_call(
        kernel,
        out_shape=[jax.ShapeDtypeStruct(*s) for s in shapes],
        in_specs=[smem_spec()] + [vmem_spec()] * (before - 1) + [any_spec()] * len(carried),
        out_specs=[vmem_spec()] + [any_spec()] * 3,
        input_output_aliases=aliases,
        scratch_shapes=[
            pltpu.VMEM((LEN, D), BF16),
            pltpu.VMEM((LEN, F1), BF16),
            pltpu.VMEM((LEN, D), F32),
            pltpu.SemaphoreType.DMA((3,)),
        ],
        compiler_params=pltpu.CompilerParams(vmem_limit_bytes=VMEM_LIMIT),
        cost_estimate=pl.CostEstimate(
            flops=2 * LEN * D * (F1 + HV), bytes_accessed=22_000_000, transcendentals=0
        ),
        name="chain",
    )(*operands)


def weights_kernel(jobs, place, normed_t, gated_t, ups, gp, *refs):
    outs, (rows_in, rows_out, buf, sems) = refs[: len(jobs)], refs[len(jobs) :]
    y, z = place[0], place[1]
    pending = [None, None]
    for count, (out, (half, blocks)) in enumerate(zip(outs, jobs)):
        turn, size = count % 2, len(blocks)
        for at, (dy, dz) in enumerate(blocks):
            row = block_row(y, z, dy, dz, LEN)
            rows_in[LEN * at : LEN * (at + 1), :] = normed_t[pl.ds(row, LEN), :]
            row = block_row(y, z, dy, dz, V_DIM)
            rows_out[V_DIM * at : V_DIM * (at + 1), :] = gated_t[pl.ds(row, V_DIM), :]
        if pending[turn] is not None:
            pending[turn].wait()
        for c in range(HALF_IN // 512):
            right = gp[:, HALF_IN * half + 512 * c : HALF_IN * half + 512 * (c + 1)]
            found = jnp.dot(rows_in[: LEN * size, :], right, preferred_element_type=F32)
            for at in range(size):
                buf[turn, at, :, 512 * c : 512 * (c + 1)] = found[
                    LEN * at : LEN * (at + 1), :
                ].astype(BF16)
        for fold in range(2):
            right = ups[:, HALF_OUT * half + FOLD * fold : HALF_OUT * half + FOLD * (fold + 1)]
            found = jnp.dot(rows_out[: V_DIM * size, :], right, preferred_element_type=F32)
            for at in range(size):
                buf[turn, at, V_DIM * fold : V_DIM * (fold + 1), HALF_IN:] = found[
                    V_DIM * at : V_DIM * (at + 1), :
                ].astype(BF16)
        pending[turn] = pltpu.make_async_copy(buf.at[turn, pl.ds(0, size)], out, sems.at[turn])
        pending[turn].start()
    for copy in pending:
        copy.wait()


def weight_parts(name, jobs, place, normed_t, gated_t, ups, gp):
    blocks = sum(len(job[1]) for job in jobs)
    return pl.pallas_call(
        lambda *refs: weights_kernel(jobs, *refs),
        out_shape=[jax.ShapeDtypeStruct((len(job[1]), LEN, PACK), BF16) for job in jobs],
        in_specs=[smem_spec()] + [vmem_spec()] * 4,
        out_specs=[any_spec()] * len(jobs),
        scratch_shapes=[
            pltpu.VMEM((SIDE * LEN, TOKENS), BF16),
            pltpu.VMEM((SIDE * V_DIM, TOKENS), BF16),
            pltpu.VMEM((2, SIDE, LEN, PACK), BF16),
            pltpu.SemaphoreType.DMA((2,)),
        ],
        compiler_params=pltpu.CompilerParams(vmem_limit_bytes=VMEM_LIMIT),
        cost_estimate=pl.CostEstimate(
            flops=2 * TOKENS * LEN * PACK * blocks,
            bytes_accessed=4_000_000 + 2 * LEN * PACK * blocks,
            transcendentals=0,
        ),
        name=name,
    )(place, normed_t, gated_t, ups, gp)


FAR_JOBS = (
    (0, ((0, 2), (1, 2))),
    (0, ((2, 2), (3, 2))),
    (1, ((2, 0), (2, 1))),
    (1, ((2, 2), (2, 3))),
)
NEAR_JOBS = (
    (0, ((0, 1), (1, 1))),
    (0, ((2, 1), (3, 1))),
    (0, ((0, 3), (1, 3))),
    (0, ((2, 3), (3, 3))),
    (1, ((1, 0), (1, 1))),
    (1, ((1, 2), (1, 3))),
    (1, ((3, 0), (3, 1))),
    (1, ((3, 2), (3, 3))),
    (0, ((0, 0), (1, 0), (2, 0), (3, 0))),
    (1, ((0, 0), (0, 1), (0, 2), (0, 3))),
)


def along(axis, by):
    return (by, 0, 0) if axis == "y" else (0, by, 0)


def spread(block, axis):
    half = block.shape[0] // 2
    plus = send(block, *along(axis, 1))
    minus = send(block, *along(axis, -1))
    far_low = send(plus[:half], *along(axis, 1))
    far_high = send(minus[half:], *along(axis, -1))
    return plus, minus, far_low, far_high


def spread_at_once(block, axis):
    plus, far, minus = [send(block, *along(axis, by)) for by in (1, 2, -1)]
    return plus, minus, far, far


def lined(block, axis):
    plus, minus, far_low, far_high = spread(block, axis)
    return jnp.stack([block, plus, jnp.concatenate([far_low, far_high], 0), minus])


def gathered(first, second, x):
    packed = jnp.concatenate([first, jnp.concatenate([second[:, :HALF_OUT], second[:, HALF_OUT:]], 0)], 1)
    other = send(packed, 0, 0, 1)
    low = jnp.where(x == 0, packed, other)
    high = jnp.where(x == 0, other, packed)
    rows = second.shape[0]
    lines = []
    for half in range(2):
        cols = slice(HALF_IN * half, HALF_IN * (half + 1))
        part = slice(rows * half, rows * (half + 1))
        out = jnp.concatenate([low[part, F1:], high[part, F1:]], 0)
        block = jnp.concatenate(
            [
                jnp.concatenate([low[:, cols], high[:, cols]], 0),
                jnp.concatenate([out[:, :FOLD], out[:, FOLD:]], 0),
            ],
            1,
        )
        lines.append(lined(block, "yz"[half]))
    pieces = []
    late = jnp.zeros((), BF16)
    for cols in (slice(0, HALF_IN), slice(HALF_IN, PACK)):
        for half in range(2):
            line = lines[half][:, :, cols] + late
            move = spread if cols.start == 0 else spread_at_once
            pieces.append((line, *move(line, "zy"[half])))
        if cols.start == 0:
            late = sum(jnp.minimum(jnp.abs(p[i][0, 0, 0]), 0.0) for p in pieces for i in (3, 4))
    return pieces


def added(*arrays):
    total = arrays[0].astype(F32)
    for array in arrays[1:]:
        total = total + array.astype(F32)
    return total


def joined(own, plus_low, plus_high, minus_low, minus_high, far_low, far_high, axis):
    through = send(far_low, *along(axis, 1))
    back = send(far_high, *along(axis, -1))
    plus = jnp.concatenate([added(plus_low, through).astype(BF16), plus_high], 0)
    minus = jnp.concatenate([minus_low, added(minus_high, back).astype(BF16)], 0)
    return added(own, send(plus, *along(axis, 1)), send(minus, *along(axis, -1)))


def scattered(far, near, x):
    a_one = joined(near[8], *near[0:4], far[0], far[1], "z").astype(BF16)
    b_one = joined(near[9], *near[4:8], far[2], far[3], "y").astype(BF16)
    ends = []
    for line, axis in ((a_one, "y"), (b_one, "z")):
        cut = [part for block in (1, 3, 2) for part in (line[block, :V_DIM], line[block, V_DIM:])]
        ends.append(joined(line[0], *cut, axis))
    first = jnp.concatenate([end[:, :HALF_IN] for end in ends], 1)
    folded = jnp.concatenate([end[:, HALF_IN:] for end in ends], 1)
    outs = [folded[:V_DIM, :FOLD], folded[V_DIM:, :FOLD], folded[:V_DIM, FOLD:], folded[V_DIM:, FOLD:]]
    second = jnp.concatenate(outs, 1)
    sides = []
    for side in range(2):
        mine = second[32 * side : 32 * (side + 1)]
        tall = jnp.concatenate([mine[:, :HALF_OUT], mine[:, HALF_OUT:]], 0)
        sides.append(jnp.concatenate([first[64 * side : 64 * (side + 1)], tall], 1))
    away = jnp.where(x == 0, sides[1], sides[0]).astype(BF16)
    total = jnp.where(x == 0, sides[0], sides[1]) + send(away, 0, 0, 1).astype(F32)
    grad_out = jnp.concatenate([total[:32, F1:], total[32:, F1:]], 1)
    return total[:, :F1], grad_out


def body(section_input, top_grad, w_in, w_out, segments):
    section = lax.axis_index("pipe")
    spot = lax.axis_index("dp")
    y, z, x = spot // 8, (spot // 2) % 4, spot % 2
    place = jnp.stack([y, z]).astype(jnp.int32)
    in_a, in_b, out_a, out_b = gathered(w_in[0], w_out[0], x)

    same = segments[:, :, None] == segments[:, None, :]
    lower = lax.broadcasted_iota(jnp.int32, (LEN, LEN), 1) <= lax.broadcasted_iota(
        jnp.int32, (LEN, LEN), 0
    )
    counts = jnp.sum(same.astype(F32), axis=2, keepdims=True)
    masks = jnp.where(jnp.logical_and(same, lower[None]), 1.0 / counts, 0.0)

    normed, slope, act, attn, turn, xhat, gated, rstd_in, rstd_mid, w_first = front(
        place, section_input[0], masks, in_a, in_b
    )
    after = (rstd_in[0, 0] < 0.0).astype(jnp.int32)
    w_second = arrange(place + after, out_a, out_b)
    saved = (normed, slope, act, attn, turn, xhat, rstd_in, rstd_mid)

    def step(slots, sources, carried):
        slot, source, busy = jnp.int32(0), jnp.int32(0), jnp.int32(0)
        for which, (own, origin) in slots.items():
            slot = jnp.where(section == which, own, slot)
            source = jnp.where(section == which, origin, source)
            busy = jnp.where(section == which, 1, busy)
        info = jnp.stack([slot, source, busy]).astype(jnp.int32)
        outgoing, *carried = chain_step(
            info, (top_grad, *sources), w_first, w_second, saved, tuple(carried)
        )
        return outgoing, carried

    def below(array, which):
        return lax.ppermute(array, "pipe", [(which, which - 1)])

    out_0, carried = step({3: (0, 0)}, (), ())
    out_1, carried = step({3: (1, 0), 2: (0, 1)}, (below(out_0, 3),), carried)
    to_one = below(out_1, 2)
    out_2, carried = step({2: (1, 1)}, (below(out_1, 3),), carried)
    again = below(out_2, 2)
    out_3, carried = step({1: (0, 1)}, (to_one,), carried)
    out_4, carried = step({1: (1, 1), 0: (0, 2)}, (again, below(out_3, 1)), carried)
    _, carried = step({0: (1, 1)}, (below(out_4, 1),), carried)
    ups, gp, grads = carried

    normed_t, gated_t = normed.T, gated.T
    far = weight_parts("far_parts", FAR_JOBS, place, normed_t, gated_t, ups, gp)
    near = weight_parts("near_parts", NEAR_JOBS, place, normed_t, gated_t, ups, gp)
    grad_first, grad_out = scattered(far, near, x)
    return (grads[None], grad_first[None], grad_out[None])


def solution(mesh):
    return jax.shard_map(
        body,
        mesh=mesh,
        in_specs=(
            P("pipe", "dp", None),
            P("dp", None),
            P("pipe", "dp", None),
            P("pipe", "dp", None),
            P("dp", None),
        ),
        out_specs=(P("pipe", "dp", None), P("pipe", "dp", None), P("pipe", "dp", None)),
        check_vma=False,
    )
```

```python
import jax
import jax.numpy as jnp
from jax import lax
from jax.experimental import pallas as pl
from jax.experimental.pallas import tpu as pltpu
from jax.sharding import PartitionSpec as P

HEADS = 16
QK_DIM = 32
V_DIM = 64
EPSILON = 1e-05
D = 2048
HV = 1024
F1 = 3072
QCOL = 2 * HV
KCOL = QCOL + HEADS * QK_DIM
LEN = 128
TOKENS = 256
SIDE = 4
HALF_IN = F1 // 2
HALF_OUT = D // 2
FOLD = HALF_OUT // 2
PACK = HALF_IN + FOLD
SCALE = QK_DIM ** (-0.5)
VMEM_LIMIT = 9 * 1024 * 1024
BF16 = jnp.bfloat16
F32 = jnp.float32

NT = (((1,), (1,)), ((), ()))
TN = (((0,), (0,)), ((), ()))


def mm(left, right, dims):
    return lax.dot_general(left, right, dims, preferred_element_type=F32)


def shifted(dy, dz, dx):
    pairs = []
    for i in range(32):
        y, z, x = i // 8, (i // 2) % 4, i % 2
        pairs.append((i, ((y + dy) % 4 * 4 + (z + dz) % 4) * 2 + (x + dx) % 2))
    return pairs


def send(array, dy, dz, dx):
    return lax.ppermute(array, "dp", shifted(dy, dz, dx))


def any_spec():
    return pl.BlockSpec(memory_space=pl.ANY)


def vmem_spec():
    return pl.BlockSpec(memory_space=pltpu.VMEM)


def block_row(y, z, dy, dz, rows):
    cell = lax.rem(y + dy + SIDE, SIDE) * SIDE + lax.rem(z + dz + SIDE, SIDE)
    return pl.multiple_of(cell * rows, rows)


def here():
    spot = lax.axis_index("dp")
    return lax.shift_right_logical(spot, 3), lax.bitwise_and(lax.shift_right_logical(spot, 1), 3)


def lane_group(width):
    return lax.broadcasted_iota(jnp.int32, (LEN, LEN), 1) // width


def keep(mask, tile):
    return jnp.where(mask, tile, jnp.zeros_like(tile))


def piece_blocks(pieces):
    own, plus, minus, far_low, far_high = pieces
    found = []
    for j in range(SIDE):
        found.append((own.at[j], j, 0))
        found.append((plus.at[j], j, 1))
        found.append((minus.at[j], j, 3))
        found.append(((far_low if j < 2 else far_high).at[j % far_low.shape[0]], j, 2))
    return found


def front_kernel(x_ref, wm_ref, *refs):
    normed, slope, act, attn, turn, xhat, gated, rstd_in, rstd_mid, w_in, w_out = refs[10:21]
    mixed, sems = refs[21:23]
    y, z = here()
    halves, last = [[], []], []
    for half in range(2):
        for n, (block, i, o) in enumerate(piece_blocks(refs[5 * half : 5 * half + 5])):
            j, k = (i, o) if half == 0 else (o, i)
            row = block_row(y, z, -j, -k, LEN)
            spot = w_in.at[pl.ds(row, LEN), pl.ds(HALF_IN * half, HALF_IN)]
            halves[half].append(
                pltpu.make_async_copy(block.at[:, pl.ds(0, HALF_IN)], spot, sems.at[half, n])
            )
            row = block_row(y, z, -j, -k, V_DIM)
            for fold in range(2):
                spot = w_out.at[pl.ds(row, V_DIM), pl.ds(HALF_OUT * half + FOLD * fold, FOLD)]
                part = block.at[pl.ds(V_DIM * fold, V_DIM), pl.ds(HALF_IN, FOLD)]
                last.append(pltpu.make_async_copy(part, spot, sems.at[2 + 2 * half + fold, n]))
    first, second = halves
    for copy in first + second:
        copy.start()

    @pl.loop(0, TOKENS // 32)
    def _(step):
        rows = pl.ds(pl.multiple_of(step * 32, 32), 32)
        values = x_ref[rows, :].astype(F32)
        center = values - jnp.mean(values, axis=-1, keepdims=True)
        rstd = lax.rsqrt(jnp.mean(center * center, axis=-1, keepdims=True) + EPSILON)
        normed[rows, :] = (center * rstd).astype(BF16)
        rstd_in[rows, :] = jnp.broadcast_to(rstd, (32, LEN))

    def columns(step):
        cols = pl.ds(pl.multiple_of(step * 256, 256), 256)
        pre = jnp.dot(normed[...], w_in[:, cols], preferred_element_type=F32)
        squash = jax.nn.sigmoid(pre)
        act[:, cols] = (pre * squash).astype(BF16)
        slope[:, cols] = (squash * (1.0 + pre * (1.0 - squash))).astype(BF16)

    for copy in last:
        copy.start()
    for copy in first:
        copy.wait()
    pl.loop(0, HALF_IN // 256)(columns)
    for copy in second:
        copy.wait()
    pl.loop(HALF_IN // 256, F1 // 256)(columns)

    quarter, half = lane_group(QK_DIM), lane_group(V_DIM)

    @pl.loop(0, TOKENS // LEN)
    def _(m):
        rows = pl.ds(pl.multiple_of(m * LEN, LEN), LEN)
        mask = wm_ref[m]
        for h4 in range(4):
            q4 = act[rows, QCOL + LEN * h4 : QCOL + LEN * (h4 + 1)]
            k4 = act[rows, KCOL + LEN * h4 : KCOL + LEN * (h4 + 1)]
            for pair in range(2):
                tile = 2 * h4 + pair
                v2 = act[rows, HV + LEN * tile : HV + LEN * (tile + 1)]
                total = jnp.zeros((LEN, LEN), F32)
                for e in range(2):
                    h = 2 * tile + e
                    score = mm(keep(quarter == 2 * pair + e, q4), k4, NT) * SCALE
                    squash = jax.nn.sigmoid(score)
                    weight = (score * squash * mask).astype(BF16)
                    attn[m, h] = weight
                    turn[m, h] = (
                        squash * (1.0 + score * (1.0 - squash)) * mask * SCALE
                    ).astype(BF16)
                    total += jnp.dot(weight, keep(half == e, v2), preferred_element_type=F32)
                mixed[:, LEN * tile : LEN * (tile + 1)] = total
        values = mixed[...]
        center = values - jnp.mean(values, axis=-1, keepdims=True)
        rstd = lax.rsqrt(jnp.mean(center * center, axis=-1, keepdims=True) + EPSILON)
        hat = center * rstd
        xhat[rows, :] = hat
        rstd_mid[rows, :] = jnp.broadcast_to(rstd, (LEN, LEN))
        gated[rows, :] = (hat * act[rows, :HV].astype(F32)).astype(BF16)

    for copy in last:
        copy.wait()


def front(inputs, masks, pieces):
    shapes = [
        ((TOKENS, D), BF16),
        ((TOKENS, F1), BF16),
        ((TOKENS, F1), BF16),
        ((2, HEADS, LEN, LEN), BF16),
        ((2, HEADS, LEN, LEN), BF16),
        ((TOKENS, HV), F32),
        ((TOKENS, HV), BF16),
        ((TOKENS, LEN), F32),
        ((TOKENS, LEN), F32),
        ((D, F1), BF16),
        ((HV, D), BF16),
    ]
    return pl.pallas_call(
        front_kernel,
        out_shape=[jax.ShapeDtypeStruct(*s) for s in shapes],
        in_specs=[vmem_spec(), vmem_spec()] + [any_spec()] * 10,
        out_specs=[vmem_spec()] * 11,
        scratch_shapes=[pltpu.VMEM((LEN, HV), F32), pltpu.SemaphoreType.DMA((6, 16))],
        compiler_params=pltpu.CompilerParams(vmem_limit_bytes=VMEM_LIMIT),
        cost_estimate=pl.CostEstimate(
            flops=2 * TOKENS * D * F1, bytes_accessed=40_000_000, transcendentals=1_500_000
        ),
        name="front",
    )(inputs, masks, *pieces[0], *pieces[1])


def flip_kernel(normed, gated, normed_t, gated_t):
    for c in range(D // LEN):
        normed_t[LEN * c : LEN * (c + 1), :] = normed[:, LEN * c : LEN * (c + 1)].T
    for c in range(HV // LEN):
        gated_t[LEN * c : LEN * (c + 1), :] = gated[:, LEN * c : LEN * (c + 1)].T


def flip(normed, gated):
    return pl.pallas_call(
        flip_kernel,
        out_shape=[
            jax.ShapeDtypeStruct((D, TOKENS), BF16),
            jax.ShapeDtypeStruct((HV, TOKENS), BF16),
        ],
        in_specs=[vmem_spec()] * 2,
        out_specs=[vmem_spec()] * 2,
        compiler_params=pltpu.CompilerParams(vmem_limit_bytes=VMEM_LIMIT),
        cost_estimate=pl.CostEstimate(flops=0, bytes_accessed=6_000_000, transcendentals=0),
        name="flip",
    )(normed, gated)


def chain_body(n_sources, n_carried, slot, source, *refs):
    sources, refs = refs[:n_sources], refs[n_sources:]
    w_in, w_out, normed, slope, act, attn, turn, xhat, rstd_in, rstd_mid = refs[:10]
    outgoing, ups_out, gp_out, grads_out, ups, gp, big, sems = refs[10 + n_carried :]
    slot, source = jnp.int32(slot), jnp.int32(source)
    rows = pl.ds(pl.multiple_of(slot * LEN, LEN), LEN)
    for i, ref in enumerate(sources):

        @pl.when(source == i)
        def _():
            ups[...] = ref[rows, :] if i == 0 else ref[...]

    put_ups = pltpu.make_async_copy(ups, ups_out.at[rows, :], sems.at[0])
    put_ups.start()

    for c in range(HV // 256):
        big[:, 256 * c : 256 * (c + 1)] = mm(ups[...], w_out[256 * c : 256 * (c + 1), :], NT)
    sums = [jnp.zeros((LEN, LEN), F32)] * 2
    for c in range(HV // LEN):
        cols = slice(LEN * c, LEN * (c + 1))
        hat = xhat[rows, cols]
        moved = big[:, cols] * act[rows, cols].astype(F32)
        sums = [sums[0] + moved, sums[1] + moved * hat]
        gp[:, cols] = (
            (big[:, cols] * hat).astype(BF16).astype(F32) * slope[rows, cols].astype(F32)
        ).astype(BF16)
        big[:, HV + LEN * c : HV + LEN * (c + 1)] = moved
    mean_one = jnp.sum(sums[0], axis=-1, keepdims=True) / HV
    mean_hat = jnp.sum(sums[1], axis=-1, keepdims=True) / HV
    rstd = rstd_mid[rows, :]

    quarter, half = lane_group(QK_DIM), lane_group(V_DIM)

    def put(value, col):
        cols = slice(col, col + LEN)
        gp[:, cols] = (
            value.astype(BF16).astype(F32) * slope[rows, cols].astype(F32)
        ).astype(BF16)

    for h4 in range(4):
        q4 = act[rows, QCOL + LEN * h4 : QCOL + LEN * (h4 + 1)]
        k4 = act[rows, KCOL + LEN * h4 : KCOL + LEN * (h4 + 1)]
        grad_q = jnp.zeros((LEN, LEN), F32)
        grad_k = jnp.zeros((LEN, LEN), F32)
        for pair in range(2):
            tile = 2 * h4 + pair
            v2 = act[rows, HV + LEN * tile : HV + LEN * (tile + 1)]
            moved = big[:, HV + LEN * tile : HV + LEN * (tile + 1)]
            hat = xhat[rows, LEN * tile : LEN * (tile + 1)]
            g2 = (rstd * (moved - mean_one - hat * mean_hat)).astype(BF16)
            grad_v = jnp.zeros((LEN, LEN), F32)
            for e in range(2):
                h = 2 * tile + e
                gh = keep(half == e, g2)
                grad_s = (mm(gh, v2, NT) * turn[slot, h].astype(F32)).astype(BF16)
                grad_v += mm(attn[slot, h], gh, TN)
                own = quarter == 2 * pair + e
                grad_q += jnp.dot(grad_s, keep(own, k4), preferred_element_type=F32)
                grad_k += mm(grad_s, keep(own, q4), TN)
            put(grad_v, HV + LEN * tile)
        put(grad_q, QCOL + LEN * h4)
        put(grad_k, KCOL + LEN * h4)

    put_gp = pltpu.make_async_copy(gp, gp_out.at[rows, :], sems.at[1])
    put_gp.start()
    sums = [jnp.zeros((LEN, LEN), F32)] * 2
    for c in range(D // 256):
        big[:, 256 * c : 256 * (c + 1)] = mm(gp[...], w_in[256 * c : 256 * (c + 1), :], NT)
        for cols in (slice(256 * c, 256 * c + LEN), slice(256 * c + LEN, 256 * (c + 1))):
            grad = big[:, cols]
            sums = [sums[0] + grad, sums[1] + grad * normed[rows, cols].astype(F32)]
    one = jnp.sum(sums[0], axis=-1, keepdims=True) / D
    two = jnp.sum(sums[1], axis=-1, keepdims=True) / D
    rstd = rstd_in[rows, :]
    for c in range(D // LEN):
        cols = slice(LEN * c, LEN * (c + 1))
        moved = rstd * (big[:, cols] - one - normed[rows, cols].astype(F32) * two)
        outgoing[:, cols] = (ups[:, cols].astype(F32) + moved).astype(BF16)
    put_grads = pltpu.make_async_copy(outgoing, grads_out.at[rows, :], sems.at[2])
    put_grads.start()
    put_ups.wait()
    put_gp.wait()
    put_grads.wait()


def chain_step(work, sources, w_in, w_out, saved, carried):
    kept = [((TOKENS, D), BF16), ((TOKENS, F1), BF16), ((TOKENS, D), BF16)]
    shapes = [((LEN, D), BF16)] + kept
    operands = [*sources, w_in, w_out, *saved, *carried]
    before = len(operands) - len(carried)
    aliases = {before + i: 1 + i for i in range(len(carried))}

    def kernel(*refs):
        section = lax.axis_index("pipe")
        if len(work) == 1:
            ((one, mine),) = work.items()
            busy = section == one
        else:
            (one, (slot, source)), (two, (slot_two, source_two)) = work.items()
            busy = jnp.logical_or(section == one, section == two)
            mine = (
                jnp.where(section == one, slot, slot_two),
                jnp.where(section == one, source, source_two),
            )

        @pl.when(busy)
        def _():
            chain_body(len(sources), len(carried), *mine, *refs)

    return pl.pallas_call(
        kernel,
        out_shape=[jax.ShapeDtypeStruct(*s) for s in shapes],
        in_specs=[vmem_spec()] * before + [any_spec()] * len(carried),
        out_specs=[vmem_spec()] + [any_spec()] * 3,
        input_output_aliases=aliases,
        scratch_shapes=[
            pltpu.VMEM((LEN, D), BF16),
            pltpu.VMEM((LEN, F1), BF16),
            pltpu.VMEM((LEN, D), F32),
            pltpu.SemaphoreType.DMA((3,)),
        ],
        compiler_params=pltpu.CompilerParams(vmem_limit_bytes=VMEM_LIMIT),
        cost_estimate=pl.CostEstimate(
            flops=2 * LEN * D * (F1 + HV), bytes_accessed=22_000_000, transcendentals=0
        ),
        name="chain",
    )(*operands)


def weights_kernel(jobs, normed_t, gated_t, ups, gp, *refs):
    outs, (rows_in, rows_out, buf, sems) = refs[: len(jobs)], refs[len(jobs) :]
    y, z = here()
    pending = [None, None]
    for count, (out, (half, blocks)) in enumerate(zip(outs, jobs)):
        turn, size = count % 2, len(blocks)
        for at, (dy, dz) in enumerate(blocks):
            row = block_row(y, z, dy, dz, LEN)
            rows_in[LEN * at : LEN * (at + 1), :] = normed_t[pl.ds(row, LEN), :]
            row = block_row(y, z, dy, dz, V_DIM)
            rows_out[V_DIM * at : V_DIM * (at + 1), :] = gated_t[pl.ds(row, V_DIM), :]
        if pending[turn] is not None:
            pending[turn].wait()
        for c in range(HALF_IN // 512):
            right = gp[:, HALF_IN * half + 512 * c : HALF_IN * half + 512 * (c + 1)]
            found = jnp.dot(rows_in[: LEN * size, :], right, preferred_element_type=F32)
            for at in range(size):
                buf[turn, at, :, 512 * c : 512 * (c + 1)] = found[
                    LEN * at : LEN * (at + 1), :
                ].astype(BF16)
        for fold in range(2):
            right = ups[:, HALF_OUT * half + FOLD * fold : HALF_OUT * half + FOLD * (fold + 1)]
            found = jnp.dot(rows_out[: V_DIM * size, :], right, preferred_element_type=F32)
            for at in range(size):
                buf[turn, at, V_DIM * fold : V_DIM * (fold + 1), HALF_IN:] = found[
                    V_DIM * at : V_DIM * (at + 1), :
                ].astype(BF16)
        pending[turn] = pltpu.make_async_copy(buf.at[turn, pl.ds(0, size)], out, sems.at[turn])
        pending[turn].start()
    for copy in pending:
        copy.wait()


def weight_parts(name, jobs, normed_t, gated_t, ups, gp):
    blocks = sum(len(job[1]) for job in jobs)
    return pl.pallas_call(
        lambda *refs: weights_kernel(jobs, *refs),
        out_shape=[jax.ShapeDtypeStruct((len(job[1]), LEN, PACK), BF16) for job in jobs],
        in_specs=[vmem_spec()] * 4,
        out_specs=[any_spec()] * len(jobs),
        scratch_shapes=[
            pltpu.VMEM((SIDE * LEN, TOKENS), BF16),
            pltpu.VMEM((SIDE * V_DIM, TOKENS), BF16),
            pltpu.VMEM((2, SIDE, LEN, PACK), BF16),
            pltpu.SemaphoreType.DMA((2,)),
        ],
        compiler_params=pltpu.CompilerParams(vmem_limit_bytes=VMEM_LIMIT),
        cost_estimate=pl.CostEstimate(
            flops=2 * TOKENS * LEN * PACK * blocks,
            bytes_accessed=4_000_000 + 2 * LEN * PACK * blocks,
            transcendentals=0,
        ),
        name=name,
    )(normed_t, gated_t, ups, gp)


FAR_JOBS = (
    (0, ((0, 2), (1, 2))),
    (0, ((2, 2), (3, 2))),
    (1, ((2, 0), (2, 1))),
    (1, ((2, 2), (2, 3))),
)
NEAR_JOBS = (
    (0, ((0, 1), (1, 1))),
    (0, ((2, 1), (3, 1))),
    (0, ((0, 3), (1, 3))),
    (0, ((2, 3), (3, 3))),
    (1, ((1, 0), (1, 1))),
    (1, ((1, 2), (1, 3))),
    (1, ((3, 0), (3, 1))),
    (1, ((3, 2), (3, 3))),
    (0, ((0, 0), (1, 0), (2, 0), (3, 0))),
    (1, ((0, 0), (0, 1), (0, 2), (0, 3))),
)


def along(axis, by):
    return (by, 0, 0) if axis == "y" else (0, by, 0)


def spread(block, axis):
    half = block.shape[0] // 2
    plus = send(block, *along(axis, 1))
    minus = send(block, *along(axis, -1))
    far_low = send(plus[:half], *along(axis, 1))
    far_high = send(minus[half:], *along(axis, -1))
    return plus, minus, far_low, far_high


def lined(block, axis):
    plus, minus, far_low, far_high = spread(block, axis)
    return jnp.stack([block, plus, jnp.concatenate([far_low, far_high], 0), minus])


def gathered(first, second, x):
    packed = jnp.concatenate([first, jnp.concatenate([second[:, :HALF_OUT], second[:, HALF_OUT:]], 0)], 1)
    other = send(packed, 0, 0, 1)
    low = jnp.where(x == 0, packed, other)
    high = jnp.where(x == 0, other, packed)
    rows = second.shape[0]
    lines = []
    for half in range(2):
        cols = slice(HALF_IN * half, HALF_IN * (half + 1))
        part = slice(rows * half, rows * (half + 1))
        out = jnp.concatenate([low[part, F1:], high[part, F1:]], 0)
        block = jnp.concatenate(
            [
                jnp.concatenate([low[:, cols], high[:, cols]], 0),
                jnp.concatenate([out[:, :FOLD], out[:, FOLD:]], 0),
            ],
            1,
        )
        lines.append(lined(block, "yz"[half]))
    return [(line, *spread(line, "zy"[half])) for half, line in enumerate(lines)]


def added(*arrays):
    total = arrays[0].astype(F32)
    for array in arrays[1:]:
        total = total + array.astype(F32)
    return total


def joined(own, plus_low, plus_high, minus_low, minus_high, far_low, far_high, axis):
    through = send(far_low, *along(axis, 1))
    back = send(far_high, *along(axis, -1))
    plus = jnp.concatenate([added(plus_low, through).astype(BF16), plus_high], 0)
    minus = jnp.concatenate([minus_low, added(minus_high, back).astype(BF16)], 0)
    return added(own, send(plus, *along(axis, 1)), send(minus, *along(axis, -1)))


def scattered(far, near, x):
    a_one = joined(near[8], *near[0:4], far[0], far[1], "z").astype(BF16)
    b_one = joined(near[9], *near[4:8], far[2], far[3], "y").astype(BF16)
    ends = []
    for line, axis in ((a_one, "y"), (b_one, "z")):
        cut = [part for block in (1, 3, 2) for part in (line[block, :V_DIM], line[block, V_DIM:])]
        ends.append(joined(line[0], *cut, axis))
    first = jnp.concatenate([end[:, :HALF_IN] for end in ends], 1)
    folded = jnp.concatenate([end[:, HALF_IN:] for end in ends], 1)
    outs = [folded[:V_DIM, :FOLD], folded[V_DIM:, :FOLD], folded[:V_DIM, FOLD:], folded[V_DIM:, FOLD:]]
    second = jnp.concatenate(outs, 1)
    sides = []
    for side in range(2):
        mine = second[32 * side : 32 * (side + 1)]
        tall = jnp.concatenate([mine[:, :HALF_OUT], mine[:, HALF_OUT:]], 0)
        sides.append(jnp.concatenate([first[64 * side : 64 * (side + 1)], tall], 1))
    away = jnp.where(x == 0, sides[1], sides[0]).astype(BF16)
    total = jnp.where(x == 0, sides[0], sides[1]) + send(away, 0, 0, 1).astype(F32)
    grad_out = jnp.concatenate([total[:32, F1:], total[32:, F1:]], 1)
    return total[:, :F1], grad_out


def body(section_input, top_grad, w_in, w_out, segments):
    x = lax.axis_index("dp") % 2
    pieces = gathered(w_in[0], w_out[0], x)

    same = segments[:, :, None] == segments[:, None, :]
    lower = lax.broadcasted_iota(jnp.int32, (LEN, LEN), 1) <= lax.broadcasted_iota(
        jnp.int32, (LEN, LEN), 0
    )
    counts = jnp.sum(same.astype(F32), axis=2, keepdims=True)
    masks = jnp.where(jnp.logical_and(same, lower[None]), 1.0 / counts, 0.0)

    normed, slope, act, attn, turn, xhat, gated, rstd_in, rstd_mid, w_first, w_second = front(
        section_input[0], masks, pieces
    )
    saved = (normed, slope, act, attn, turn, xhat, rstd_in, rstd_mid)

    def step(work, sources, carried):
        outgoing, *carried = chain_step(
            work, (top_grad, *sources), w_first, w_second, saved, tuple(carried)
        )
        return outgoing, carried

    def below(array, which):
        return lax.ppermute(array, "pipe", [(which, which - 1)])

    out_0, carried = step({3: (0, 0)}, (), ())
    out_1, carried = step({3: (1, 0), 2: (0, 1)}, (below(out_0, 3),), carried)
    to_one = below(out_1, 2)
    out_2, carried = step({2: (1, 1)}, (below(out_1, 3),), carried)
    again = below(out_2, 2)
    out_3, carried = step({1: (0, 1)}, (to_one,), carried)
    out_4, carried = step({1: (1, 1), 0: (0, 2)}, (again, below(out_3, 1)), carried)
    _, carried = step({0: (1, 1)}, (below(out_4, 1),), carried)
    ups, gp, grads = carried

    normed_t, gated_t = flip(normed, gated)
    far = weight_parts("far_parts", FAR_JOBS, normed_t, gated_t, ups, gp)
    near = weight_parts("near_parts", NEAR_JOBS, normed_t, gated_t, ups, gp)
    grad_first, grad_out = scattered(far, near, x)
    return (grads[None], grad_first[None], grad_out[None])


def solution(mesh):
    return jax.shard_map(
        body,
        mesh=mesh,
        in_specs=(
            P("pipe", "dp", None),
            P("dp", None),
            P("pipe", "dp", None),
            P("pipe", "dp", None),
            P("dp", None),
        ),
        out_specs=(P("pipe", "dp", None), P("pipe", "dp", None), P("pipe", "dp", None)),
        check_vma=False,
    )
```

```python
import jax
import jax.numpy as jnp
from jax import lax
from jax.experimental import pallas as pl
from jax.experimental.pallas import tpu as pltpu
from jax.sharding import PartitionSpec as P

HEADS = 16
QK_DIM = 32
V_DIM = 64
EPSILON = 1e-05
D = 2048
HV = 1024
F1 = 3072
QCOL = 2 * HV
KCOL = QCOL + HEADS * QK_DIM
LEN = 128
TOKENS = 256
SIDE = 4
HALF_IN = F1 // 2
HALF_OUT = D // 2
FOLD = HALF_OUT // 2
PACK = HALF_IN + FOLD
SCALE = QK_DIM ** (-0.5)
VMEM_LIMIT = 10 * 1024 * 1024
BF16 = jnp.bfloat16
F32 = jnp.float32

NT = (((1,), (1,)), ((), ()))
TN = (((0,), (0,)), ((), ()))


def mm(left, right, dims):
    return lax.dot_general(left, right, dims, preferred_element_type=F32)


def shifted(dy, dz, dx):
    pairs = []
    for i in range(32):
        y, z, x = i // 8, (i // 2) % 4, i % 2
        pairs.append((i, ((y + dy) % 4 * 4 + (z + dz) % 4) * 2 + (x + dx) % 2))
    return pairs


def send(array, dy, dz, dx):
    return lax.ppermute(array, "dp", shifted(dy, dz, dx))


def any_spec():
    return pl.BlockSpec(memory_space=pl.ANY)


def vmem_spec():
    return pl.BlockSpec(memory_space=pltpu.VMEM)


def block_row(y, z, dy, dz, rows):
    cell = lax.rem(y + dy + SIDE, SIDE) * SIDE + lax.rem(z + dz + SIDE, SIDE)
    return pl.multiple_of(cell * rows, rows)


def here():
    spot = lax.axis_index("dp")
    return lax.shift_right_logical(spot, 3), lax.bitwise_and(lax.shift_right_logical(spot, 1), 3)


def lane_group(width):
    return lax.broadcasted_iota(jnp.int32, (LEN, LEN), 1) // width


def keep(mask, tile):
    return jnp.where(mask, tile, jnp.zeros_like(tile))


def cells(half, across):
    return [(i, across) if half == 0 else (across, i) for i in range(SIDE)]


def chosen(normed, half, across):
    y, z = here()
    cols = [block_row(y, z, -j, -k, LEN) for j, k in cells(half, across)]
    return jnp.concatenate([normed[:, pl.ds(col, LEN)] for col in cols], axis=1)


def near_front_kernel(x_ref, *refs):
    pieces, (normed, pre, w_in_t, w_out, rstd_in, left) = refs[:6], refs[6:]
    y, z = here()

    @pl.loop(0, TOKENS // 32)
    def _(step):
        rows = pl.ds(pl.multiple_of(step * 32, 32), 32)
        values = x_ref[rows, :].astype(F32)
        center = values - jnp.mean(values, axis=-1, keepdims=True)
        rstd = lax.rsqrt(jnp.mean(center * center, axis=-1, keepdims=True) + EPSILON)
        normed[rows, :] = (center * rstd).astype(BF16)
        rstd_in[rows, :] = jnp.broadcast_to(rstd, (32, LEN))

    for half in range(2):
        trio = [(pieces[3 * half + n], n, across) for n, across in enumerate((0, 1, 3))]
        for _, n, across in trio:
            left[n] = chosen(normed, half, across)
        for c in range(HALF_IN // 512):
            cols = slice(512 * c, 512 * (c + 1))
            total = jnp.zeros((TOKENS, 512), F32)
            for piece, n, _ in trio:
                right = piece[:, :, cols].reshape(SIDE * LEN, 512)
                total += jnp.dot(left[n], right, preferred_element_type=F32)
            pre[:, HALF_IN * half + 512 * c : HALF_IN * half + 512 * (c + 1)] = total
        for piece, _, across in trio:
            for at, (j, k) in enumerate(cells(half, across)):
                col = block_row(y, z, -j, -k, LEN)
                row = block_row(y, z, -j, -k, V_DIM)
                for c in range(HALF_IN // 512):
                    rows = slice(HALF_IN * half + 512 * c, HALF_IN * half + 512 * (c + 1))
                    w_in_t[rows, pl.ds(col, LEN)] = piece[at, :, 512 * c : 512 * (c + 1)].T
                for fold in range(2):
                    first = HALF_OUT * half + FOLD * fold
                    w_out[pl.ds(row, V_DIM), first : first + FOLD] = piece[
                        at, V_DIM * fold : V_DIM * (fold + 1), HALF_IN:
                    ]


def near_front(inputs, pieces):
    shapes = [
        ((TOKENS, D), BF16),
        ((TOKENS, F1), F32),
        ((F1, D), BF16),
        ((HV, D), BF16),
        ((TOKENS, LEN), F32),
    ]
    return pl.pallas_call(
        near_front_kernel,
        out_shape=[jax.ShapeDtypeStruct(*s) for s in shapes],
        in_specs=[vmem_spec()] * 7,
        out_specs=[vmem_spec()] * 5,
        scratch_shapes=[pltpu.VMEM((3, TOKENS, SIDE * LEN), BF16)],
        compiler_params=pltpu.CompilerParams(vmem_limit_bytes=VMEM_LIMIT),
        cost_estimate=pl.CostEstimate(
            flops=3 * TOKENS * D * F1 // 2, bytes_accessed=20_000_000, transcendentals=0
        ),
        name="near_front",
    )(inputs, *pieces[0][:3], *pieces[1][:3])


def front_kernel(normed, pre, wm_ref, *refs):
    fars, refs = (refs[0:2], refs[2:4]), refs[6:]
    slope, act, attn, turn, xhat, gated, rstd_mid, w_in_t, w_out = refs[:9]
    mixed, left, flipped, sems, sems_out = refs[9:]
    y, z = here()
    copies = []
    for half in range(2):
        left[...] = chosen(normed, half, 2)
        for at, (j, k) in enumerate(cells(half, 2)):
            block = fars[half][at // 2].at[at % 2]
            row = block_row(y, z, -j, -k, V_DIM)
            for fold in range(2):
                spot = w_out.at[pl.ds(row, V_DIM), pl.ds(HALF_OUT * half + FOLD * fold, FOLD)]
                part = block.at[pl.ds(V_DIM * fold, V_DIM), pl.ds(HALF_IN, FOLD)]
                copies.append(pltpu.make_async_copy(part, spot, sems_out.at[half, at, fold]))
                copies[-1].start()
        for c in range(HALF_IN // 512):
            cols = slice(512 * c, 512 * (c + 1))
            into = slice(HALF_IN * half + 512 * c, HALF_IN * half + 512 * (c + 1))
            total = pre[:, into]
            for n in range(2):
                right = fars[half][n][:, :, cols].reshape(2 * LEN, 512)
                total += jnp.dot(
                    left[:, 256 * n : 256 * (n + 1)], right, preferred_element_type=F32
                )
            squash = jax.nn.sigmoid(total)
            act[:, into] = (total * squash).astype(BF16)
            slope[:, into] = (squash * (1.0 + total * (1.0 - squash))).astype(BF16)
        for at, (j, k) in enumerate(cells(half, 2)):
            block = fars[half][at // 2]
            for c in range(HALF_IN // 512):
                flipped[half, at, 512 * c : 512 * (c + 1), :] = block[
                    at % 2, :, 512 * c : 512 * (c + 1)
                ].T
            col = block_row(y, z, -j, -k, LEN)
            spot = w_in_t.at[pl.ds(HALF_IN * half, HALF_IN), pl.ds(col, LEN)]
            copies.append(pltpu.make_async_copy(flipped.at[half, at], spot, sems.at[half, at]))
            copies[-1].start()

    quarter, half = lane_group(QK_DIM), lane_group(V_DIM)

    @pl.loop(0, TOKENS // LEN)
    def _(m):
        rows = pl.ds(pl.multiple_of(m * LEN, LEN), LEN)
        mask = wm_ref[m]
        for h4 in range(4):
            q4 = act[rows, QCOL + LEN * h4 : QCOL + LEN * (h4 + 1)]
            k4 = act[rows, KCOL + LEN * h4 : KCOL + LEN * (h4 + 1)]
            for pair in range(2):
                tile = 2 * h4 + pair
                v2 = act[rows, HV + LEN * tile : HV + LEN * (tile + 1)]
                total = jnp.zeros((LEN, LEN), F32)
                for e in range(2):
                    h = 2 * tile + e
                    score = mm(keep(quarter == 2 * pair + e, q4), k4, NT) * SCALE
                    squash = jax.nn.sigmoid(score)
                    weight = (score * squash * mask).astype(BF16)
                    attn[m, h] = weight
                    turn[m, h] = (
                        squash * (1.0 + score * (1.0 - squash)) * mask * SCALE
                    ).astype(BF16)
                    total += jnp.dot(weight, keep(half == e, v2), preferred_element_type=F32)
                mixed[:, LEN * tile : LEN * (tile + 1)] = total
        values = mixed[...]
        center = values - jnp.mean(values, axis=-1, keepdims=True)
        rstd = lax.rsqrt(jnp.mean(center * center, axis=-1, keepdims=True) + EPSILON)
        hat = center * rstd
        xhat[rows, :] = hat
        rstd_mid[rows, :] = jnp.broadcast_to(rstd, (LEN, LEN))
        gated[rows, :] = (hat * act[rows, :HV].astype(F32)).astype(BF16)

    for copy in copies:
        copy.wait()


def front(inputs, masks, pieces):
    normed, pre, w_in_t, w_out, rstd_in = near_front(inputs, pieces)
    shapes = [
        ((TOKENS, F1), BF16),
        ((TOKENS, F1), BF16),
        ((2, HEADS, LEN, LEN), BF16),
        ((2, HEADS, LEN, LEN), BF16),
        ((TOKENS, HV), F32),
        ((TOKENS, HV), BF16),
        ((TOKENS, LEN), F32),
        ((F1, D), BF16),
        ((HV, D), BF16),
    ]
    slope, act, attn, turn, xhat, gated, rstd_mid, w_in_t, w_out = pl.pallas_call(
        front_kernel,
        out_shape=[jax.ShapeDtypeStruct(*s) for s in shapes],
        in_specs=[vmem_spec()] * 7 + [any_spec()] * 2,
        out_specs=[vmem_spec()] * 7 + [any_spec()] * 2,
        input_output_aliases={7: 7, 8: 8},
        scratch_shapes=[
            pltpu.VMEM((LEN, HV), F32),
            pltpu.VMEM((TOKENS, SIDE * LEN), BF16),
            pltpu.VMEM((2, SIDE, HALF_IN, LEN), BF16),
            pltpu.SemaphoreType.DMA((2, SIDE)),
            pltpu.SemaphoreType.DMA((2, SIDE, 2)),
        ],
        compiler_params=pltpu.CompilerParams(vmem_limit_bytes=VMEM_LIMIT),
        cost_estimate=pl.CostEstimate(
            flops=TOKENS * D * F1 // 2, bytes_accessed=30_000_000, transcendentals=1_500_000
        ),
        name="front",
    )(normed, pre, masks, *pieces[0][3:], *pieces[1][3:], w_in_t, w_out)
    saved = (normed, slope, act, attn, turn, xhat, rstd_in, rstd_mid)
    return saved, gated, w_in_t, w_out


def flip_kernel(normed, gated, normed_t, gated_t):
    for c in range(D // LEN):
        normed_t[LEN * c : LEN * (c + 1), :] = normed[:, LEN * c : LEN * (c + 1)].T
    for c in range(HV // LEN):
        gated_t[LEN * c : LEN * (c + 1), :] = gated[:, LEN * c : LEN * (c + 1)].T


def flip(normed, gated):
    return pl.pallas_call(
        flip_kernel,
        out_shape=[
            jax.ShapeDtypeStruct((D, TOKENS), BF16),
            jax.ShapeDtypeStruct((HV, TOKENS), BF16),
        ],
        in_specs=[vmem_spec()] * 2,
        out_specs=[vmem_spec()] * 2,
        compiler_params=pltpu.CompilerParams(vmem_limit_bytes=VMEM_LIMIT),
        cost_estimate=pl.CostEstimate(flops=0, bytes_accessed=6_000_000, transcendentals=0),
        name="flip",
    )(normed, gated)


def chain_body(n_sources, n_carried, slot, source, *refs):
    sources, refs = refs[:n_sources], refs[n_sources:]
    w_in_t, w_out, normed, slope, act, attn, turn, xhat, rstd_in, rstd_mid = refs[:10]
    outgoing, ups_out, gp_out, grads_out, ups, gp, big, sems = refs[10 + n_carried :]
    slot, source = jnp.int32(slot), jnp.int32(source)
    rows = pl.ds(pl.multiple_of(slot * LEN, LEN), LEN)
    for i, ref in enumerate(sources):

        @pl.when(source == i)
        def _():
            ups[...] = ref[rows, :] if i == 0 else ref[...]

    put_ups = pltpu.make_async_copy(ups, ups_out.at[rows, :], sems.at[0])
    put_ups.start()

    for c in range(HV // 256):
        big[:, 256 * c : 256 * (c + 1)] = mm(ups[...], w_out[256 * c : 256 * (c + 1), :], NT)
    sums = [jnp.zeros((LEN, LEN), F32)] * 2
    for c in range(HV // LEN):
        cols = slice(LEN * c, LEN * (c + 1))
        hat = xhat[rows, cols]
        moved = big[:, cols] * act[rows, cols].astype(F32)
        sums = [sums[0] + moved, sums[1] + moved * hat]
        gp[:, cols] = (
            (big[:, cols] * hat).astype(BF16).astype(F32) * slope[rows, cols].astype(F32)
        ).astype(BF16)
        big[:, HV + LEN * c : HV + LEN * (c + 1)] = moved
    mean_one = jnp.sum(sums[0], axis=-1, keepdims=True) / HV
    mean_hat = jnp.sum(sums[1], axis=-1, keepdims=True) / HV
    rstd = rstd_mid[rows, :]

    quarter, half = lane_group(QK_DIM), lane_group(V_DIM)

    def put(value, col):
        cols = slice(col, col + LEN)
        gp[:, cols] = (
            value.astype(BF16).astype(F32) * slope[rows, cols].astype(F32)
        ).astype(BF16)

    for h4 in range(4):
        q4 = act[rows, QCOL + LEN * h4 : QCOL + LEN * (h4 + 1)]
        k4 = act[rows, KCOL + LEN * h4 : KCOL + LEN * (h4 + 1)]
        grad_q = jnp.zeros((LEN, LEN), F32)
        grad_k = jnp.zeros((LEN, LEN), F32)
        for pair in range(2):
            tile = 2 * h4 + pair
            v2 = act[rows, HV + LEN * tile : HV + LEN * (tile + 1)]
            moved = big[:, HV + LEN * tile : HV + LEN * (tile + 1)]
            hat = xhat[rows, LEN * tile : LEN * (tile + 1)]
            g2 = (rstd * (moved - mean_one - hat * mean_hat)).astype(BF16)
            grad_v = jnp.zeros((LEN, LEN), F32)
            for e in range(2):
                h = 2 * tile + e
                gh = keep(half == e, g2)
                grad_s = (mm(gh, v2, NT) * turn[slot, h].astype(F32)).astype(BF16)
                grad_v += mm(attn[slot, h], gh, TN)
                own = quarter == 2 * pair + e
                grad_q += jnp.dot(grad_s, keep(own, k4), preferred_element_type=F32)
                grad_k += mm(grad_s, keep(own, q4), TN)
            put(grad_v, HV + LEN * tile)
        put(grad_q, QCOL + LEN * h4)
        put(grad_k, KCOL + LEN * h4)

    put_gp = pltpu.make_async_copy(gp, gp_out.at[rows, :], sems.at[1])
    put_gp.start()
    sums = [jnp.zeros((LEN, LEN), F32)] * 2
    for c in range(D // 256):
        big[:, 256 * c : 256 * (c + 1)] = jnp.dot(
            gp[...], w_in_t[:, 256 * c : 256 * (c + 1)], preferred_element_type=F32
        )
        for cols in (slice(256 * c, 256 * c + LEN), slice(256 * c + LEN, 256 * (c + 1))):
            grad = big[:, cols]
            sums = [sums[0] + grad, sums[1] + grad * normed[rows, cols].astype(F32)]
    one = jnp.sum(sums[0], axis=-1, keepdims=True) / D
    two = jnp.sum(sums[1], axis=-1, keepdims=True) / D
    rstd = rstd_in[rows, :]
    for c in range(D // LEN):
        cols = slice(LEN * c, LEN * (c + 1))
        moved = rstd * (big[:, cols] - one - normed[rows, cols].astype(F32) * two)
        outgoing[:, cols] = (ups[:, cols].astype(F32) + moved).astype(BF16)
    put_grads = pltpu.make_async_copy(outgoing, grads_out.at[rows, :], sems.at[2])
    put_grads.start()
    put_ups.wait()
    put_gp.wait()
    put_grads.wait()


def chain_step(work, sources, w_in_t, w_out, saved, carried):
    kept = [((TOKENS, D), BF16), ((TOKENS, F1), BF16), ((TOKENS, D), BF16)]
    shapes = [((LEN, D), BF16)] + kept
    operands = [*sources, w_in_t, w_out, *saved, *carried]
    before = len(operands) - len(carried)
    aliases = {before + i: 1 + i for i in range(len(carried))}

    def kernel(*refs):
        section = lax.axis_index("pipe")
        if len(work) == 1:
            ((one, mine),) = work.items()
            busy = section == one
        else:
            (one, (slot, source)), (two, (slot_two, source_two)) = work.items()
            busy = jnp.logical_or(section == one, section == two)
            mine = (
                jnp.where(section == one, slot, slot_two),
                jnp.where(section == one, source, source_two),
            )

        @pl.when(busy)
        def _():
            chain_body(len(sources), len(carried), *mine, *refs)

    return pl.pallas_call(
        kernel,
        out_shape=[jax.ShapeDtypeStruct(*s) for s in shapes],
        in_specs=[vmem_spec()] * before + [any_spec()] * len(carried),
        out_specs=[vmem_spec()] + [any_spec()] * 3,
        input_output_aliases=aliases,
        scratch_shapes=[
            pltpu.VMEM((LEN, D), BF16),
            pltpu.VMEM((LEN, F1), BF16),
            pltpu.VMEM((LEN, D), F32),
            pltpu.SemaphoreType.DMA((3,)),
        ],
        compiler_params=pltpu.CompilerParams(vmem_limit_bytes=VMEM_LIMIT),
        cost_estimate=pl.CostEstimate(
            flops=2 * LEN * D * (F1 + HV), bytes_accessed=22_000_000, transcendentals=0
        ),
        name="chain",
    )(*operands)


def weights_kernel(jobs, normed_t, gated_t, ups, gp, *refs):
    outs, (rows_in, rows_out, buf, sems) = refs[: len(jobs)], refs[len(jobs) :]
    y, z = here()
    pending = [None, None]
    for count, (out, (half, blocks)) in enumerate(zip(outs, jobs)):
        turn, size = count % 2, len(blocks)
        for at, (dy, dz) in enumerate(blocks):
            row = block_row(y, z, dy, dz, LEN)
            rows_in[LEN * at : LEN * (at + 1), :] = normed_t[pl.ds(row, LEN), :]
            row = block_row(y, z, dy, dz, V_DIM)
            rows_out[V_DIM * at : V_DIM * (at + 1), :] = gated_t[pl.ds(row, V_DIM), :]
        if pending[turn] is not None:
            pending[turn].wait()
        for c in range(HALF_IN // 512):
            right = gp[:, HALF_IN * half + 512 * c : HALF_IN * half + 512 * (c + 1)]
            found = jnp.dot(rows_in[: LEN * size, :], right, preferred_element_type=F32)
            for at in range(size):
                buf[turn, at, :, 512 * c : 512 * (c + 1)] = found[
                    LEN * at : LEN * (at + 1), :
                ].astype(BF16)
        for fold in range(2):
            right = ups[:, HALF_OUT * half + FOLD * fold : HALF_OUT * half + FOLD * (fold + 1)]
            found = jnp.dot(rows_out[: V_DIM * size, :], right, preferred_element_type=F32)
            for at in range(size):
                buf[turn, at, V_DIM * fold : V_DIM * (fold + 1), HALF_IN:] = found[
                    V_DIM * at : V_DIM * (at + 1), :
                ].astype(BF16)
        pending[turn] = pltpu.make_async_copy(buf.at[turn, pl.ds(0, size)], out, sems.at[turn])
        pending[turn].start()
    for copy in pending:
        copy.wait()


def weight_parts(name, jobs, normed_t, gated_t, ups, gp):
    blocks = sum(len(job[1]) for job in jobs)
    return pl.pallas_call(
        lambda *refs: weights_kernel(jobs, *refs),
        out_shape=[jax.ShapeDtypeStruct((len(job[1]), LEN, PACK), BF16) for job in jobs],
        in_specs=[vmem_spec()] * 4,
        out_specs=[any_spec()] * len(jobs),
        scratch_shapes=[
            pltpu.VMEM((SIDE * LEN, TOKENS), BF16),
            pltpu.VMEM((SIDE * V_DIM, TOKENS), BF16),
            pltpu.VMEM((2, SIDE, LEN, PACK), BF16),
            pltpu.SemaphoreType.DMA((2,)),
        ],
        compiler_params=pltpu.CompilerParams(vmem_limit_bytes=VMEM_LIMIT),
        cost_estimate=pl.CostEstimate(
            flops=2 * TOKENS * LEN * PACK * blocks,
            bytes_accessed=4_000_000 + 2 * LEN * PACK * blocks,
            transcendentals=0,
        ),
        name=name,
    )(normed_t, gated_t, ups, gp)


FAR_JOBS = (
    (0, ((0, 2), (1, 2))),
    (0, ((2, 2), (3, 2))),
    (1, ((2, 0), (2, 1))),
    (1, ((2, 2), (2, 3))),
)
NEAR_JOBS = (
    (0, ((0, 1), (1, 1))),
    (0, ((2, 1), (3, 1))),
    (0, ((0, 3), (1, 3))),
    (0, ((2, 3), (3, 3))),
    (1, ((1, 0), (1, 1))),
    (1, ((1, 2), (1, 3))),
    (1, ((3, 0), (3, 1))),
    (1, ((3, 2), (3, 3))),
    (0, ((0, 0), (1, 0), (2, 0), (3, 0))),
    (1, ((0, 0), (0, 1), (0, 2), (0, 3))),
)


def along(axis, by):
    return (by, 0, 0) if axis == "y" else (0, by, 0)


def spread(block, axis):
    half = block.shape[0] // 2
    plus = send(block, *along(axis, 1))
    minus = send(block, *along(axis, -1))
    far_low = send(plus[:half], *along(axis, 1))
    far_high = send(minus[half:], *along(axis, -1))
    return plus, minus, far_low, far_high


def lined(block, axis):
    plus, minus, far_low, far_high = spread(block, axis)
    return jnp.stack([block, plus, jnp.concatenate([far_low, far_high], 0), minus])


def gathered(first, second, x):
    packed = jnp.concatenate([first, jnp.concatenate([second[:, :HALF_OUT], second[:, HALF_OUT:]], 0)], 1)
    other = send(packed, 0, 0, 1)
    low = jnp.where(x == 0, packed, other)
    high = jnp.where(x == 0, other, packed)
    rows = second.shape[0]
    lines = []
    for half in range(2):
        cols = slice(HALF_IN * half, HALF_IN * (half + 1))
        part = slice(rows * half, rows * (half + 1))
        out = jnp.concatenate([low[part, F1:], high[part, F1:]], 0)
        block = jnp.concatenate(
            [
                jnp.concatenate([low[:, cols], high[:, cols]], 0),
                jnp.concatenate([out[:, :FOLD], out[:, FOLD:]], 0),
            ],
            1,
        )
        lines.append(lined(block, "yz"[half]))
    return [(line, *spread(line, "zy"[half])) for half, line in enumerate(lines)]


def added(*arrays):
    total = arrays[0].astype(F32)
    for array in arrays[1:]:
        total = total + array.astype(F32)
    return total


def joined(own, plus_low, plus_high, minus_low, minus_high, far_low, far_high, axis):
    through = send(far_low, *along(axis, 1))
    back = send(far_high, *along(axis, -1))
    plus = jnp.concatenate([added(plus_low, through).astype(BF16), plus_high], 0)
    minus = jnp.concatenate([minus_low, added(minus_high, back).astype(BF16)], 0)
    return added(own, send(plus, *along(axis, 1)), send(minus, *along(axis, -1)))


def scattered(far, near, x):
    a_one = joined(near[8], *near[0:4], far[0], far[1], "z").astype(BF16)
    b_one = joined(near[9], *near[4:8], far[2], far[3], "y").astype(BF16)
    ends = []
    for line, axis in ((a_one, "y"), (b_one, "z")):
        cut = [part for block in (1, 3, 2) for part in (line[block, :V_DIM], line[block, V_DIM:])]
        ends.append(joined(line[0], *cut, axis))
    first = jnp.concatenate([end[:, :HALF_IN] for end in ends], 1)
    folded = jnp.concatenate([end[:, HALF_IN:] for end in ends], 1)
    outs = [folded[:V_DIM, :FOLD], folded[V_DIM:, :FOLD], folded[:V_DIM, FOLD:], folded[V_DIM:, FOLD:]]
    second = jnp.concatenate(outs, 1)
    sides = []
    for side in range(2):
        mine = second[32 * side : 32 * (side + 1)]
        tall = jnp.concatenate([mine[:, :HALF_OUT], mine[:, HALF_OUT:]], 0)
        sides.append(jnp.concatenate([first[64 * side : 64 * (side + 1)], tall], 1))
    away = jnp.where(x == 0, sides[1], sides[0]).astype(BF16)
    total = jnp.where(x == 0, sides[0], sides[1]) + send(away, 0, 0, 1).astype(F32)
    grad_out = jnp.concatenate([total[:32, F1:], total[32:, F1:]], 1)
    return total[:, :F1], grad_out


def body(section_input, top_grad, w_in, w_out, segments):
    x = lax.axis_index("dp") % 2
    pieces = gathered(w_in[0], w_out[0], x)

    same = segments[:, :, None] == segments[:, None, :]
    lower = lax.broadcasted_iota(jnp.int32, (LEN, LEN), 1) <= lax.broadcasted_iota(
        jnp.int32, (LEN, LEN), 0
    )
    counts = jnp.sum(same.astype(F32), axis=2, keepdims=True)
    masks = jnp.where(jnp.logical_and(same, lower[None]), 1.0 / counts, 0.0)

    saved, gated, w_first, w_second = front(section_input[0], masks, pieces)

    def step(work, sources, carried):
        outgoing, *carried = chain_step(
            work, (top_grad, *sources), w_first, w_second, saved, tuple(carried)
        )
        return outgoing, carried

    def below(array, which):
        return lax.ppermute(array, "pipe", [(which, which - 1)])

    out_0, carried = step({3: (0, 0)}, (), ())
    out_1, carried = step({3: (1, 0), 2: (0, 1)}, (below(out_0, 3),), carried)
    to_one = below(out_1, 2)
    out_2, carried = step({2: (1, 1)}, (below(out_1, 3),), carried)
    again = below(out_2, 2)
    out_3, carried = step({1: (0, 1)}, (to_one,), carried)
    out_4, carried = step({1: (1, 1), 0: (0, 2)}, (again, below(out_3, 1)), carried)
    _, carried = step({0: (1, 1)}, (below(out_4, 1),), carried)
    ups, gp, grads = carried

    normed_t, gated_t = flip(saved[0], gated)
    far = weight_parts("far_parts", FAR_JOBS, normed_t, gated_t, ups, gp)
    near = weight_parts("near_parts", NEAR_JOBS, normed_t, gated_t, ups, gp)
    grad_first, grad_out = scattered(far, near, x)
    return (grads[None], grad_first[None], grad_out[None])


def solution(mesh):
    return jax.shard_map(
        body,
        mesh=mesh,
        in_specs=(
            P("pipe", "dp", None),
            P("dp", None),
            P("pipe", "dp", None),
            P("pipe", "dp", None),
            P("dp", None),
        ),
        out_specs=(P("pipe", "dp", None), P("pipe", "dp", None), P("pipe", "dp", None)),
        check_vma=False,
    )
```

```python
import jax
import jax.numpy as jnp
from jax import lax
from jax.experimental import pallas as pl
from jax.experimental.pallas import tpu as pltpu
from jax.sharding import PartitionSpec as P

HEADS = 16
QK_DIM = 32
V_DIM = 64
EPSILON = 1e-05
D = 2048
HV = 1024
F1 = 3072
QCOL = 2 * HV
KCOL = QCOL + HEADS * QK_DIM
LEN = 128
TOKENS = 256
SIDE = 4
HALF_IN = F1 // 2
HALF_OUT = D // 2
FOLD = HALF_OUT // 2
PACK = HALF_IN + FOLD
SCALE = QK_DIM ** (-0.5)
VMEM_LIMIT = 10 * 1024 * 1024
BF16 = jnp.bfloat16
F32 = jnp.float32

NT = (((1,), (1,)), ((), ()))
TN = (((0,), (0,)), ((), ()))


def mm(left, right, dims):
    return lax.dot_general(left, right, dims, preferred_element_type=F32)


def shifted(dy, dz, dx):
    pairs = []
    for i in range(32):
        y, z, x = i // 8, (i // 2) % 4, i % 2
        pairs.append((i, ((y + dy) % 4 * 4 + (z + dz) % 4) * 2 + (x + dx) % 2))
    return pairs


def send(array, dy, dz, dx):
    return lax.ppermute(array, "dp", shifted(dy, dz, dx))


def any_spec():
    return pl.BlockSpec(memory_space=pl.ANY)


def vmem_spec():
    return pl.BlockSpec(memory_space=pltpu.VMEM)


def block_row(y, z, dy, dz, rows):
    cell = lax.rem(y + dy + SIDE, SIDE) * SIDE + lax.rem(z + dz + SIDE, SIDE)
    return pl.multiple_of(cell * rows, rows)


def here():
    spot = lax.axis_index("dp")
    return lax.shift_right_logical(spot, 3), lax.bitwise_and(lax.shift_right_logical(spot, 1), 3)


def lane_group(width):
    return lax.broadcasted_iota(jnp.int32, (LEN, LEN), 1) // width


def keep(mask, tile):
    return jnp.where(mask, tile, jnp.zeros_like(tile))


def cells(half, across):
    return [(i, across) if half == 0 else (across, i) for i in range(SIDE)]


def chosen(normed, half, across):
    y, z = here()
    cols = [block_row(y, z, -j, -k, LEN) for j, k in cells(half, across)]
    return jnp.concatenate([normed[:, pl.ds(col, LEN)] for col in cols], axis=1)


def near_front_kernel(x_ref, *refs):
    pieces, (normed, pre, w_in_t, rstd_in, left) = refs[:6], refs[6:]
    y, z = here()

    @pl.loop(0, TOKENS // 32)
    def _(step):
        rows = pl.ds(pl.multiple_of(step * 32, 32), 32)
        values = x_ref[rows, :].astype(F32)
        center = values - jnp.mean(values, axis=-1, keepdims=True)
        rstd = lax.rsqrt(jnp.mean(center * center, axis=-1, keepdims=True) + EPSILON)
        normed[rows, :] = (center * rstd).astype(BF16)
        rstd_in[rows, :] = jnp.broadcast_to(rstd, (32, LEN))

    for half in range(2):
        trio = [(pieces[3 * half + n], n, across) for n, across in enumerate((0, 1, 3))]
        for _, n, across in trio:
            left[n] = chosen(normed, half, across)
        for c in range(HALF_IN // 512):
            cols = slice(512 * c, 512 * (c + 1))
            total = jnp.zeros((TOKENS, 512), F32)
            for piece, n, _ in trio:
                right = piece[:, :, cols].reshape(SIDE * LEN, 512)
                total += jnp.dot(left[n], right, preferred_element_type=F32)
            pre[:, HALF_IN * half + 512 * c : HALF_IN * half + 512 * (c + 1)] = total
        for piece, _, across in trio:
            for at, (j, k) in enumerate(cells(half, across)):
                col = block_row(y, z, -j, -k, LEN)
                for c in range(HALF_IN // 512):
                    rows = slice(HALF_IN * half + 512 * c, HALF_IN * half + 512 * (c + 1))
                    w_in_t[rows, pl.ds(col, LEN)] = piece[at, :, 512 * c : 512 * (c + 1)].T


def near_front(inputs, pieces):
    shapes = [
        ((TOKENS, D), BF16),
        ((TOKENS, F1), F32),
        ((F1, D), BF16),
        ((TOKENS, LEN), F32),
    ]
    return pl.pallas_call(
        near_front_kernel,
        out_shape=[jax.ShapeDtypeStruct(*s) for s in shapes],
        in_specs=[vmem_spec()] * 7,
        out_specs=[vmem_spec()] * 4,
        scratch_shapes=[pltpu.VMEM((3, TOKENS, SIDE * LEN), BF16)],
        compiler_params=pltpu.CompilerParams(vmem_limit_bytes=VMEM_LIMIT),
        cost_estimate=pl.CostEstimate(
            flops=3 * TOKENS * D * F1 // 2, bytes_accessed=20_000_000, transcendentals=0
        ),
        name="near_front",
    )(inputs, *pieces[0][:3], *pieces[1][:3])


def front_kernel(normed, pre, wm_ref, *refs):
    fars, refs = (refs[0:2], refs[2:4]), refs[5:]
    slope, act, attn, turn, xhat, gated, rstd_mid, w_in_t = refs[:8]
    mixed, left, flipped, sems = refs[8:]
    y, z = here()
    copies = []
    for half in range(2):
        left[...] = chosen(normed, half, 2)
        for c in range(HALF_IN // 512):
            cols = slice(512 * c, 512 * (c + 1))
            into = slice(HALF_IN * half + 512 * c, HALF_IN * half + 512 * (c + 1))
            total = pre[:, into]
            for n in range(2):
                right = fars[half][n][:, :, cols].reshape(2 * LEN, 512)
                total += jnp.dot(
                    left[:, 256 * n : 256 * (n + 1)], right, preferred_element_type=F32
                )
            squash = jax.nn.sigmoid(total)
            act[:, into] = (total * squash).astype(BF16)
            slope[:, into] = (squash * (1.0 + total * (1.0 - squash))).astype(BF16)
        for at, (j, k) in enumerate(cells(half, 2)):
            block = fars[half][at // 2]
            for c in range(HALF_IN // 512):
                flipped[half, at, 512 * c : 512 * (c + 1), :] = block[
                    at % 2, :, 512 * c : 512 * (c + 1)
                ].T
            col = block_row(y, z, -j, -k, LEN)
            spot = w_in_t.at[pl.ds(HALF_IN * half, HALF_IN), pl.ds(col, LEN)]
            copies.append(pltpu.make_async_copy(flipped.at[half, at], spot, sems.at[half, at]))
            copies[-1].start()

    quarter, half = lane_group(QK_DIM), lane_group(V_DIM)

    @pl.loop(0, TOKENS // LEN)
    def _(m):
        rows = pl.ds(pl.multiple_of(m * LEN, LEN), LEN)
        mask = wm_ref[m]
        for h4 in range(4):
            q4 = act[rows, QCOL + LEN * h4 : QCOL + LEN * (h4 + 1)]
            k4 = act[rows, KCOL + LEN * h4 : KCOL + LEN * (h4 + 1)]
            for pair in range(2):
                tile = 2 * h4 + pair
                v2 = act[rows, HV + LEN * tile : HV + LEN * (tile + 1)]
                total = jnp.zeros((LEN, LEN), F32)
                for e in range(2):
                    h = 2 * tile + e
                    score = mm(keep(quarter == 2 * pair + e, q4), k4, NT) * SCALE
                    squash = jax.nn.sigmoid(score)
                    weight = (score * squash * mask).astype(BF16)
                    attn[m, h] = weight
                    turn[m, h] = (
                        squash * (1.0 + score * (1.0 - squash)) * mask * SCALE
                    ).astype(BF16)
                    total += jnp.dot(weight, keep(half == e, v2), preferred_element_type=F32)
                mixed[:, LEN * tile : LEN * (tile + 1)] = total
        values = mixed[...]
        center = values - jnp.mean(values, axis=-1, keepdims=True)
        rstd = lax.rsqrt(jnp.mean(center * center, axis=-1, keepdims=True) + EPSILON)
        hat = center * rstd
        xhat[rows, :] = hat
        rstd_mid[rows, :] = jnp.broadcast_to(rstd, (LEN, LEN))
        gated[rows, :] = (hat * act[rows, :HV].astype(F32)).astype(BF16)

    for copy in copies:
        copy.wait()


def front(inputs, masks, pieces):
    normed, pre, w_in_t, rstd_in = near_front(inputs, pieces)
    shapes = [
        ((TOKENS, F1), BF16),
        ((TOKENS, F1), BF16),
        ((2, HEADS, LEN, LEN), BF16),
        ((2, HEADS, LEN, LEN), BF16),
        ((TOKENS, HV), F32),
        ((TOKENS, HV), BF16),
        ((TOKENS, LEN), F32),
        ((F1, D), BF16),
    ]
    slope, act, attn, turn, xhat, gated, rstd_mid, w_in_t = pl.pallas_call(
        front_kernel,
        out_shape=[jax.ShapeDtypeStruct(*s) for s in shapes],
        in_specs=[vmem_spec()] * 7 + [any_spec()],
        out_specs=[vmem_spec()] * 7 + [any_spec()],
        input_output_aliases={7: 7},
        scratch_shapes=[
            pltpu.VMEM((LEN, HV), F32),
            pltpu.VMEM((TOKENS, SIDE * LEN), BF16),
            pltpu.VMEM((2, SIDE, HALF_IN, LEN), BF16),
            pltpu.SemaphoreType.DMA((2, SIDE)),
        ],
        compiler_params=pltpu.CompilerParams(vmem_limit_bytes=VMEM_LIMIT),
        cost_estimate=pl.CostEstimate(
            flops=TOKENS * D * F1 // 2, bytes_accessed=30_000_000, transcendentals=1_500_000
        ),
        name="front",
    )(normed, pre, masks, *pieces[0][3:], *pieces[1][3:], w_in_t)
    saved = (normed, slope, act, attn, turn, xhat, rstd_in, rstd_mid)
    return saved, gated, w_in_t


def flip_kernel(normed, gated, normed_t, gated_t):
    for c in range(D // LEN):
        normed_t[LEN * c : LEN * (c + 1), :] = normed[:, LEN * c : LEN * (c + 1)].T
    for c in range(HV // LEN):
        gated_t[LEN * c : LEN * (c + 1), :] = gated[:, LEN * c : LEN * (c + 1)].T


def flip(normed, gated):
    return pl.pallas_call(
        flip_kernel,
        out_shape=[
            jax.ShapeDtypeStruct((D, TOKENS), BF16),
            jax.ShapeDtypeStruct((HV, TOKENS), BF16),
        ],
        in_specs=[vmem_spec()] * 2,
        out_specs=[vmem_spec()] * 2,
        compiler_params=pltpu.CompilerParams(vmem_limit_bytes=VMEM_LIMIT),
        cost_estimate=pl.CostEstimate(flops=0, bytes_accessed=6_000_000, transcendentals=0),
        name="flip",
    )(normed, gated)


def chain_body(n_sources, n_carried, slot, source, *refs):
    sources, refs = refs[:n_sources], refs[n_sources:]
    w_in_t, w_out, normed, slope, act, attn, turn, xhat, rstd_in, rstd_mid = refs[:10]
    outgoing, ups_out, gp_out, grads_out, ups, gp, big, sems = refs[10 + n_carried :]
    slot, source = jnp.int32(slot), jnp.int32(source)
    rows = pl.ds(pl.multiple_of(slot * LEN, LEN), LEN)
    for i, ref in enumerate(sources):

        @pl.when(source == i)
        def _():
            ups[...] = ref[rows, :] if i == 0 else ref[...]

    put_ups = pltpu.make_async_copy(ups, ups_out.at[rows, :], sems.at[0])
    put_ups.start()

    for c in range(HV // 256):
        big[:, 256 * c : 256 * (c + 1)] = mm(ups[...], w_out[256 * c : 256 * (c + 1), :], NT)
    sums = [jnp.zeros((LEN, LEN), F32)] * 2
    for c in range(HV // LEN):
        cols = slice(LEN * c, LEN * (c + 1))
        hat = xhat[rows, cols]
        moved = big[:, cols] * act[rows, cols].astype(F32)
        sums = [sums[0] + moved, sums[1] + moved * hat]
        gp[:, cols] = (
            (big[:, cols] * hat).astype(BF16).astype(F32) * slope[rows, cols].astype(F32)
        ).astype(BF16)
        big[:, HV + LEN * c : HV + LEN * (c + 1)] = moved
    mean_one = jnp.sum(sums[0], axis=-1, keepdims=True) / HV
    mean_hat = jnp.sum(sums[1], axis=-1, keepdims=True) / HV
    rstd = rstd_mid[rows, :]

    quarter, half = lane_group(QK_DIM), lane_group(V_DIM)

    def put(value, col):
        cols = slice(col, col + LEN)
        gp[:, cols] = (
            value.astype(BF16).astype(F32) * slope[rows, cols].astype(F32)
        ).astype(BF16)

    for h4 in range(4):
        q4 = act[rows, QCOL + LEN * h4 : QCOL + LEN * (h4 + 1)]
        k4 = act[rows, KCOL + LEN * h4 : KCOL + LEN * (h4 + 1)]
        grad_q = jnp.zeros((LEN, LEN), F32)
        grad_k = jnp.zeros((LEN, LEN), F32)
        for pair in range(2):
            tile = 2 * h4 + pair
            v2 = act[rows, HV + LEN * tile : HV + LEN * (tile + 1)]
            moved = big[:, HV + LEN * tile : HV + LEN * (tile + 1)]
            hat = xhat[rows, LEN * tile : LEN * (tile + 1)]
            g2 = (rstd * (moved - mean_one - hat * mean_hat)).astype(BF16)
            grad_v = jnp.zeros((LEN, LEN), F32)
            for e in range(2):
                h = 2 * tile + e
                gh = keep(half == e, g2)
                grad_s = (mm(gh, v2, NT) * turn[slot, h].astype(F32)).astype(BF16)
                grad_v += mm(attn[slot, h], gh, TN)
                own = quarter == 2 * pair + e
                grad_q += jnp.dot(grad_s, keep(own, k4), preferred_element_type=F32)
                grad_k += mm(grad_s, keep(own, q4), TN)
            put(grad_v, HV + LEN * tile)
        put(grad_q, QCOL + LEN * h4)
        put(grad_k, KCOL + LEN * h4)

    put_gp = pltpu.make_async_copy(gp, gp_out.at[rows, :], sems.at[1])
    put_gp.start()
    sums = [jnp.zeros((LEN, LEN), F32)] * 2
    for c in range(D // 256):
        big[:, 256 * c : 256 * (c + 1)] = jnp.dot(
            gp[...], w_in_t[:, 256 * c : 256 * (c + 1)], preferred_element_type=F32
        )
        for cols in (slice(256 * c, 256 * c + LEN), slice(256 * c + LEN, 256 * (c + 1))):
            grad = big[:, cols]
            sums = [sums[0] + grad, sums[1] + grad * normed[rows, cols].astype(F32)]
    one = jnp.sum(sums[0], axis=-1, keepdims=True) / D
    two = jnp.sum(sums[1], axis=-1, keepdims=True) / D
    rstd = rstd_in[rows, :]
    for c in range(D // LEN):
        cols = slice(LEN * c, LEN * (c + 1))
        moved = rstd * (big[:, cols] - one - normed[rows, cols].astype(F32) * two)
        outgoing[:, cols] = (ups[:, cols].astype(F32) + moved).astype(BF16)
    put_grads = pltpu.make_async_copy(outgoing, grads_out.at[rows, :], sems.at[2])
    put_grads.start()
    put_ups.wait()
    put_gp.wait()
    put_grads.wait()


def chain_step(work, sources, w_in_t, w_out, saved, carried):
    kept = [((TOKENS, D), BF16), ((TOKENS, F1), BF16), ((TOKENS, D), BF16)]
    shapes = [((LEN, D), BF16)] + kept
    operands = [*sources, w_in_t, w_out, *saved, *carried]
    before = len(operands) - len(carried)
    aliases = {before + i: 1 + i for i in range(len(carried))}

    def kernel(*refs):
        section = lax.axis_index("pipe")
        if len(work) == 1:
            ((one, mine),) = work.items()
            busy = section == one
        else:
            (one, (slot, source)), (two, (slot_two, source_two)) = work.items()
            busy = jnp.logical_or(section == one, section == two)
            mine = (
                jnp.where(section == one, slot, slot_two),
                jnp.where(section == one, source, source_two),
            )

        @pl.when(busy)
        def _():
            chain_body(len(sources), len(carried), *mine, *refs)

    return pl.pallas_call(
        kernel,
        out_shape=[jax.ShapeDtypeStruct(*s) for s in shapes],
        in_specs=[vmem_spec()] * before + [any_spec()] * len(carried),
        out_specs=[vmem_spec()] + [any_spec()] * 3,
        input_output_aliases=aliases,
        scratch_shapes=[
            pltpu.VMEM((LEN, D), BF16),
            pltpu.VMEM((LEN, F1), BF16),
            pltpu.VMEM((LEN, D), F32),
            pltpu.SemaphoreType.DMA((3,)),
        ],
        compiler_params=pltpu.CompilerParams(vmem_limit_bytes=VMEM_LIMIT),
        cost_estimate=pl.CostEstimate(
            flops=2 * LEN * D * (F1 + HV), bytes_accessed=22_000_000, transcendentals=0
        ),
        name="chain",
    )(*operands)


def weights_kernel(jobs, normed_t, gated_t, ups, gp, *refs):
    outs, (rows_in, rows_out, buf, sems) = refs[: len(jobs)], refs[len(jobs) :]
    y, z = here()
    pending = [None, None]
    for count, (out, (half, blocks)) in enumerate(zip(outs, jobs)):
        turn, size = count % 2, len(blocks)
        for at, (dy, dz) in enumerate(blocks):
            row = block_row(y, z, dy, dz, LEN)
            rows_in[LEN * at : LEN * (at + 1), :] = normed_t[pl.ds(row, LEN), :]
            row = block_row(y, z, dy, dz, V_DIM)
            rows_out[V_DIM * at : V_DIM * (at + 1), :] = gated_t[pl.ds(row, V_DIM), :]
        if pending[turn] is not None:
            pending[turn].wait()
        for c in range(HALF_IN // 512):
            right = gp[:, HALF_IN * half + 512 * c : HALF_IN * half + 512 * (c + 1)]
            found = jnp.dot(rows_in[: LEN * size, :], right, preferred_element_type=F32)
            for at in range(size):
                buf[turn, at, :, 512 * c : 512 * (c + 1)] = found[
                    LEN * at : LEN * (at + 1), :
                ].astype(BF16)
        for fold in range(2):
            right = ups[:, HALF_OUT * half + FOLD * fold : HALF_OUT * half + FOLD * (fold + 1)]
            found = jnp.dot(rows_out[: V_DIM * size, :], right, preferred_element_type=F32)
            for at in range(size):
                buf[turn, at, V_DIM * fold : V_DIM * (fold + 1), HALF_IN:] = found[
                    V_DIM * at : V_DIM * (at + 1), :
                ].astype(BF16)
        pending[turn] = pltpu.make_async_copy(buf.at[turn, pl.ds(0, size)], out, sems.at[turn])
        pending[turn].start()
    for copy in pending:
        copy.wait()


def weight_parts(name, jobs, normed_t, gated_t, ups, gp):
    blocks = sum(len(job[1]) for job in jobs)
    return pl.pallas_call(
        lambda *refs: weights_kernel(jobs, *refs),
        out_shape=[jax.ShapeDtypeStruct((len(job[1]), LEN, PACK), BF16) for job in jobs],
        in_specs=[vmem_spec()] * 4,
        out_specs=[any_spec()] * len(jobs),
        scratch_shapes=[
            pltpu.VMEM((SIDE * LEN, TOKENS), BF16),
            pltpu.VMEM((SIDE * V_DIM, TOKENS), BF16),
            pltpu.VMEM((2, SIDE, LEN, PACK), BF16),
            pltpu.SemaphoreType.DMA((2,)),
        ],
        compiler_params=pltpu.CompilerParams(vmem_limit_bytes=VMEM_LIMIT),
        cost_estimate=pl.CostEstimate(
            flops=2 * TOKENS * LEN * PACK * blocks,
            bytes_accessed=4_000_000 + 2 * LEN * PACK * blocks,
            transcendentals=0,
        ),
        name=name,
    )(normed_t, gated_t, ups, gp)


FAR_JOBS = (
    (0, ((0, 2), (1, 2))),
    (0, ((2, 2), (3, 2))),
    (1, ((2, 0), (2, 1))),
    (1, ((2, 2), (2, 3))),
)
NEAR_JOBS = (
    (0, ((0, 1), (1, 1))),
    (0, ((2, 1), (3, 1))),
    (0, ((0, 3), (1, 3))),
    (0, ((2, 3), (3, 3))),
    (1, ((1, 0), (1, 1))),
    (1, ((1, 2), (1, 3))),
    (1, ((3, 0), (3, 1))),
    (1, ((3, 2), (3, 3))),
    (0, ((0, 0), (1, 0), (2, 0), (3, 0))),
    (1, ((0, 0), (0, 1), (0, 2), (0, 3))),
)


def along(axis, by):
    return (by, 0, 0) if axis == "y" else (0, by, 0)


def spread(block, axis):
    half = block.shape[0] // 2
    plus = send(block, *along(axis, 1))
    minus = send(block, *along(axis, -1))
    far_low = send(plus[:half], *along(axis, 1))
    far_high = send(minus[half:], *along(axis, -1))
    return plus, minus, far_low, far_high


def lined(block, axis):
    plus, minus, far_low, far_high = spread(block, axis)
    return jnp.stack([block, plus, jnp.concatenate([far_low, far_high], 0), minus])


def gathered(shard, x):
    other = send(shard, 0, 0, 1)
    low = jnp.where(x == 0, shard, other)
    high = jnp.where(x == 0, other, shard)
    pieces = []
    for half in range(2):
        cols = slice(HALF_IN * half, HALF_IN * (half + 1))
        line = lined(jnp.concatenate([low[:, cols], high[:, cols]], 0), "yz"[half])
        pieces.append((line, *spread(line, "zy"[half])))
    return pieces


def added(*arrays):
    total = arrays[0].astype(F32)
    for array in arrays[1:]:
        total = total + array.astype(F32)
    return total


def joined(own, plus_low, plus_high, minus_low, minus_high, far_low, far_high, axis):
    through = send(far_low, *along(axis, 1))
    back = send(far_high, *along(axis, -1))
    plus = jnp.concatenate([added(plus_low, through).astype(BF16), plus_high], 0)
    minus = jnp.concatenate([minus_low, added(minus_high, back).astype(BF16)], 0)
    return added(own, send(plus, *along(axis, 1)), send(minus, *along(axis, -1)))


def scattered(far, near, x):
    a_one = joined(near[8], *near[0:4], far[0], far[1], "z").astype(BF16)
    b_one = joined(near[9], *near[4:8], far[2], far[3], "y").astype(BF16)
    ends = []
    for line, axis in ((a_one, "y"), (b_one, "z")):
        cut = [part for block in (1, 3, 2) for part in (line[block, :V_DIM], line[block, V_DIM:])]
        ends.append(joined(line[0], *cut, axis))
    first = jnp.concatenate([end[:, :HALF_IN] for end in ends], 1)
    folded = jnp.concatenate([end[:, HALF_IN:] for end in ends], 1)
    outs = [folded[:V_DIM, :FOLD], folded[V_DIM:, :FOLD], folded[:V_DIM, FOLD:], folded[V_DIM:, FOLD:]]
    second = jnp.concatenate(outs, 1)
    sides = []
    for side in range(2):
        mine = second[32 * side : 32 * (side + 1)]
        tall = jnp.concatenate([mine[:, :HALF_OUT], mine[:, HALF_OUT:]], 0)
        sides.append(jnp.concatenate([first[64 * side : 64 * (side + 1)], tall], 1))
    away = jnp.where(x == 0, sides[1], sides[0]).astype(BF16)
    total = jnp.where(x == 0, sides[0], sides[1]) + send(away, 0, 0, 1).astype(F32)
    grad_out = jnp.concatenate([total[:32, F1:], total[32:, F1:]], 1)
    return total[:, :F1], grad_out


def body(section_input, top_grad, w_in, w_out, segments):
    x = lax.axis_index("dp") % 2
    w_second = lax.all_gather(w_out[0], "dp", axis=0, tiled=True)
    pieces = gathered(w_in[0], x)

    same = segments[:, :, None] == segments[:, None, :]
    lower = lax.broadcasted_iota(jnp.int32, (LEN, LEN), 1) <= lax.broadcasted_iota(
        jnp.int32, (LEN, LEN), 0
    )
    counts = jnp.sum(same.astype(F32), axis=2, keepdims=True)
    masks = jnp.where(jnp.logical_and(same, lower[None]), 1.0 / counts, 0.0)

    saved, gated, w_first = front(section_input[0], masks, pieces)

    def step(work, sources, carried):
        outgoing, *carried = chain_step(
            work, (top_grad, *sources), w_first, w_second, saved, tuple(carried)
        )
        return outgoing, carried

    def below(array, which):
        return lax.ppermute(array, "pipe", [(which, which - 1)])

    out_0, carried = step({3: (0, 0)}, (), ())
    out_1, carried = step({3: (1, 0), 2: (0, 1)}, (below(out_0, 3),), carried)
    to_one = below(out_1, 2)
    out_2, carried = step({2: (1, 1)}, (below(out_1, 3),), carried)
    again = below(out_2, 2)
    out_3, carried = step({1: (0, 1)}, (to_one,), carried)
    out_4, carried = step({1: (1, 1), 0: (0, 2)}, (again, below(out_3, 1)), carried)
    _, carried = step({0: (1, 1)}, (below(out_4, 1),), carried)
    ups, gp, grads = carried

    normed_t, gated_t = flip(saved[0], gated)
    far = weight_parts("far_parts", FAR_JOBS, normed_t, gated_t, ups, gp)
    near = weight_parts("near_parts", NEAR_JOBS, normed_t, gated_t, ups, gp)
    grad_first, grad_out = scattered(far, near, x)
    return (grads[None], grad_first[None], grad_out[None])


def solution(mesh):
    return jax.shard_map(
        body,
        mesh=mesh,
        in_specs=(
            P("pipe", "dp", None),
            P("dp", None),
            P("pipe", "dp", None),
            P("pipe", "dp", None),
            P("dp", None),
        ),
        out_specs=(P("pipe", "dp", None), P("pipe", "dp", None), P("pipe", "dp", None)),
        check_vma=False,
    )
```

```python
import jax
import jax.numpy as jnp
from jax import lax
from jax.experimental import pallas as pl
from jax.experimental.pallas import tpu as pltpu
from jax.sharding import PartitionSpec as P

HEADS = 16
QK_DIM = 32
V_DIM = 64
EPSILON = 1e-05
D = 2048
HV = 1024
F1 = 3072
QCOL = 2 * HV
KCOL = QCOL + HEADS * QK_DIM
LEN = 128
TOKENS = 256
SIDE = 4
HALF_IN = F1 // 2
HALF_OUT = D // 2
FOLD = HALF_OUT // 2
PACK = HALF_IN + FOLD
SCALE = QK_DIM ** (-0.5)
VMEM_LIMIT = 10 * 1024 * 1024
BF16 = jnp.bfloat16
F32 = jnp.float32

NT = (((1,), (1,)), ((), ()))
TN = (((0,), (0,)), ((), ()))


def mm(left, right, dims):
    return lax.dot_general(left, right, dims, preferred_element_type=F32)


def shifted(dy, dz, dx):
    pairs = []
    for i in range(32):
        y, z, x = i // 8, (i // 2) % 4, i % 2
        pairs.append((i, ((y + dy) % 4 * 4 + (z + dz) % 4) * 2 + (x + dx) % 2))
    return pairs


def send(array, dy, dz, dx):
    return lax.ppermute(array, "dp", shifted(dy, dz, dx))


def any_spec():
    return pl.BlockSpec(memory_space=pl.ANY)


def vmem_spec():
    return pl.BlockSpec(memory_space=pltpu.VMEM)


def block_row(y, z, dy, dz, rows):
    cell = lax.rem(y + dy + SIDE, SIDE) * SIDE + lax.rem(z + dz + SIDE, SIDE)
    return pl.multiple_of(cell * rows, rows)


def here():
    spot = lax.axis_index("dp")
    return lax.shift_right_logical(spot, 3), lax.bitwise_and(lax.shift_right_logical(spot, 1), 3)


def lane_group(width):
    return lax.broadcasted_iota(jnp.int32, (LEN, LEN), 1) // width


def keep(mask, tile):
    return jnp.where(mask, tile, jnp.zeros_like(tile))


def cells(half, across):
    return [(i, across) if half == 0 else (across, i) for i in range(SIDE)]


def chosen(normed, half, across):
    y, z = here()
    cols = [block_row(y, z, -j, -k, LEN) for j, k in cells(half, across)]
    return jnp.concatenate([normed[:, pl.ds(col, LEN)] for col in cols], axis=1)


def near_front_kernel(x_ref, w_second, *refs):
    pieces, (normed, pre, w_in_t, w_out_t, rstd_in, left) = refs[:6], refs[6:]
    y, z = here()

    @pl.loop(0, TOKENS // 32)
    def _(step):
        rows = pl.ds(pl.multiple_of(step * 32, 32), 32)
        values = x_ref[rows, :].astype(F32)
        center = values - jnp.mean(values, axis=-1, keepdims=True)
        rstd = lax.rsqrt(jnp.mean(center * center, axis=-1, keepdims=True) + EPSILON)
        normed[rows, :] = (center * rstd).astype(BF16)
        rstd_in[rows, :] = jnp.broadcast_to(rstd, (32, LEN))

    for half in range(2):
        trio = [(pieces[3 * half + n], n, across) for n, across in enumerate((0, 1, 3))]
        for _, n, across in trio:
            left[n] = chosen(normed, half, across)
        for c in range(HALF_IN // 512):
            cols = slice(512 * c, 512 * (c + 1))
            total = jnp.zeros((TOKENS, 512), F32)
            for piece, n, _ in trio:
                right = piece[:, :, cols].reshape(SIDE * LEN, 512)
                total += jnp.dot(left[n], right, preferred_element_type=F32)
            pre[:, HALF_IN * half + 512 * c : HALF_IN * half + 512 * (c + 1)] = total
        for piece, _, across in trio:
            for at, (j, k) in enumerate(cells(half, across)):
                col = block_row(y, z, -j, -k, LEN)
                for c in range(HALF_IN // 512):
                    rows = slice(HALF_IN * half + 512 * c, HALF_IN * half + 512 * (c + 1))
                    w_in_t[rows, pl.ds(col, LEN)] = piece[at, :, 512 * c : 512 * (c + 1)].T
    for r in range(HV // LEN):
        for c in range(D // 512):
            w_out_t[512 * c : 512 * (c + 1), LEN * r : LEN * (r + 1)] = w_second[
                LEN * r : LEN * (r + 1), 512 * c : 512 * (c + 1)
            ].T


def near_front(inputs, w_second, pieces):
    shapes = [
        ((TOKENS, D), BF16),
        ((TOKENS, F1), F32),
        ((F1, D), BF16),
        ((D, HV), BF16),
        ((TOKENS, LEN), F32),
    ]
    return pl.pallas_call(
        near_front_kernel,
        out_shape=[jax.ShapeDtypeStruct(*s) for s in shapes],
        in_specs=[vmem_spec()] * 8,
        out_specs=[vmem_spec()] * 5,
        scratch_shapes=[pltpu.VMEM((3, TOKENS, SIDE * LEN), BF16)],
        compiler_params=pltpu.CompilerParams(vmem_limit_bytes=VMEM_LIMIT),
        cost_estimate=pl.CostEstimate(
            flops=3 * TOKENS * D * F1 // 2, bytes_accessed=20_000_000, transcendentals=0
        ),
        name="near_front",
    )(inputs, w_second, *pieces[0][:3], *pieces[1][:3])


def front_kernel(normed, pre, wm_ref, *refs):
    fars, refs = (refs[0:2], refs[2:4]), refs[5:]
    slope, act, attn, turn, xhat, gated, rstd_mid, w_in_t = refs[:8]
    mixed, left, flipped, sems = refs[8:]
    y, z = here()
    copies = []
    for half in range(2):
        left[...] = chosen(normed, half, 2)
        for c in range(HALF_IN // 512):
            cols = slice(512 * c, 512 * (c + 1))
            into = slice(HALF_IN * half + 512 * c, HALF_IN * half + 512 * (c + 1))
            total = pre[:, into]
            for n in range(2):
                right = fars[half][n][:, :, cols].reshape(2 * LEN, 512)
                total += jnp.dot(
                    left[:, 256 * n : 256 * (n + 1)], right, preferred_element_type=F32
                )
            squash = jax.nn.sigmoid(total)
            act[:, into] = (total * squash).astype(BF16)
            slope[:, into] = (squash * (1.0 + total * (1.0 - squash))).astype(BF16)
        for at, (j, k) in enumerate(cells(half, 2)):
            block = fars[half][at // 2]
            for c in range(HALF_IN // 512):
                flipped[half, at, 512 * c : 512 * (c + 1), :] = block[
                    at % 2, :, 512 * c : 512 * (c + 1)
                ].T
            col = block_row(y, z, -j, -k, LEN)
            spot = w_in_t.at[pl.ds(HALF_IN * half, HALF_IN), pl.ds(col, LEN)]
            copies.append(pltpu.make_async_copy(flipped.at[half, at], spot, sems.at[half, at]))
            copies[-1].start()

    quarter, half = lane_group(QK_DIM), lane_group(V_DIM)

    @pl.loop(0, TOKENS // LEN)
    def _(m):
        rows = pl.ds(pl.multiple_of(m * LEN, LEN), LEN)
        mask = wm_ref[m]
        for h4 in range(4):
            q4 = act[rows, QCOL + LEN * h4 : QCOL + LEN * (h4 + 1)]
            k4 = act[rows, KCOL + LEN * h4 : KCOL + LEN * (h4 + 1)]
            for pair in range(2):
                tile = 2 * h4 + pair
                v2 = act[rows, HV + LEN * tile : HV + LEN * (tile + 1)]
                total = jnp.zeros((LEN, LEN), F32)
                for e in range(2):
                    h = 2 * tile + e
                    score = mm(keep(quarter == 2 * pair + e, q4), k4, NT) * SCALE
                    squash = jax.nn.sigmoid(score)
                    weight = (score * squash * mask).astype(BF16)
                    attn[m, h] = weight
                    turn[m, h] = (
                        squash * (1.0 + score * (1.0 - squash)) * mask * SCALE
                    ).astype(BF16)
                    total += jnp.dot(weight, keep(half == e, v2), preferred_element_type=F32)
                mixed[:, LEN * tile : LEN * (tile + 1)] = total
        values = mixed[...]
        center = values - jnp.mean(values, axis=-1, keepdims=True)
        rstd = lax.rsqrt(jnp.mean(center * center, axis=-1, keepdims=True) + EPSILON)
        hat = center * rstd
        xhat[rows, :] = hat
        rstd_mid[rows, :] = jnp.broadcast_to(rstd, (LEN, LEN))
        gated[rows, :] = (hat * act[rows, :HV].astype(F32)).astype(BF16)

    for copy in copies:
        copy.wait()


def front(inputs, masks, w_second, pieces):
    normed, pre, w_in_t, w_out_t, rstd_in = near_front(inputs, w_second, pieces)
    shapes = [
        ((TOKENS, F1), BF16),
        ((TOKENS, F1), BF16),
        ((2, HEADS, LEN, LEN), BF16),
        ((2, HEADS, LEN, LEN), BF16),
        ((TOKENS, HV), F32),
        ((TOKENS, HV), BF16),
        ((TOKENS, LEN), F32),
        ((F1, D), BF16),
    ]
    slope, act, attn, turn, xhat, gated, rstd_mid, w_in_t = pl.pallas_call(
        front_kernel,
        out_shape=[jax.ShapeDtypeStruct(*s) for s in shapes],
        in_specs=[vmem_spec()] * 7 + [any_spec()],
        out_specs=[vmem_spec()] * 7 + [any_spec()],
        input_output_aliases={7: 7},
        scratch_shapes=[
            pltpu.VMEM((LEN, HV), F32),
            pltpu.VMEM((TOKENS, SIDE * LEN), BF16),
            pltpu.VMEM((2, SIDE, HALF_IN, LEN), BF16),
            pltpu.SemaphoreType.DMA((2, SIDE)),
        ],
        compiler_params=pltpu.CompilerParams(vmem_limit_bytes=VMEM_LIMIT),
        cost_estimate=pl.CostEstimate(
            flops=TOKENS * D * F1 // 2, bytes_accessed=30_000_000, transcendentals=1_500_000
        ),
        name="front",
    )(normed, pre, masks, *pieces[0][3:], *pieces[1][3:], w_in_t)
    saved = (normed, slope, act, attn, turn, xhat, rstd_in, rstd_mid)
    return saved, gated, w_in_t, w_out_t


def flip_kernel(normed, gated, normed_t, gated_t):
    for c in range(D // LEN):
        normed_t[LEN * c : LEN * (c + 1), :] = normed[:, LEN * c : LEN * (c + 1)].T
    for c in range(HV // LEN):
        gated_t[LEN * c : LEN * (c + 1), :] = gated[:, LEN * c : LEN * (c + 1)].T


def flip(normed, gated):
    return pl.pallas_call(
        flip_kernel,
        out_shape=[
            jax.ShapeDtypeStruct((D, TOKENS), BF16),
            jax.ShapeDtypeStruct((HV, TOKENS), BF16),
        ],
        in_specs=[vmem_spec()] * 2,
        out_specs=[vmem_spec()] * 2,
        compiler_params=pltpu.CompilerParams(vmem_limit_bytes=VMEM_LIMIT),
        cost_estimate=pl.CostEstimate(flops=0, bytes_accessed=6_000_000, transcendentals=0),
        name="flip",
    )(normed, gated)


def chain_body(n_sources, n_carried, slot, source, *refs):
    sources, refs = refs[:n_sources], refs[n_sources:]
    w_in_t, w_out_t, normed, slope, act, attn, turn, xhat, rstd_in, rstd_mid = refs[:10]
    outgoing, ups_out, gp_out, grads_out, ups, gp, big, sems = refs[10 + n_carried :]
    slot, source = jnp.int32(slot), jnp.int32(source)
    rows = pl.ds(pl.multiple_of(slot * LEN, LEN), LEN)
    for i, ref in enumerate(sources):

        @pl.when(source == i)
        def _():
            ups[...] = ref[rows, :] if i == 0 else ref[...]

    put_ups = pltpu.make_async_copy(ups, ups_out.at[rows, :], sems.at[0])
    put_ups.start()

    for c in range(HV // 256):
        big[:, 256 * c : 256 * (c + 1)] = jnp.dot(
            ups[...], w_out_t[:, 256 * c : 256 * (c + 1)], preferred_element_type=F32
        )
    sums = [jnp.zeros((LEN, LEN), F32)] * 2
    for c in range(HV // LEN):
        cols = slice(LEN * c, LEN * (c + 1))
        hat = xhat[rows, cols]
        moved = big[:, cols] * act[rows, cols].astype(F32)
        sums = [sums[0] + moved, sums[1] + moved * hat]
        gp[:, cols] = (
            (big[:, cols] * hat).astype(BF16).astype(F32) * slope[rows, cols].astype(F32)
        ).astype(BF16)
        big[:, HV + LEN * c : HV + LEN * (c + 1)] = moved
    mean_one = jnp.sum(sums[0], axis=-1, keepdims=True) / HV
    mean_hat = jnp.sum(sums[1], axis=-1, keepdims=True) / HV
    rstd = rstd_mid[rows, :]

    quarter, half = lane_group(QK_DIM), lane_group(V_DIM)

    def put(value, col):
        cols = slice(col, col + LEN)
        gp[:, cols] = (
            value.astype(BF16).astype(F32) * slope[rows, cols].astype(F32)
        ).astype(BF16)

    for h4 in range(4):
        q4 = act[rows, QCOL + LEN * h4 : QCOL + LEN * (h4 + 1)]
        k4 = act[rows, KCOL + LEN * h4 : KCOL + LEN * (h4 + 1)]
        grad_q = jnp.zeros((LEN, LEN), F32)
        grad_k = jnp.zeros((LEN, LEN), F32)
        for pair in range(2):
            tile = 2 * h4 + pair
            v2 = act[rows, HV + LEN * tile : HV + LEN * (tile + 1)]
            moved = big[:, HV + LEN * tile : HV + LEN * (tile + 1)]
            hat = xhat[rows, LEN * tile : LEN * (tile + 1)]
            g2 = (rstd * (moved - mean_one - hat * mean_hat)).astype(BF16)
            grad_v = jnp.zeros((LEN, LEN), F32)
            for e in range(2):
                h = 2 * tile + e
                gh = keep(half == e, g2)
                grad_s = (mm(gh, v2, NT) * turn[slot, h].astype(F32)).astype(BF16)
                grad_v += mm(attn[slot, h], gh, TN)
                own = quarter == 2 * pair + e
                grad_q += jnp.dot(grad_s, keep(own, k4), preferred_element_type=F32)
                grad_k += mm(grad_s, keep(own, q4), TN)
            put(grad_v, HV + LEN * tile)
        put(grad_q, QCOL + LEN * h4)
        put(grad_k, KCOL + LEN * h4)

    put_gp = pltpu.make_async_copy(gp, gp_out.at[rows, :], sems.at[1])
    put_gp.start()
    sums = [jnp.zeros((LEN, LEN), F32)] * 2
    for c in range(D // 256):
        big[:, 256 * c : 256 * (c + 1)] = jnp.dot(
            gp[...], w_in_t[:, 256 * c : 256 * (c + 1)], preferred_element_type=F32
        )
        for cols in (slice(256 * c, 256 * c + LEN), slice(256 * c + LEN, 256 * (c + 1))):
            grad = big[:, cols]
            sums = [sums[0] + grad, sums[1] + grad * normed[rows, cols].astype(F32)]
    one = jnp.sum(sums[0], axis=-1, keepdims=True) / D
    two = jnp.sum(sums[1], axis=-1, keepdims=True) / D
    rstd = rstd_in[rows, :]
    for c in range(D // LEN):
        cols = slice(LEN * c, LEN * (c + 1))
        moved = rstd * (big[:, cols] - one - normed[rows, cols].astype(F32) * two)
        outgoing[:, cols] = (ups[:, cols].astype(F32) + moved).astype(BF16)
    put_grads = pltpu.make_async_copy(outgoing, grads_out.at[rows, :], sems.at[2])
    put_grads.start()
    put_ups.wait()
    put_gp.wait()
    put_grads.wait()


def chain_step(work, sources, w_in_t, w_out_t, saved, carried):
    kept = [((TOKENS, D), BF16), ((TOKENS, F1), BF16), ((TOKENS, D), BF16)]
    shapes = [((LEN, D), BF16)] + kept
    operands = [*sources, w_in_t, w_out_t, *saved, *carried]
    before = len(operands) - len(carried)
    aliases = {before + i: 1 + i for i in range(len(carried))}

    def kernel(*refs):
        section = lax.axis_index("pipe")
        if len(work) == 1:
            ((one, mine),) = work.items()
            busy = section == one
        else:
            (one, (slot, source)), (two, (slot_two, source_two)) = work.items()
            busy = jnp.logical_or(section == one, section == two)
            mine = (
                jnp.where(section == one, slot, slot_two),
                jnp.where(section == one, source, source_two),
            )

        @pl.when(busy)
        def _():
            chain_body(len(sources), len(carried), *mine, *refs)

    return pl.pallas_call(
        kernel,
        out_shape=[jax.ShapeDtypeStruct(*s) for s in shapes],
        in_specs=[vmem_spec()] * before + [any_spec()] * len(carried),
        out_specs=[vmem_spec()] + [any_spec()] * 3,
        input_output_aliases=aliases,
        scratch_shapes=[
            pltpu.VMEM((LEN, D), BF16),
            pltpu.VMEM((LEN, F1), BF16),
            pltpu.VMEM((LEN, D), F32),
            pltpu.SemaphoreType.DMA((3,)),
        ],
        compiler_params=pltpu.CompilerParams(vmem_limit_bytes=VMEM_LIMIT),
        cost_estimate=pl.CostEstimate(
            flops=2 * LEN * D * (F1 + HV), bytes_accessed=22_000_000, transcendentals=0
        ),
        name="chain",
    )(*operands)


def weights_kernel(jobs, normed_t, gated_t, ups, gp, *refs):
    outs, (rows_in, rows_out, buf, sems) = refs[: len(jobs)], refs[len(jobs) :]
    y, z = here()
    pending = [None, None]
    for count, (out, (half, blocks)) in enumerate(zip(outs, jobs)):
        turn, size = count % 2, len(blocks)
        for at, (dy, dz) in enumerate(blocks):
            row = block_row(y, z, dy, dz, LEN)
            rows_in[LEN * at : LEN * (at + 1), :] = normed_t[pl.ds(row, LEN), :]
            row = block_row(y, z, dy, dz, V_DIM)
            rows_out[V_DIM * at : V_DIM * (at + 1), :] = gated_t[pl.ds(row, V_DIM), :]
        if pending[turn] is not None:
            pending[turn].wait()
        for c in range(HALF_IN // 512):
            right = gp[:, HALF_IN * half + 512 * c : HALF_IN * half + 512 * (c + 1)]
            found = jnp.dot(rows_in[: LEN * size, :], right, preferred_element_type=F32)
            for at in range(size):
                buf[turn, at, :, 512 * c : 512 * (c + 1)] = found[
                    LEN * at : LEN * (at + 1), :
                ].astype(BF16)
        for fold in range(2):
            right = ups[:, HALF_OUT * half + FOLD * fold : HALF_OUT * half + FOLD * (fold + 1)]
            found = jnp.dot(rows_out[: V_DIM * size, :], right, preferred_element_type=F32)
            for at in range(size):
                buf[turn, at, V_DIM * fold : V_DIM * (fold + 1), HALF_IN:] = found[
                    V_DIM * at : V_DIM * (at + 1), :
                ].astype(BF16)
        pending[turn] = pltpu.make_async_copy(buf.at[turn, pl.ds(0, size)], out, sems.at[turn])
        pending[turn].start()
    for copy in pending:
        copy.wait()


def weight_parts(name, jobs, normed_t, gated_t, ups, gp):
    blocks = sum(len(job[1]) for job in jobs)
    return pl.pallas_call(
        lambda *refs: weights_kernel(jobs, *refs),
        out_shape=[jax.ShapeDtypeStruct((len(job[1]), LEN, PACK), BF16) for job in jobs],
        in_specs=[vmem_spec()] * 4,
        out_specs=[any_spec()] * len(jobs),
        scratch_shapes=[
            pltpu.VMEM((SIDE * LEN, TOKENS), BF16),
            pltpu.VMEM((SIDE * V_DIM, TOKENS), BF16),
            pltpu.VMEM((2, SIDE, LEN, PACK), BF16),
            pltpu.SemaphoreType.DMA((2,)),
        ],
        compiler_params=pltpu.CompilerParams(vmem_limit_bytes=VMEM_LIMIT),
        cost_estimate=pl.CostEstimate(
            flops=2 * TOKENS * LEN * PACK * blocks,
            bytes_accessed=4_000_000 + 2 * LEN * PACK * blocks,
            transcendentals=0,
        ),
        name=name,
    )(normed_t, gated_t, ups, gp)


FAR_JOBS = (
    (0, ((0, 2), (1, 2))),
    (0, ((2, 2), (3, 2))),
    (1, ((2, 0), (2, 1))),
    (1, ((2, 2), (2, 3))),
)
NEAR_JOBS = (
    (0, ((0, 1), (1, 1))),
    (0, ((2, 1), (3, 1))),
    (0, ((0, 3), (1, 3))),
    (0, ((2, 3), (3, 3))),
    (1, ((1, 0), (1, 1))),
    (1, ((1, 2), (1, 3))),
    (1, ((3, 0), (3, 1))),
    (1, ((3, 2), (3, 3))),
    (0, ((0, 0), (1, 0), (2, 0), (3, 0))),
    (1, ((0, 0), (0, 1), (0, 2), (0, 3))),
)


def along(axis, by):
    return (by, 0, 0) if axis == "y" else (0, by, 0)


def spread(block, axis):
    half = block.shape[0] // 2
    plus = send(block, *along(axis, 1))
    minus = send(block, *along(axis, -1))
    far_low = send(plus[:half], *along(axis, 1))
    far_high = send(minus[half:], *along(axis, -1))
    return plus, minus, far_low, far_high


def lined(block, axis):
    plus, minus, far_low, far_high = spread(block, axis)
    return jnp.stack([block, plus, jnp.concatenate([far_low, far_high], 0), minus])


def gathered(shard, x):
    other = send(shard, 0, 0, 1)
    low = jnp.where(x == 0, shard, other)
    high = jnp.where(x == 0, other, shard)
    pieces = []
    for half in range(2):
        cols = slice(HALF_IN * half, HALF_IN * (half + 1))
        line = lined(jnp.concatenate([low[:, cols], high[:, cols]], 0), "yz"[half])
        pieces.append((line, *spread(line, "zy"[half])))
    return pieces


def added(*arrays):
    total = arrays[0].astype(F32)
    for array in arrays[1:]:
        total = total + array.astype(F32)
    return total


def joined(own, plus_low, plus_high, minus_low, minus_high, far_low, far_high, axis):
    through = send(far_low, *along(axis, 1))
    back = send(far_high, *along(axis, -1))
    plus = jnp.concatenate([added(plus_low, through).astype(BF16), plus_high], 0)
    minus = jnp.concatenate([minus_low, added(minus_high, back).astype(BF16)], 0)
    return added(own, send(plus, *along(axis, 1)), send(minus, *along(axis, -1)))


def scattered(far, near, x):
    a_one = joined(near[8], *near[0:4], far[0], far[1], "z").astype(BF16)
    b_one = joined(near[9], *near[4:8], far[2], far[3], "y").astype(BF16)
    ends = []
    for line, axis in ((a_one, "y"), (b_one, "z")):
        cut = [part for block in (1, 3, 2) for part in (line[block, :V_DIM], line[block, V_DIM:])]
        ends.append(joined(line[0], *cut, axis))
    first = jnp.concatenate([end[:, :HALF_IN] for end in ends], 1)
    folded = jnp.concatenate([end[:, HALF_IN:] for end in ends], 1)
    outs = [folded[:V_DIM, :FOLD], folded[V_DIM:, :FOLD], folded[:V_DIM, FOLD:], folded[V_DIM:, FOLD:]]
    second = jnp.concatenate(outs, 1)
    sides = []
    for side in range(2):
        mine = second[32 * side : 32 * (side + 1)]
        tall = jnp.concatenate([mine[:, :HALF_OUT], mine[:, HALF_OUT:]], 0)
        sides.append(jnp.concatenate([first[64 * side : 64 * (side + 1)], tall], 1))
    away = jnp.where(x == 0, sides[1], sides[0]).astype(BF16)
    total = jnp.where(x == 0, sides[0], sides[1]) + send(away, 0, 0, 1).astype(F32)
    grad_out = jnp.concatenate([total[:32, F1:], total[32:, F1:]], 1)
    return total[:, :F1], grad_out


def body(section_input, top_grad, w_in, w_out, segments):
    x = lax.axis_index("dp") % 2
    w_second = lax.all_gather(w_out[0], "dp", axis=0, tiled=True)
    pieces = gathered(w_in[0], x)

    same = segments[:, :, None] == segments[:, None, :]
    lower = lax.broadcasted_iota(jnp.int32, (LEN, LEN), 1) <= lax.broadcasted_iota(
        jnp.int32, (LEN, LEN), 0
    )
    counts = jnp.sum(same.astype(F32), axis=2, keepdims=True)
    masks = jnp.where(jnp.logical_and(same, lower[None]), 1.0 / counts, 0.0)

    saved, gated, w_first, w_second = front(section_input[0], masks, w_second, pieces)

    def step(work, sources, carried):
        outgoing, *carried = chain_step(
            work, (top_grad, *sources), w_first, w_second, saved, tuple(carried)
        )
        return outgoing, carried

    def below(array, which):
        return lax.ppermute(array, "pipe", [(which, which - 1)])

    out_0, carried = step({3: (0, 0)}, (), ())
    out_1, carried = step({3: (1, 0), 2: (0, 1)}, (below(out_0, 3),), carried)
    to_one = below(out_1, 2)
    out_2, carried = step({2: (1, 1)}, (below(out_1, 3),), carried)
    again = below(out_2, 2)
    out_3, carried = step({1: (0, 1)}, (to_one,), carried)
    out_4, carried = step({1: (1, 1), 0: (0, 2)}, (again, below(out_3, 1)), carried)
    _, carried = step({0: (1, 1)}, (below(out_4, 1),), carried)
    ups, gp, grads = carried

    normed_t, gated_t = flip(saved[0], gated)
    far = weight_parts("far_parts", FAR_JOBS, normed_t, gated_t, ups, gp)
    near = weight_parts("near_parts", NEAR_JOBS, normed_t, gated_t, ups, gp)
    grad_first, grad_out = scattered(far, near, x)
    return (grads[None], grad_first[None], grad_out[None])


def solution(mesh):
    return jax.shard_map(
        body,
        mesh=mesh,
        in_specs=(
            P("pipe", "dp", None),
            P("dp", None),
            P("pipe", "dp", None),
            P("pipe", "dp", None),
            P("dp", None),
        ),
        out_specs=(P("pipe", "dp", None), P("pipe", "dp", None), P("pipe", "dp", None)),
        check_vma=False,
    )
```

```python
import jax
import jax.numpy as jnp
from jax import lax
from jax.experimental import pallas as pl
from jax.experimental.pallas import tpu as pltpu
from jax.sharding import PartitionSpec as P

HEADS = 16
QK_DIM = 32
V_DIM = 64
EPSILON = 1e-05
D = 2048
HV = 1024
F1 = 3072
QCOL = 2 * HV
KCOL = QCOL + HEADS * QK_DIM
LEN = 128
TOKENS = 256
SIDE = 4
HALF_IN = F1 // 2
HALF_OUT = D // 2
FOLD = HALF_OUT // 2
PACK = HALF_IN + FOLD
SCALE = QK_DIM ** (-0.5)
VMEM_LIMIT = 10 * 1024 * 1024
BF16 = jnp.bfloat16
F32 = jnp.float32

NT = (((1,), (1,)), ((), ()))
TN = (((0,), (0,)), ((), ()))


def mm(left, right, dims):
    return lax.dot_general(left, right, dims, preferred_element_type=F32)


def shifted(dy, dz, dx):
    pairs = []
    for i in range(32):
        y, z, x = i // 8, (i // 2) % 4, i % 2
        pairs.append((i, ((y + dy) % 4 * 4 + (z + dz) % 4) * 2 + (x + dx) % 2))
    return pairs


def send(array, dy, dz, dx):
    return lax.ppermute(array, "dp", shifted(dy, dz, dx))


def any_spec():
    return pl.BlockSpec(memory_space=pl.ANY)


def vmem_spec():
    return pl.BlockSpec(memory_space=pltpu.VMEM)


def block_row(y, z, dy, dz, rows):
    cell = lax.rem(y + dy + SIDE, SIDE) * SIDE + lax.rem(z + dz + SIDE, SIDE)
    return pl.multiple_of(cell * rows, rows)


def here():
    spot = lax.axis_index("dp")
    return lax.shift_right_logical(spot, 3), lax.bitwise_and(lax.shift_right_logical(spot, 1), 3)


def lane_group(width):
    return lax.broadcasted_iota(jnp.int32, (LEN, LEN), 1) // width


def keep(mask, tile):
    return jnp.where(mask, tile, jnp.zeros_like(tile))


def cells(half, across):
    return [(i, across) if half == 0 else (across, i) for i in range(SIDE)]


def chosen(normed, half, across):
    y, z = here()
    cols = [block_row(y, z, -j, -k, LEN) for j, k in cells(half, across)]
    return jnp.concatenate([normed[:, pl.ds(col, LEN)] for col in cols], axis=1)


def near_front_kernel(x_ref, *refs):
    pieces, (normed, pre, w_in_t, w_out, rstd_in, left) = refs[:6], refs[6:]
    y, z = here()

    @pl.loop(0, TOKENS // 32)
    def _(step):
        rows = pl.ds(pl.multiple_of(step * 32, 32), 32)
        values = x_ref[rows, :].astype(F32)
        center = values - jnp.mean(values, axis=-1, keepdims=True)
        rstd = lax.rsqrt(jnp.mean(center * center, axis=-1, keepdims=True) + EPSILON)
        normed[rows, :] = (center * rstd).astype(BF16)
        rstd_in[rows, :] = jnp.broadcast_to(rstd, (32, LEN))

    for half in range(2):
        trio = [(pieces[3 * half + n], n, across) for n, across in enumerate((0, 1, 3))]
        for _, n, across in trio:
            left[n] = chosen(normed, half, across)
        for c in range(HALF_IN // 512):
            cols = slice(512 * c, 512 * (c + 1))
            total = jnp.zeros((TOKENS, 512), F32)
            for piece, n, _ in trio:
                right = piece[:, :, cols].reshape(SIDE * LEN, 512)
                total += jnp.dot(left[n], right, preferred_element_type=F32)
            pre[:, HALF_IN * half + 512 * c : HALF_IN * half + 512 * (c + 1)] = total
        for piece, _, across in trio:
            for at, (j, k) in enumerate(cells(half, across)):
                col = block_row(y, z, -j, -k, LEN)
                row = block_row(y, z, -j, -k, V_DIM)
                for c in range(HALF_IN // 512):
                    rows = slice(HALF_IN * half + 512 * c, HALF_IN * half + 512 * (c + 1))
                    w_in_t[rows, pl.ds(col, LEN)] = piece[at, :, 512 * c : 512 * (c + 1)].T
                for fold in range(2):
                    first = HALF_OUT * half + FOLD * fold
                    w_out[pl.ds(row, V_DIM), first : first + FOLD] = piece[
                        at, V_DIM * fold : V_DIM * (fold + 1), HALF_IN:
                    ]


def near_front(inputs, pieces):
    shapes = [
        ((TOKENS, D), BF16),
        ((TOKENS, F1), F32),
        ((F1, D), BF16),
        ((HV, D), BF16),
        ((TOKENS, LEN), F32),
    ]
    return pl.pallas_call(
        near_front_kernel,
        out_shape=[jax.ShapeDtypeStruct(*s) for s in shapes],
        in_specs=[vmem_spec()] * 7,
        out_specs=[vmem_spec()] * 5,
        scratch_shapes=[pltpu.VMEM((3, TOKENS, SIDE * LEN), BF16)],
        compiler_params=pltpu.CompilerParams(vmem_limit_bytes=VMEM_LIMIT),
        cost_estimate=pl.CostEstimate(
            flops=3 * TOKENS * D * F1 // 2, bytes_accessed=20_000_000, transcendentals=0
        ),
        name="near_front",
    )(inputs, *pieces[0][:3], *pieces[1][:3])


def front_kernel(normed, pre, wm_ref, *refs):
    fars, refs = (refs[0:2], refs[2:4]), refs[6:]
    slope, act, attn, turn, xhat, gated, rstd_mid, w_in_t, w_out = refs[:9]
    mixed, left, flipped, sems, sems_out = refs[9:]
    y, z = here()
    copies = []
    for half in range(2):
        left[...] = chosen(normed, half, 2)
        for at, (j, k) in enumerate(cells(half, 2)):
            block = fars[half][at // 2].at[at % 2]
            row = block_row(y, z, -j, -k, V_DIM)
            for fold in range(2):
                spot = w_out.at[pl.ds(row, V_DIM), pl.ds(HALF_OUT * half + FOLD * fold, FOLD)]
                part = block.at[pl.ds(V_DIM * fold, V_DIM), pl.ds(HALF_IN, FOLD)]
                copies.append(pltpu.make_async_copy(part, spot, sems_out.at[half, at, fold]))
                copies[-1].start()
        for c in range(HALF_IN // 512):
            cols = slice(512 * c, 512 * (c + 1))
            into = slice(HALF_IN * half + 512 * c, HALF_IN * half + 512 * (c + 1))
            total = pre[:, into]
            for n in range(2):
                right = fars[half][n][:, :, cols].reshape(2 * LEN, 512)
                total += jnp.dot(
                    left[:, 256 * n : 256 * (n + 1)], right, preferred_element_type=F32
                )
            squash = jax.nn.sigmoid(total)
            act[:, into] = (total * squash).astype(BF16)
            slope[:, into] = (squash * (1.0 + total * (1.0 - squash))).astype(BF16)
        for at, (j, k) in enumerate(cells(half, 2)):
            block = fars[half][at // 2]
            for c in range(HALF_IN // 512):
                flipped[half, at, 512 * c : 512 * (c + 1), :] = block[
                    at % 2, :, 512 * c : 512 * (c + 1)
                ].T
            col = block_row(y, z, -j, -k, LEN)
            spot = w_in_t.at[pl.ds(HALF_IN * half, HALF_IN), pl.ds(col, LEN)]
            copies.append(pltpu.make_async_copy(flipped.at[half, at], spot, sems.at[half, at]))
            copies[-1].start()

    quarter, half = lane_group(QK_DIM), lane_group(V_DIM)

    @pl.loop(0, TOKENS // LEN)
    def _(m):
        rows = pl.ds(pl.multiple_of(m * LEN, LEN), LEN)
        mask = wm_ref[m]
        for h4 in range(4):
            q4 = act[rows, QCOL + LEN * h4 : QCOL + LEN * (h4 + 1)]
            k4 = act[rows, KCOL + LEN * h4 : KCOL + LEN * (h4 + 1)]
            for pair in range(2):
                tile = 2 * h4 + pair
                v2 = act[rows, HV + LEN * tile : HV + LEN * (tile + 1)]
                total = jnp.zeros((LEN, LEN), F32)
                for e in range(2):
                    h = 2 * tile + e
                    score = mm(keep(quarter == 2 * pair + e, q4), k4, NT) * SCALE
                    squash = jax.nn.sigmoid(score)
                    weight = (score * squash * mask).astype(BF16)
                    attn[m, h] = weight
                    turn[m, h] = (
                        squash * (1.0 + score * (1.0 - squash)) * mask * SCALE
                    ).astype(BF16)
                    total += jnp.dot(weight, keep(half == e, v2), preferred_element_type=F32)
                mixed[:, LEN * tile : LEN * (tile + 1)] = total
        values = mixed[...]
        center = values - jnp.mean(values, axis=-1, keepdims=True)
        rstd = lax.rsqrt(jnp.mean(center * center, axis=-1, keepdims=True) + EPSILON)
        hat = center * rstd
        xhat[rows, :] = hat
        rstd_mid[rows, :] = jnp.broadcast_to(rstd, (LEN, LEN))
        gated[rows, :] = (hat * act[rows, :HV].astype(F32)).astype(BF16)

    for copy in copies:
        copy.wait()


def front(inputs, masks, pieces):
    normed, pre, w_in_t, w_out, rstd_in = near_front(inputs, pieces)
    shapes = [
        ((TOKENS, F1), BF16),
        ((TOKENS, F1), BF16),
        ((2, HEADS, LEN, LEN), BF16),
        ((2, HEADS, LEN, LEN), BF16),
        ((TOKENS, HV), F32),
        ((TOKENS, HV), BF16),
        ((TOKENS, LEN), F32),
        ((F1, D), BF16),
        ((HV, D), BF16),
    ]
    slope, act, attn, turn, xhat, gated, rstd_mid, w_in_t, w_out = pl.pallas_call(
        front_kernel,
        out_shape=[jax.ShapeDtypeStruct(*s) for s in shapes],
        in_specs=[vmem_spec()] * 7 + [any_spec()] * 2,
        out_specs=[vmem_spec()] * 7 + [any_spec()] * 2,
        input_output_aliases={7: 7, 8: 8},
        scratch_shapes=[
            pltpu.VMEM((LEN, HV), F32),
            pltpu.VMEM((TOKENS, SIDE * LEN), BF16),
            pltpu.VMEM((2, SIDE, HALF_IN, LEN), BF16),
            pltpu.SemaphoreType.DMA((2, SIDE)),
            pltpu.SemaphoreType.DMA((2, SIDE, 2)),
        ],
        compiler_params=pltpu.CompilerParams(vmem_limit_bytes=VMEM_LIMIT),
        cost_estimate=pl.CostEstimate(
            flops=TOKENS * D * F1 // 2, bytes_accessed=30_000_000, transcendentals=1_500_000
        ),
        name="front",
    )(normed, pre, masks, *pieces[0][3:], *pieces[1][3:], w_in_t, w_out)
    saved = (normed, slope, act, attn, turn, xhat, rstd_in, rstd_mid)
    return saved, gated, w_in_t, w_out


def flip_kernel(normed, gated, normed_t, gated_t):
    for c in range(D // LEN):
        normed_t[LEN * c : LEN * (c + 1), :] = normed[:, LEN * c : LEN * (c + 1)].T
    for c in range(HV // LEN):
        gated_t[LEN * c : LEN * (c + 1), :] = gated[:, LEN * c : LEN * (c + 1)].T


def flip_second_kernel(w_out, _, w_out_t):
    for r in range(HV // LEN):
        for c in range(D // 512):
            w_out_t[512 * c : 512 * (c + 1), LEN * r : LEN * (r + 1)] = w_out[
                LEN * r : LEN * (r + 1), 512 * c : 512 * (c + 1)
            ].T


def flip_second(w_out, after):
    return pl.pallas_call(
        flip_second_kernel,
        out_shape=jax.ShapeDtypeStruct((D, HV), BF16),
        in_specs=[vmem_spec(), any_spec()],
        out_specs=vmem_spec(),
        compiler_params=pltpu.CompilerParams(vmem_limit_bytes=VMEM_LIMIT),
        cost_estimate=pl.CostEstimate(flops=0, bytes_accessed=8_000_000, transcendentals=0),
        name="flip_second",
    )(w_out, after)


def flip(normed, gated):
    return pl.pallas_call(
        flip_kernel,
        out_shape=[
            jax.ShapeDtypeStruct((D, TOKENS), BF16),
            jax.ShapeDtypeStruct((HV, TOKENS), BF16),
        ],
        in_specs=[vmem_spec()] * 2,
        out_specs=[vmem_spec()] * 2,
        compiler_params=pltpu.CompilerParams(vmem_limit_bytes=VMEM_LIMIT),
        cost_estimate=pl.CostEstimate(flops=0, bytes_accessed=6_000_000, transcendentals=0),
        name="flip",
    )(normed, gated)


def chain_body(n_sources, n_carried, slot, source, *refs):
    sources, refs = refs[:n_sources], refs[n_sources:]
    w_in_t, w_out, normed, slope, act, attn, turn, xhat, rstd_in, rstd_mid = refs[:10]
    outgoing, ups_out, gp_out, grads_out, ups, gp, big, sems = refs[10 + n_carried :]
    slot, source = jnp.int32(slot), jnp.int32(source)
    rows = pl.ds(pl.multiple_of(slot * LEN, LEN), LEN)
    for i, ref in enumerate(sources):

        @pl.when(source == i)
        def _():
            ups[...] = ref[rows, :] if i == 0 else ref[...]

    put_ups = pltpu.make_async_copy(ups, ups_out.at[rows, :], sems.at[0])
    put_ups.start()

    for c in range(HV // 256):
        cols = slice(256 * c, 256 * (c + 1))
        if w_out.shape[0] == HV:
            big[:, cols] = mm(ups[...], w_out[cols, :], NT)
        else:
            big[:, cols] = jnp.dot(ups[...], w_out[:, cols], preferred_element_type=F32)
    sums = [jnp.zeros((LEN, LEN), F32)] * 2
    for c in range(HV // LEN):
        cols = slice(LEN * c, LEN * (c + 1))
        hat = xhat[rows, cols]
        moved = big[:, cols] * act[rows, cols].astype(F32)
        sums = [sums[0] + moved, sums[1] + moved * hat]
        gp[:, cols] = (
            (big[:, cols] * hat).astype(BF16).astype(F32) * slope[rows, cols].astype(F32)
        ).astype(BF16)
        big[:, HV + LEN * c : HV + LEN * (c + 1)] = moved
    mean_one = jnp.sum(sums[0], axis=-1, keepdims=True) / HV
    mean_hat = jnp.sum(sums[1], axis=-1, keepdims=True) / HV
    rstd = rstd_mid[rows, :]

    quarter, half = lane_group(QK_DIM), lane_group(V_DIM)

    def put(value, col):
        cols = slice(col, col + LEN)
        gp[:, cols] = (
            value.astype(BF16).astype(F32) * slope[rows, cols].astype(F32)
        ).astype(BF16)

    for h4 in range(4):
        q4 = act[rows, QCOL + LEN * h4 : QCOL + LEN * (h4 + 1)]
        k4 = act[rows, KCOL + LEN * h4 : KCOL + LEN * (h4 + 1)]
        grad_q = jnp.zeros((LEN, LEN), F32)
        grad_k = jnp.zeros((LEN, LEN), F32)
        for pair in range(2):
            tile = 2 * h4 + pair
            v2 = act[rows, HV + LEN * tile : HV + LEN * (tile + 1)]
            moved = big[:, HV + LEN * tile : HV + LEN * (tile + 1)]
            hat = xhat[rows, LEN * tile : LEN * (tile + 1)]
            g2 = (rstd * (moved - mean_one - hat * mean_hat)).astype(BF16)
            grad_v = jnp.zeros((LEN, LEN), F32)
            for e in range(2):
                h = 2 * tile + e
                gh = keep(half == e, g2)
                grad_s = (mm(gh, v2, NT) * turn[slot, h].astype(F32)).astype(BF16)
                grad_v += mm(attn[slot, h], gh, TN)
                own = quarter == 2 * pair + e
                grad_q += jnp.dot(grad_s, keep(own, k4), preferred_element_type=F32)
                grad_k += mm(grad_s, keep(own, q4), TN)
            put(grad_v, HV + LEN * tile)
        put(grad_q, QCOL + LEN * h4)
        put(grad_k, KCOL + LEN * h4)

    put_gp = pltpu.make_async_copy(gp, gp_out.at[rows, :], sems.at[1])
    put_gp.start()
    sums = [jnp.zeros((LEN, LEN), F32)] * 2
    for c in range(D // 256):
        big[:, 256 * c : 256 * (c + 1)] = jnp.dot(
            gp[...], w_in_t[:, 256 * c : 256 * (c + 1)], preferred_element_type=F32
        )
        for cols in (slice(256 * c, 256 * c + LEN), slice(256 * c + LEN, 256 * (c + 1))):
            grad = big[:, cols]
            sums = [sums[0] + grad, sums[1] + grad * normed[rows, cols].astype(F32)]
    one = jnp.sum(sums[0], axis=-1, keepdims=True) / D
    two = jnp.sum(sums[1], axis=-1, keepdims=True) / D
    rstd = rstd_in[rows, :]
    for c in range(D // LEN):
        cols = slice(LEN * c, LEN * (c + 1))
        moved = rstd * (big[:, cols] - one - normed[rows, cols].astype(F32) * two)
        outgoing[:, cols] = (ups[:, cols].astype(F32) + moved).astype(BF16)
    put_grads = pltpu.make_async_copy(outgoing, grads_out.at[rows, :], sems.at[2])
    put_grads.start()
    put_ups.wait()
    put_gp.wait()
    put_grads.wait()


def chain_step(work, sources, w_in_t, w_out, saved, carried):
    kept = [((TOKENS, D), BF16), ((TOKENS, F1), BF16), ((TOKENS, D), BF16)]
    shapes = [((LEN, D), BF16)] + kept
    operands = [*sources, w_in_t, w_out, *saved, *carried]
    before = len(operands) - len(carried)
    aliases = {before + i: 1 + i for i in range(len(carried))}

    def kernel(*refs):
        section = lax.axis_index("pipe")
        if len(work) == 1:
            ((one, mine),) = work.items()
            busy = section == one
        else:
            (one, (slot, source)), (two, (slot_two, source_two)) = work.items()
            busy = jnp.logical_or(section == one, section == two)
            mine = (
                jnp.where(section == one, slot, slot_two),
                jnp.where(section == one, source, source_two),
            )

        @pl.when(busy)
        def _():
            chain_body(len(sources), len(carried), *mine, *refs)

    return pl.pallas_call(
        kernel,
        out_shape=[jax.ShapeDtypeStruct(*s) for s in shapes],
        in_specs=[vmem_spec()] * before + [any_spec()] * len(carried),
        out_specs=[vmem_spec()] + [any_spec()] * 3,
        input_output_aliases=aliases,
        scratch_shapes=[
            pltpu.VMEM((LEN, D), BF16),
            pltpu.VMEM((LEN, F1), BF16),
            pltpu.VMEM((LEN, D), F32),
            pltpu.SemaphoreType.DMA((3,)),
        ],
        compiler_params=pltpu.CompilerParams(vmem_limit_bytes=VMEM_LIMIT),
        cost_estimate=pl.CostEstimate(
            flops=2 * LEN * D * (F1 + HV), bytes_accessed=22_000_000, transcendentals=0
        ),
        name="chain",
    )(*operands)


def weights_kernel(jobs, normed_t, gated_t, ups, gp, *refs):
    outs, (rows_in, rows_out, buf, sems) = refs[: len(jobs)], refs[len(jobs) :]
    y, z = here()
    pending = [None, None]
    for count, (out, (half, blocks)) in enumerate(zip(outs, jobs)):
        turn, size = count % 2, len(blocks)
        for at, (dy, dz) in enumerate(blocks):
            row = block_row(y, z, dy, dz, LEN)
            rows_in[LEN * at : LEN * (at + 1), :] = normed_t[pl.ds(row, LEN), :]
            row = block_row(y, z, dy, dz, V_DIM)
            rows_out[V_DIM * at : V_DIM * (at + 1), :] = gated_t[pl.ds(row, V_DIM), :]
        if pending[turn] is not None:
            pending[turn].wait()
        for c in range(HALF_IN // 512):
            right = gp[:, HALF_IN * half + 512 * c : HALF_IN * half + 512 * (c + 1)]
            found = jnp.dot(rows_in[: LEN * size, :], right, preferred_element_type=F32)
            for at in range(size):
                buf[turn, at, :, 512 * c : 512 * (c + 1)] = found[
                    LEN * at : LEN * (at + 1), :
                ].astype(BF16)
        for fold in range(2):
            right = ups[:, HALF_OUT * half + FOLD * fold : HALF_OUT * half + FOLD * (fold + 1)]
            found = jnp.dot(rows_out[: V_DIM * size, :], right, preferred_element_type=F32)
            for at in range(size):
                buf[turn, at, V_DIM * fold : V_DIM * (fold + 1), HALF_IN:] = found[
                    V_DIM * at : V_DIM * (at + 1), :
                ].astype(BF16)
        pending[turn] = pltpu.make_async_copy(buf.at[turn, pl.ds(0, size)], out, sems.at[turn])
        pending[turn].start()
    for copy in pending:
        copy.wait()


def weight_parts(name, jobs, normed_t, gated_t, ups, gp):
    blocks = sum(len(job[1]) for job in jobs)
    return pl.pallas_call(
        lambda *refs: weights_kernel(jobs, *refs),
        out_shape=[jax.ShapeDtypeStruct((len(job[1]), LEN, PACK), BF16) for job in jobs],
        in_specs=[vmem_spec()] * 4,
        out_specs=[any_spec()] * len(jobs),
        scratch_shapes=[
            pltpu.VMEM((SIDE * LEN, TOKENS), BF16),
            pltpu.VMEM((SIDE * V_DIM, TOKENS), BF16),
            pltpu.VMEM((2, SIDE, LEN, PACK), BF16),
            pltpu.SemaphoreType.DMA((2,)),
        ],
        compiler_params=pltpu.CompilerParams(vmem_limit_bytes=VMEM_LIMIT),
        cost_estimate=pl.CostEstimate(
            flops=2 * TOKENS * LEN * PACK * blocks,
            bytes_accessed=4_000_000 + 2 * LEN * PACK * blocks,
            transcendentals=0,
        ),
        name=name,
    )(normed_t, gated_t, ups, gp)


FAR_JOBS = (
    (0, ((0, 2), (1, 2))),
    (0, ((2, 2), (3, 2))),
    (1, ((2, 0), (2, 1))),
    (1, ((2, 2), (2, 3))),
)
NEAR_JOBS = (
    (0, ((0, 1), (1, 1))),
    (0, ((2, 1), (3, 1))),
    (0, ((0, 3), (1, 3))),
    (0, ((2, 3), (3, 3))),
    (1, ((1, 0), (1, 1))),
    (1, ((1, 2), (1, 3))),
    (1, ((3, 0), (3, 1))),
    (1, ((3, 2), (3, 3))),
    (0, ((0, 0), (1, 0), (2, 0), (3, 0))),
    (1, ((0, 0), (0, 1), (0, 2), (0, 3))),
)


def along(axis, by):
    return (by, 0, 0) if axis == "y" else (0, by, 0)


def spread(block, axis):
    half = block.shape[0] // 2
    plus = send(block, *along(axis, 1))
    minus = send(block, *along(axis, -1))
    far_low = send(plus[:half], *along(axis, 1))
    far_high = send(minus[half:], *along(axis, -1))
    return plus, minus, far_low, far_high


def lined(block, axis):
    plus, minus, far_low, far_high = spread(block, axis)
    return jnp.stack([block, plus, jnp.concatenate([far_low, far_high], 0), minus])


def gathered(first, second, x):
    packed = jnp.concatenate([first, jnp.concatenate([second[:, :HALF_OUT], second[:, HALF_OUT:]], 0)], 1)
    other = send(packed, 0, 0, 1)
    low = jnp.where(x == 0, packed, other)
    high = jnp.where(x == 0, other, packed)
    rows = second.shape[0]
    lines = []
    for half in range(2):
        cols = slice(HALF_IN * half, HALF_IN * (half + 1))
        part = slice(rows * half, rows * (half + 1))
        out = jnp.concatenate([low[part, F1:], high[part, F1:]], 0)
        block = jnp.concatenate(
            [
                jnp.concatenate([low[:, cols], high[:, cols]], 0),
                jnp.concatenate([out[:, :FOLD], out[:, FOLD:]], 0),
            ],
            1,
        )
        lines.append(lined(block, "yz"[half]))
    return [(line, *spread(line, "zy"[half])) for half, line in enumerate(lines)]


def added(*arrays):
    total = arrays[0].astype(F32)
    for array in arrays[1:]:
        total = total + array.astype(F32)
    return total


def joined(own, plus_low, plus_high, minus_low, minus_high, far_low, far_high, axis):
    through = send(far_low, *along(axis, 1))
    back = send(far_high, *along(axis, -1))
    plus = jnp.concatenate([added(plus_low, through).astype(BF16), plus_high], 0)
    minus = jnp.concatenate([minus_low, added(minus_high, back).astype(BF16)], 0)
    return added(own, send(plus, *along(axis, 1)), send(minus, *along(axis, -1)))


def scattered(far, near, x):
    a_one = joined(near[8], *near[0:4], far[0], far[1], "z").astype(BF16)
    b_one = joined(near[9], *near[4:8], far[2], far[3], "y").astype(BF16)
    ends = []
    for line, axis in ((a_one, "y"), (b_one, "z")):
        cut = [part for block in (1, 3, 2) for part in (line[block, :V_DIM], line[block, V_DIM:])]
        ends.append(joined(line[0], *cut, axis))
    first = jnp.concatenate([end[:, :HALF_IN] for end in ends], 1)
    folded = jnp.concatenate([end[:, HALF_IN:] for end in ends], 1)
    outs = [folded[:V_DIM, :FOLD], folded[V_DIM:, :FOLD], folded[:V_DIM, FOLD:], folded[V_DIM:, FOLD:]]
    second = jnp.concatenate(outs, 1)
    sides = []
    for side in range(2):
        mine = second[32 * side : 32 * (side + 1)]
        tall = jnp.concatenate([mine[:, :HALF_OUT], mine[:, HALF_OUT:]], 0)
        sides.append(jnp.concatenate([first[64 * side : 64 * (side + 1)], tall], 1))
    away = jnp.where(x == 0, sides[1], sides[0]).astype(BF16)
    total = jnp.where(x == 0, sides[0], sides[1]) + send(away, 0, 0, 1).astype(F32)
    grad_out = jnp.concatenate([total[:32, F1:], total[32:, F1:]], 1)
    return total[:, :F1], grad_out


def body(section_input, top_grad, w_in, w_out, segments):
    x = lax.axis_index("dp") % 2
    pieces = gathered(w_in[0], w_out[0], x)

    same = segments[:, :, None] == segments[:, None, :]
    lower = lax.broadcasted_iota(jnp.int32, (LEN, LEN), 1) <= lax.broadcasted_iota(
        jnp.int32, (LEN, LEN), 0
    )
    counts = jnp.sum(same.astype(F32), axis=2, keepdims=True)
    masks = jnp.where(jnp.logical_and(same, lower[None]), 1.0 / counts, 0.0)

    saved, gated, w_first, w_second = front(section_input[0], masks, pieces)

    def step(work, sources, carried, second):
        outgoing, *carried = chain_step(
            work, (top_grad, *sources), w_first, second, saved, tuple(carried)
        )
        return outgoing, carried

    def below(array, which):
        return lax.ppermute(array, "pipe", [(which, which - 1)])

    out_0, carried = step({3: (0, 0)}, (), (), w_second)
    second_t = flip_second(w_second, out_0)
    out_1, carried = step({3: (1, 0), 2: (0, 1)}, (below(out_0, 3),), carried, second_t)
    to_one = below(out_1, 2)
    out_2, carried = step({2: (1, 1)}, (below(out_1, 3),), carried, second_t)
    again = below(out_2, 2)
    out_3, carried = step({1: (0, 1)}, (to_one,), carried, second_t)
    out_4, carried = step({1: (1, 1), 0: (0, 2)}, (again, below(out_3, 1)), carried, second_t)
    _, carried = step({0: (1, 1)}, (below(out_4, 1),), carried, second_t)
    ups, gp, grads = carried

    normed_t, gated_t = flip(saved[0], gated)
    far = weight_parts("far_parts", FAR_JOBS, normed_t, gated_t, ups, gp)
    near = weight_parts("near_parts", NEAR_JOBS, normed_t, gated_t, ups, gp)
    grad_first, grad_out = scattered(far, near, x)
    return (grads[None], grad_first[None], grad_out[None])


def solution(mesh):
    return jax.shard_map(
        body,
        mesh=mesh,
        in_specs=(
            P("pipe", "dp", None),
            P("dp", None),
            P("pipe", "dp", None),
            P("pipe", "dp", None),
            P("dp", None),
        ),
        out_specs=(P("pipe", "dp", None), P("pipe", "dp", None), P("pipe", "dp", None)),
        check_vma=False,
    )
```

```python
import jax
import jax.numpy as jnp
from jax import lax
from jax.experimental import pallas as pl
from jax.experimental.pallas import tpu as pltpu
from jax.sharding import PartitionSpec as P

HEADS = 16
QK_DIM = 32
V_DIM = 64
EPSILON = 1e-05
D = 2048
HV = 1024
F1 = 3072
QCOL = 2 * HV
KCOL = QCOL + HEADS * QK_DIM
LEN = 128
TOKENS = 256
SIDE = 4
HALF_IN = F1 // 2
HALF_OUT = D // 2
FOLD = HALF_OUT // 2
PACK = HALF_IN + FOLD
SCALE = QK_DIM ** (-0.5)
VMEM_LIMIT = 10 * 1024 * 1024
BF16 = jnp.bfloat16
F32 = jnp.float32

NT = (((1,), (1,)), ((), ()))
TN = (((0,), (0,)), ((), ()))


def mm(left, right, dims):
    return lax.dot_general(left, right, dims, preferred_element_type=F32)


def shifted(dy, dz, dx):
    pairs = []
    for i in range(32):
        y, z, x = i // 8, (i // 2) % 4, i % 2
        pairs.append((i, ((y + dy) % 4 * 4 + (z + dz) % 4) * 2 + (x + dx) % 2))
    return pairs


def send(array, dy, dz, dx):
    return lax.ppermute(array, "dp", shifted(dy, dz, dx))


def any_spec():
    return pl.BlockSpec(memory_space=pl.ANY)


def vmem_spec():
    return pl.BlockSpec(memory_space=pltpu.VMEM)


def block_row(y, z, dy, dz, rows):
    cell = lax.rem(y + dy + SIDE, SIDE) * SIDE + lax.rem(z + dz + SIDE, SIDE)
    return pl.multiple_of(cell * rows, rows)


def here():
    spot = lax.axis_index("dp")
    return lax.shift_right_logical(spot, 3), lax.bitwise_and(lax.shift_right_logical(spot, 1), 3)


def lane_group(width):
    return lax.broadcasted_iota(jnp.int32, (LEN, LEN), 1) // width


def keep(mask, tile):
    return jnp.where(mask, tile, jnp.zeros_like(tile))


def cells(half, across):
    return [(i, across) if half == 0 else (across, i) for i in range(SIDE)]


def chosen(normed, half, across):
    y, z = here()
    cols = [block_row(y, z, -j, -k, LEN) for j, k in cells(half, across)]
    return jnp.concatenate([normed[:, pl.ds(col, LEN)] for col in cols], axis=1)


def near_front_kernel(x_ref, *refs):
    pieces, (normed, pre, w_in_t, w_out, rstd_in, left) = refs[:6], refs[6:]
    y, z = here()

    @pl.loop(0, TOKENS // 32)
    def _(step):
        rows = pl.ds(pl.multiple_of(step * 32, 32), 32)
        values = x_ref[rows, :].astype(F32)
        center = values - jnp.mean(values, axis=-1, keepdims=True)
        rstd = lax.rsqrt(jnp.mean(center * center, axis=-1, keepdims=True) + EPSILON)
        normed[rows, :] = (center * rstd).astype(BF16)
        rstd_in[rows, :] = jnp.broadcast_to(rstd, (32, LEN))

    for half in range(2):
        trio = [(pieces[3 * half + n], n, across) for n, across in enumerate((0, 1, 3))]
        for _, n, across in trio:
            left[n] = chosen(normed, half, across)
        for c in range(HALF_IN // 512):
            cols = slice(512 * c, 512 * (c + 1))
            total = jnp.zeros((TOKENS, 512), F32)
            for piece, n, _ in trio:
                right = piece[:, :, cols].reshape(SIDE * LEN, 512)
                total += jnp.dot(left[n], right, preferred_element_type=F32)
            pre[:, HALF_IN * half + 512 * c : HALF_IN * half + 512 * (c + 1)] = total
        for piece, _, across in trio:
            for at, (j, k) in enumerate(cells(half, across)):
                col = block_row(y, z, -j, -k, LEN)
                row = block_row(y, z, -j, -k, V_DIM)
                for c in range(HALF_IN // 512):
                    rows = slice(HALF_IN * half + 512 * c, HALF_IN * half + 512 * (c + 1))
                    w_in_t[rows, pl.ds(col, LEN)] = piece[at, :, 512 * c : 512 * (c + 1)].T
                for fold in range(2):
                    first = HALF_OUT * half + FOLD * fold
                    w_out[pl.ds(row, V_DIM), first : first + FOLD] = piece[
                        at, V_DIM * fold : V_DIM * (fold + 1), HALF_IN:
                    ]


def near_front(inputs, pieces):
    shapes = [
        ((TOKENS, D), BF16),
        ((TOKENS, F1), F32),
        ((F1, D), BF16),
        ((HV, D), BF16),
        ((TOKENS, LEN), F32),
    ]
    return pl.pallas_call(
        near_front_kernel,
        out_shape=[jax.ShapeDtypeStruct(*s) for s in shapes],
        in_specs=[vmem_spec()] * 7,
        out_specs=[vmem_spec()] * 5,
        scratch_shapes=[pltpu.VMEM((3, TOKENS, SIDE * LEN), BF16)],
        compiler_params=pltpu.CompilerParams(vmem_limit_bytes=VMEM_LIMIT),
        cost_estimate=pl.CostEstimate(
            flops=3 * TOKENS * D * F1 // 2, bytes_accessed=20_000_000, transcendentals=0
        ),
        name="near_front",
    )(inputs, *pieces[0][:3], *pieces[1][:3])


def front_kernel(normed, pre, wm_ref, *refs):
    fars, refs = (refs[0:2], refs[2:4]), refs[6:]
    slope, act, attn, turn, xhat, gated, rstd_mid, w_in_t, w_out = refs[:9]
    mixed, left, flipped, sems, sems_out = refs[9:]
    y, z = here()
    copies = []
    for half in range(2):
        left[...] = chosen(normed, half, 2)
        for at, (j, k) in enumerate(cells(half, 2)):
            block = fars[half][at // 2].at[at % 2]
            row = block_row(y, z, -j, -k, V_DIM)
            for fold in range(2):
                spot = w_out.at[pl.ds(row, V_DIM), pl.ds(HALF_OUT * half + FOLD * fold, FOLD)]
                part = block.at[pl.ds(V_DIM * fold, V_DIM), pl.ds(HALF_IN, FOLD)]
                copies.append(pltpu.make_async_copy(part, spot, sems_out.at[half, at, fold]))
                copies[-1].start()
        for c in range(HALF_IN // 512):
            cols = slice(512 * c, 512 * (c + 1))
            into = slice(HALF_IN * half + 512 * c, HALF_IN * half + 512 * (c + 1))
            total = pre[:, into]
            for n in range(2):
                right = fars[half][n][:, :, cols].reshape(2 * LEN, 512)
                total += jnp.dot(
                    left[:, 256 * n : 256 * (n + 1)], right, preferred_element_type=F32
                )
            squash = jax.nn.sigmoid(total)
            act[:, into] = (total * squash).astype(BF16)
            slope[:, into] = (squash * (1.0 + total * (1.0 - squash))).astype(BF16)
        for at, (j, k) in enumerate(cells(half, 2)):
            block = fars[half][at // 2]
            for c in range(HALF_IN // 512):
                flipped[half, at, 512 * c : 512 * (c + 1), :] = block[
                    at % 2, :, 512 * c : 512 * (c + 1)
                ].T
            col = block_row(y, z, -j, -k, LEN)
            spot = w_in_t.at[pl.ds(HALF_IN * half, HALF_IN), pl.ds(col, LEN)]
            copies.append(pltpu.make_async_copy(flipped.at[half, at], spot, sems.at[half, at]))
            copies[-1].start()

    quarter, half = lane_group(QK_DIM), lane_group(V_DIM)

    @pl.loop(0, TOKENS // LEN)
    def _(m):
        rows = pl.ds(pl.multiple_of(m * LEN, LEN), LEN)
        mask = wm_ref[m]
        for h4 in range(4):
            q4 = act[rows, QCOL + LEN * h4 : QCOL + LEN * (h4 + 1)]
            k4 = act[rows, KCOL + LEN * h4 : KCOL + LEN * (h4 + 1)]
            for pair in range(2):
                tile = 2 * h4 + pair
                v2 = act[rows, HV + LEN * tile : HV + LEN * (tile + 1)]
                total = jnp.zeros((LEN, LEN), F32)
                for e in range(2):
                    h = 2 * tile + e
                    score = mm(keep(quarter == 2 * pair + e, q4), k4, NT) * SCALE
                    squash = jax.nn.sigmoid(score)
                    weight = (score * squash * mask).astype(BF16)
                    attn[m, h] = weight
                    turn[m, h] = (
                        squash * (1.0 + score * (1.0 - squash)) * mask * SCALE
                    ).astype(BF16)
                    total += jnp.dot(weight, keep(half == e, v2), preferred_element_type=F32)
                mixed[:, LEN * tile : LEN * (tile + 1)] = total
        values = mixed[...]
        center = values - jnp.mean(values, axis=-1, keepdims=True)
        rstd = lax.rsqrt(jnp.mean(center * center, axis=-1, keepdims=True) + EPSILON)
        hat = center * rstd
        xhat[rows, :] = hat
        rstd_mid[rows, :] = jnp.broadcast_to(rstd, (LEN, LEN))
        gated[rows, :] = (hat * act[rows, :HV].astype(F32)).astype(BF16)

    for copy in copies:
        copy.wait()


def front(inputs, masks, pieces):
    normed, pre, w_in_t, w_out, rstd_in = near_front(inputs, pieces)
    shapes = [
        ((TOKENS, F1), BF16),
        ((TOKENS, F1), BF16),
        ((2, HEADS, LEN, LEN), BF16),
        ((2, HEADS, LEN, LEN), BF16),
        ((TOKENS, HV), F32),
        ((TOKENS, HV), BF16),
        ((TOKENS, LEN), F32),
        ((F1, D), BF16),
        ((HV, D), BF16),
    ]
    slope, act, attn, turn, xhat, gated, rstd_mid, w_in_t, w_out = pl.pallas_call(
        front_kernel,
        out_shape=[jax.ShapeDtypeStruct(*s) for s in shapes],
        in_specs=[vmem_spec()] * 7 + [any_spec()] * 2,
        out_specs=[vmem_spec()] * 7 + [any_spec()] * 2,
        input_output_aliases={7: 7, 8: 8},
        scratch_shapes=[
            pltpu.VMEM((LEN, HV), F32),
            pltpu.VMEM((TOKENS, SIDE * LEN), BF16),
            pltpu.VMEM((2, SIDE, HALF_IN, LEN), BF16),
            pltpu.SemaphoreType.DMA((2, SIDE)),
            pltpu.SemaphoreType.DMA((2, SIDE, 2)),
        ],
        compiler_params=pltpu.CompilerParams(vmem_limit_bytes=VMEM_LIMIT),
        cost_estimate=pl.CostEstimate(
            flops=TOKENS * D * F1 // 2, bytes_accessed=30_000_000, transcendentals=1_500_000
        ),
        name="front",
    )(normed, pre, masks, *pieces[0][3:], *pieces[1][3:], w_in_t, w_out)
    saved = (normed, slope, act, attn, turn, xhat, rstd_in, rstd_mid)
    return saved, gated, w_in_t, w_out


def flip_kernel(normed, gated, normed_t, gated_t):
    for c in range(D // LEN):
        normed_t[LEN * c : LEN * (c + 1), :] = normed[:, LEN * c : LEN * (c + 1)].T
    for c in range(HV // LEN):
        gated_t[LEN * c : LEN * (c + 1), :] = gated[:, LEN * c : LEN * (c + 1)].T


def flip_second_kernel(w_out, _, w_out_t):
    for r in range(HV // LEN):
        for c in range(D // 512):
            w_out_t[512 * c : 512 * (c + 1), LEN * r : LEN * (r + 1)] = w_out[
                LEN * r : LEN * (r + 1), 512 * c : 512 * (c + 1)
            ].T


def flip_second(w_out, after):
    return pl.pallas_call(
        flip_second_kernel,
        out_shape=jax.ShapeDtypeStruct((D, HV), BF16),
        in_specs=[vmem_spec(), any_spec()],
        out_specs=vmem_spec(),
        compiler_params=pltpu.CompilerParams(vmem_limit_bytes=VMEM_LIMIT),
        cost_estimate=pl.CostEstimate(flops=0, bytes_accessed=8_000_000, transcendentals=0),
        name="flip_second",
    )(w_out, after)


def flip(normed, gated):
    return pl.pallas_call(
        flip_kernel,
        out_shape=[
            jax.ShapeDtypeStruct((D, TOKENS), BF16),
            jax.ShapeDtypeStruct((HV, TOKENS), BF16),
        ],
        in_specs=[vmem_spec()] * 2,
        out_specs=[vmem_spec()] * 2,
        compiler_params=pltpu.CompilerParams(vmem_limit_bytes=VMEM_LIMIT),
        cost_estimate=pl.CostEstimate(flops=0, bytes_accessed=6_000_000, transcendentals=0),
        name="flip",
    )(normed, gated)


def chain_body(n_sources, n_carried, slot, source, *refs):
    sources, refs = refs[:n_sources], refs[n_sources:]
    w_in_t, w_out, normed, slope, act, attn, turn, xhat, rstd_in, rstd_mid = refs[:10]
    outgoing, ups_out, gp_out, grads_out, ups, gp, big, sems = refs[10 + n_carried :]
    slot, source = jnp.int32(slot), jnp.int32(source)
    rows = pl.ds(pl.multiple_of(slot * LEN, LEN), LEN)
    for i, ref in enumerate(sources):

        @pl.when(source == i)
        def _():
            ups[...] = ref[rows, :] if i == 0 else ref[...]

    put_ups = pltpu.make_async_copy(ups, ups_out.at[rows, :], sems.at[0])
    put_ups.start()

    for c in range(HV // 256):
        cols = slice(256 * c, 256 * (c + 1))
        if w_out.shape[0] == HV:
            big[:, cols] = mm(ups[...], w_out[cols, :], NT)
        else:
            big[:, cols] = jnp.dot(ups[...], w_out[:, cols], preferred_element_type=F32)
    sums = [jnp.zeros((LEN, LEN), F32)] * 2
    for c in range(HV // LEN):
        cols = slice(LEN * c, LEN * (c + 1))
        hat = xhat[rows, cols]
        moved = big[:, cols] * act[rows, cols].astype(F32)
        sums = [sums[0] + moved, sums[1] + moved * hat]
        gp[:, cols] = (
            (big[:, cols] * hat).astype(BF16).astype(F32) * slope[rows, cols].astype(F32)
        ).astype(BF16)
        big[:, HV + LEN * c : HV + LEN * (c + 1)] = moved
    mean_one = jnp.sum(sums[0], axis=-1, keepdims=True) / HV
    mean_hat = jnp.sum(sums[1], axis=-1, keepdims=True) / HV
    rstd = rstd_mid[rows, :]

    quarter, half = lane_group(QK_DIM), lane_group(V_DIM)

    def put(value, col):
        cols = slice(col, col + LEN)
        gp[:, cols] = (
            value.astype(BF16).astype(F32) * slope[rows, cols].astype(F32)
        ).astype(BF16)

    for h4 in range(4):
        q4 = act[rows, QCOL + LEN * h4 : QCOL + LEN * (h4 + 1)]
        k4 = act[rows, KCOL + LEN * h4 : KCOL + LEN * (h4 + 1)]
        grad_q = jnp.zeros((LEN, LEN), F32)
        grad_k = jnp.zeros((LEN, LEN), F32)
        for pair in range(2):
            tile = 2 * h4 + pair
            v2 = act[rows, HV + LEN * tile : HV + LEN * (tile + 1)]
            moved = big[:, HV + LEN * tile : HV + LEN * (tile + 1)]
            hat = xhat[rows, LEN * tile : LEN * (tile + 1)]
            g2 = (rstd * (moved - mean_one - hat * mean_hat)).astype(BF16)
            grad_v = jnp.zeros((LEN, LEN), F32)
            for e in range(2):
                h = 2 * tile + e
                gh = keep(half == e, g2)
                grad_s = (mm(gh, v2, NT) * turn[slot, h].astype(F32)).astype(BF16)
                grad_v += mm(attn[slot, h], gh, TN)
                own = quarter == 2 * pair + e
                grad_q += jnp.dot(grad_s, keep(own, k4), preferred_element_type=F32)
                grad_k += mm(grad_s, keep(own, q4), TN)
            put(grad_v, HV + LEN * tile)
        put(grad_q, QCOL + LEN * h4)
        put(grad_k, KCOL + LEN * h4)

    put_gp = pltpu.make_async_copy(gp, gp_out.at[rows, :], sems.at[1])
    put_gp.start()
    sums = [jnp.zeros((LEN, LEN), F32)] * 2
    for c in range(D // 256):
        big[:, 256 * c : 256 * (c + 1)] = jnp.dot(
            gp[...], w_in_t[:, 256 * c : 256 * (c + 1)], preferred_element_type=F32
        )
        for cols in (slice(256 * c, 256 * c + LEN), slice(256 * c + LEN, 256 * (c + 1))):
            grad = big[:, cols]
            sums = [sums[0] + grad, sums[1] + grad * normed[rows, cols].astype(F32)]
    one = jnp.sum(sums[0], axis=-1, keepdims=True) / D
    two = jnp.sum(sums[1], axis=-1, keepdims=True) / D
    rstd = rstd_in[rows, :]
    for c in range(D // LEN):
        cols = slice(LEN * c, LEN * (c + 1))
        moved = rstd * (big[:, cols] - one - normed[rows, cols].astype(F32) * two)
        outgoing[:, cols] = (ups[:, cols].astype(F32) + moved).astype(BF16)
    put_grads = pltpu.make_async_copy(outgoing, grads_out.at[rows, :], sems.at[2])
    put_grads.start()
    put_ups.wait()
    put_gp.wait()
    put_grads.wait()


def chain_step(work, sources, w_in_t, w_out, saved, carried):
    kept = [((TOKENS, D), BF16), ((TOKENS, F1), BF16), ((TOKENS, D), BF16)]
    shapes = [((LEN, D), BF16)] + kept
    operands = [*sources, w_in_t, w_out, *saved, *carried]
    before = len(operands) - len(carried)
    aliases = {before + i: 1 + i for i in range(len(carried))}

    def kernel(*refs):
        section = lax.axis_index("pipe")
        if len(work) == 1:
            ((one, mine),) = work.items()
            busy = section == one
        else:
            (one, (slot, source)), (two, (slot_two, source_two)) = work.items()
            busy = jnp.logical_or(section == one, section == two)
            mine = (
                jnp.where(section == one, slot, slot_two),
                jnp.where(section == one, source, source_two),
            )

        @pl.when(busy)
        def _():
            chain_body(len(sources), len(carried), *mine, *refs)

    return pl.pallas_call(
        kernel,
        out_shape=[jax.ShapeDtypeStruct(*s) for s in shapes],
        in_specs=[vmem_spec()] * before + [any_spec()] * len(carried),
        out_specs=[vmem_spec()] + [any_spec()] * 3,
        input_output_aliases=aliases,
        scratch_shapes=[
            pltpu.VMEM((LEN, D), BF16),
            pltpu.VMEM((LEN, F1), BF16),
            pltpu.VMEM((LEN, D), F32),
            pltpu.SemaphoreType.DMA((3,)),
        ],
        compiler_params=pltpu.CompilerParams(vmem_limit_bytes=VMEM_LIMIT),
        cost_estimate=pl.CostEstimate(
            flops=2 * LEN * D * (F1 + HV), bytes_accessed=22_000_000, transcendentals=0
        ),
        name="chain",
    )(*operands)


def weights_kernel(jobs, normed_t, gated_t, ups, gp, *refs):
    outs, (rows_in, rows_out, buf, sems) = refs[: len(jobs)], refs[len(jobs) :]
    y, z = here()
    pending = [None, None]
    for count, (out, (half, blocks)) in enumerate(zip(outs, jobs)):
        turn, size = count % 2, len(blocks)
        for at, (dy, dz) in enumerate(blocks):
            row = block_row(y, z, dy, dz, LEN)
            rows_in[LEN * at : LEN * (at + 1), :] = normed_t[pl.ds(row, LEN), :]
            row = block_row(y, z, dy, dz, V_DIM)
            rows_out[V_DIM * at : V_DIM * (at + 1), :] = gated_t[pl.ds(row, V_DIM), :]
        if pending[turn] is not None:
            pending[turn].wait()
        for c in range(HALF_IN // 512):
            right = gp[:, HALF_IN * half + 512 * c : HALF_IN * half + 512 * (c + 1)]
            found = jnp.dot(rows_in[: LEN * size, :], right, preferred_element_type=F32)
            for at in range(size):
                buf[turn, at, :, 512 * c : 512 * (c + 1)] = found[
                    LEN * at : LEN * (at + 1), :
                ].astype(BF16)
        for fold in range(2):
            right = ups[:, HALF_OUT * half + FOLD * fold : HALF_OUT * half + FOLD * (fold + 1)]
            found = jnp.dot(rows_out[: V_DIM * size, :], right, preferred_element_type=F32)
            for at in range(size):
                buf[turn, at, V_DIM * fold : V_DIM * (fold + 1), HALF_IN:] = found[
                    V_DIM * at : V_DIM * (at + 1), :
                ].astype(BF16)
        pending[turn] = pltpu.make_async_copy(buf.at[turn, pl.ds(0, size)], out, sems.at[turn])
        pending[turn].start()
    for copy in pending:
        copy.wait()


def weight_parts(name, jobs, normed_t, gated_t, ups, gp):
    blocks = sum(len(job[1]) for job in jobs)
    return pl.pallas_call(
        lambda *refs: weights_kernel(jobs, *refs),
        out_shape=[jax.ShapeDtypeStruct((len(job[1]), LEN, PACK), BF16) for job in jobs],
        in_specs=[vmem_spec()] * 4,
        out_specs=[any_spec()] * len(jobs),
        scratch_shapes=[
            pltpu.VMEM((SIDE * LEN, TOKENS), BF16),
            pltpu.VMEM((SIDE * V_DIM, TOKENS), BF16),
            pltpu.VMEM((2, SIDE, LEN, PACK), BF16),
            pltpu.SemaphoreType.DMA((2,)),
        ],
        compiler_params=pltpu.CompilerParams(vmem_limit_bytes=VMEM_LIMIT),
        cost_estimate=pl.CostEstimate(
            flops=2 * TOKENS * LEN * PACK * blocks,
            bytes_accessed=4_000_000 + 2 * LEN * PACK * blocks,
            transcendentals=0,
        ),
        name=name,
    )(normed_t, gated_t, ups, gp)


FAR_JOBS = (
    (0, ((0, 2), (1, 2))),
    (0, ((2, 2), (3, 2))),
    (1, ((2, 0), (2, 1))),
    (1, ((2, 2), (2, 3))),
)
NEAR_JOBS = (
    (0, ((0, 1), (1, 1))),
    (0, ((2, 1), (3, 1))),
    (0, ((0, 3), (1, 3))),
    (0, ((2, 3), (3, 3))),
    (1, ((1, 0), (1, 1))),
    (1, ((1, 2), (1, 3))),
    (1, ((3, 0), (3, 1))),
    (1, ((3, 2), (3, 3))),
    (0, ((0, 0), (1, 0), (2, 0), (3, 0))),
    (1, ((0, 0), (0, 1), (0, 2), (0, 3))),
)


def along(axis, by):
    return (by, 0, 0) if axis == "y" else (0, by, 0)


def spread(block, axis):
    half = block.shape[0] // 2
    plus = send(block, *along(axis, 1))
    minus = send(block, *along(axis, -1))
    far_low = send(plus[:half], *along(axis, 1))
    far_high = send(minus[half:], *along(axis, -1))
    return plus, minus, far_low, far_high


def lined(block, axis):
    far, plus, minus = [send(block, *along(axis, by)) for by in (2, 1, -1)]
    return jnp.stack([block, plus, far, minus])


def gathered(first, second, x):
    packed = jnp.concatenate([first, jnp.concatenate([second[:, :HALF_OUT], second[:, HALF_OUT:]], 0)], 1)
    other = send(packed, 0, 0, 1)
    low = jnp.where(x == 0, packed, other)
    high = jnp.where(x == 0, other, packed)
    rows = second.shape[0]
    lines = []
    for half in range(2):
        cols = slice(HALF_IN * half, HALF_IN * (half + 1))
        part = slice(rows * half, rows * (half + 1))
        out = jnp.concatenate([low[part, F1:], high[part, F1:]], 0)
        block = jnp.concatenate(
            [
                jnp.concatenate([low[:, cols], high[:, cols]], 0),
                jnp.concatenate([out[:, :FOLD], out[:, FOLD:]], 0),
            ],
            1,
        )
        lines.append(lined(block, "yz"[half]))
    return [(line, *spread(line, "zy"[half])) for half, line in enumerate(lines)]


def added(*arrays):
    total = arrays[0].astype(F32)
    for array in arrays[1:]:
        total = total + array.astype(F32)
    return total


def joined(own, plus_low, plus_high, minus_low, minus_high, far_low, far_high, axis):
    through = send(far_low, *along(axis, 1))
    back = send(far_high, *along(axis, -1))
    plus = jnp.concatenate([added(plus_low, through).astype(BF16), plus_high], 0)
    minus = jnp.concatenate([minus_low, added(minus_high, back).astype(BF16)], 0)
    return added(own, send(plus, *along(axis, 1)), send(minus, *along(axis, -1)))


def scattered(far, near, x):
    a_one = joined(near[8], *near[0:4], far[0], far[1], "z").astype(BF16)
    b_one = joined(near[9], *near[4:8], far[2], far[3], "y").astype(BF16)
    ends = []
    for line, axis in ((a_one, "y"), (b_one, "z")):
        sent = [send(line[step], *along(axis, by)) for step, by in ((2, 2), (1, 1), (3, -1))]
        ends.append(added(line[0], *sent))
    first = jnp.concatenate([end[:, :HALF_IN] for end in ends], 1)
    folded = jnp.concatenate([end[:, HALF_IN:] for end in ends], 1)
    outs = [folded[:V_DIM, :FOLD], folded[V_DIM:, :FOLD], folded[:V_DIM, FOLD:], folded[V_DIM:, FOLD:]]
    second = jnp.concatenate(outs, 1)
    sides = []
    for side in range(2):
        mine = second[32 * side : 32 * (side + 1)]
        tall = jnp.concatenate([mine[:, :HALF_OUT], mine[:, HALF_OUT:]], 0)
        sides.append(jnp.concatenate([first[64 * side : 64 * (side + 1)], tall], 1))
    away = jnp.where(x == 0, sides[1], sides[0]).astype(BF16)
    total = jnp.where(x == 0, sides[0], sides[1]) + send(away, 0, 0, 1).astype(F32)
    grad_out = jnp.concatenate([total[:32, F1:], total[32:, F1:]], 1)
    return total[:, :F1], grad_out


def body(section_input, top_grad, w_in, w_out, segments):
    x = lax.axis_index("dp") % 2
    pieces = gathered(w_in[0], w_out[0], x)

    same = segments[:, :, None] == segments[:, None, :]
    lower = lax.broadcasted_iota(jnp.int32, (LEN, LEN), 1) <= lax.broadcasted_iota(
        jnp.int32, (LEN, LEN), 0
    )
    counts = jnp.sum(same.astype(F32), axis=2, keepdims=True)
    masks = jnp.where(jnp.logical_and(same, lower[None]), 1.0 / counts, 0.0)

    saved, gated, w_first, w_second = front(section_input[0], masks, pieces)

    def step(work, sources, carried, second):
        outgoing, *carried = chain_step(
            work, (top_grad, *sources), w_first, second, saved, tuple(carried)
        )
        return outgoing, carried

    def below(array, which):
        return lax.ppermute(array, "pipe", [(which, which - 1)])

    out_0, carried = step({3: (0, 0)}, (), (), w_second)
    second_t = flip_second(w_second, out_0)
    out_1, carried = step({3: (1, 0), 2: (0, 1)}, (below(out_0, 3),), carried, second_t)
    to_one = below(out_1, 2)
    out_2, carried = step({2: (1, 1)}, (below(out_1, 3),), carried, second_t)
    again = below(out_2, 2)
    out_3, carried = step({1: (0, 1)}, (to_one,), carried, second_t)
    out_4, carried = step({1: (1, 1), 0: (0, 2)}, (again, below(out_3, 1)), carried, second_t)
    _, carried = step({0: (1, 1)}, (below(out_4, 1),), carried, second_t)
    ups, gp, grads = carried

    normed_t, gated_t = flip(saved[0], gated)
    far = weight_parts("far_parts", FAR_JOBS, normed_t, gated_t, ups, gp)
    near = weight_parts("near_parts", NEAR_JOBS, normed_t, gated_t, ups, gp)
    grad_first, grad_out = scattered(far, near, x)
    return (grads[None], grad_first[None], grad_out[None])


def solution(mesh):
    return jax.shard_map(
        body,
        mesh=mesh,
        in_specs=(
            P("pipe", "dp", None),
            P("dp", None),
            P("pipe", "dp", None),
            P("pipe", "dp", None),
            P("dp", None),
        ),
        out_specs=(P("pipe", "dp", None), P("pipe", "dp", None), P("pipe", "dp", None)),
        check_vma=False,
    )
```
